32 devices in a mesh: dp: 16 (over z, x, core), mp: 2 (over y).
Axes of the slice: x: 2, y: 2, z: 4, core: 2. Of those that a mesh axis runs over, the one named last changes fastest.
Arguments:
- tokens: bfloat16 [25088, 768], P(('dp', 'mp')), may hold values from -6 to 6
- image_ids: int32 [25088], P('dp'), may hold values from -1 to 5, as said below
- rel_index: int32 [49, 49], replicated, may hold values from 0 to 168, as said below
- gain_one: bfloat16 [768], replicated, may hold values from 0.5 to 1.5
- shift_one: bfloat16 [768], replicated, may hold values from -3 to 3
- w_qkv: bfloat16 [768, 2304], P(None, 'mp'), may hold values from -0.21875 to 0.21875
- bias_query: bfloat16 [768], P('mp'), may hold values from -3 to 3
- bias_value: bfloat16 [768], P('mp'), may hold values from -3 to 3
- bias_table: bfloat16 [169, 24], P(None, 'mp'), may hold values from -4 to 4
- w_proj: bfloat16 [768, 768], P('mp'), may hold values from -0.5 to 0.5
- bias_proj: bfloat16 [768], replicated, may hold values from -2 to 2
- gain_two: bfloat16 [768], replicated, may hold values from 0.5 to 1.5
- shift_two: bfloat16 [768], replicated, may hold values from -3 to 3
- w_up: bfloat16 [768, 3072], P(None, 'mp'), may hold values from -0.21875 to 0.21875
- bias_up: bfloat16 [3072], P('mp'), may hold values from -3 to 3
- w_down: bfloat16 [3072, 768], P('mp'), may hold values from -0.109375 to 0.109375
- bias_down: bfloat16 [768], replicated, may hold values from -2 to 2
- cotangent: bfloat16 [25088, 768], P(('dp', 'mp')), may hold values from -6 to 6
Outputs:
- block_out: bfloat16 [25088, 768], P(('dp', 'mp'))
- grad_tokens: bfloat16 [25088, 768], P(('dp', 'mp'))
- grad_gain_one: float32 [768], replicated
- grad_shift_one: float32 [768], replicated
- grad_w_qkv: float32 [768, 2304], P(None, 'mp')
- grad_bias_query: float32 [768], P('mp')
- grad_bias_value: float32 [768], P('mp')
- grad_bias_table: float32 [169, 24], P(None, 'mp')
- grad_w_proj: float32 [768, 768], P('mp')
- grad_bias_proj: float32 [768], replicated
- grad_gain_two: float32 [768], replicated
- grad_shift_two: float32 [768], replicated
- grad_w_up: float32 [768, 3072], P(None, 'mp')
- grad_bias_up: float32 [3072], P('mp')
- grad_w_down: float32 [3072, 768], P('mp')
- grad_bias_down: float32 [768], replicated
The draws below stay inside these ranges and needn't reach their ends.
Inputs may be any that keep to these rules, and one draw needn't show every extreme that they name: `image_ids`: in each window either all 49 slots hold 0 (one image), or five images of 9 slots hold 1 to 5 and 4 padding slots hold -1; the first window is of the second kind. rel_index[a, b] = (r_a - r_b + 6) * 13 + c_a - c_b + 6, where slot a sits at row r_a and column c_a of the window, each grid place taken by one slot.
All inputs are finite; a program needn't handle non-finite values.
Results may differ from the reference program's by a relative error of at most 0.018.
Values may be sent and summed in bfloat16 or wider, within the bound.
No kernel may reach another device: no remote copies, remote signals or barrier semaphores. Data moves between devices by JAX's collectives and lax.ppermute only.
A program may use at most 256 MiB of HBM per device.

```python
import jax
import jax.numpy as jnp
from jax import lax

D = 768
HEADS = 24
HEAD_DIM = 32
FF = 3072
WIN_SIDE = 7
SLOTS = 49
TABLE_ROWS = 169
TOKENS = 25088


def draw_image_ids(key, part):
    key = jax.random.fold_in(key, 11)
    windows = TOKENS // SLOTS
    kind_key, order_key = jax.random.split(key)
    packed = jax.random.randint(kind_key, (windows,), 0, 2)
    packed = jnp.where(jnp.arange(windows) == 0, 1, packed)
    window_keys = jax.random.split(order_key, windows)
    orders = jax.vmap(lambda sub_key: jax.random.permutation(sub_key, SLOTS))(window_keys)
    groups = jnp.where(orders < 45, orders // 9 + 1, -1)
    labels = jnp.where(packed[:, None] == 1, groups, 0)
    return labels.reshape(-1).astype(jnp.int32)


def draw_rel_index(key, part):
    key = jax.random.fold_in(key, 23)
    placement = jax.random.permutation(key, SLOTS)
    grid_row = placement // WIN_SIDE
    grid_col = placement % WIN_SIDE
    table_side = 2 * WIN_SIDE - 1
    row_part = (grid_row[:, None] - grid_row[None, :] + WIN_SIDE - 1) * table_side
    col_part = grid_col[:, None] - grid_col[None, :] + WIN_SIDE - 1
    return (row_part + col_part).astype(jnp.int32)


def levels(rng, shape, cuts, low, largest):
    def one(axis_at, shards_of):
        draws = jax.random.uniform(jax.random.fold_in(jax.random.fold_in(rng, 6), axis_at), (shards_of,), jnp.float32, low / len(cuts), largest / len(cuts))
        return jnp.repeat(jnp.exp(draws), shape[axis_at] // shards_of).reshape((-1,) + (1,) * (len(shape) - axis_at - 1))

    gain = one(*cuts[0])
    for cut in cuts[1:]:
        gain = gain * one(*cut)
    return gain


def normal_values(stream_key, dims, width, reach, shards=(), held_as=jnp.bfloat16):
    loudness = levels(stream_key, dims, shards, -0.22, 0.18) if shards else 1.0
    values = jax.random.normal(stream_key, dims, jnp.float32) * width * loudness
    return jnp.minimum(jnp.maximum(values, -reach), reach).astype(held_as)


def setup_inputs(seed: int = 0) -> dict:
    arg_keys = jax.random.split(jax.random.key(seed), 19)
    tokens = normal_values(arg_keys[0], (TOKENS, D), 1.0, 6.0, ((0, 32),))
    image_ids = draw_image_ids(jax.random.fold_in(arg_keys[18], 71), 0)
    rel_index = draw_rel_index(jax.random.fold_in(arg_keys[18], 71), 0)
    gain_one = jnp.clip(1.0 + 0.1 * jax.random.normal(arg_keys[3], (D,), jnp.float32), 0.5, 1.5).astype(jnp.bfloat16)
    shift_one = normal_values(arg_keys[4], (D,), 0.5, 3.0)
    w_qkv = normal_values(arg_keys[5], (D, 3 * D), D ** -0.5, 0.21875, ((1, 2),))
    bias_query = normal_values(arg_keys[6], (D,), 0.5, 3.0, ((0, 2),))
    bias_value = normal_values(arg_keys[7], (D,), 0.5, 3.0, ((0, 2),))
    bias_table = normal_values(arg_keys[8], (TABLE_ROWS, HEADS), 1.0, 4.0, ((1, 2),))
    w_proj = normal_values(arg_keys[9], (D, D), (D // 5) ** -0.5, 0.5, ((0, 2),))
    bias_proj = normal_values(arg_keys[10], (D,), 0.3, 2.0)
    gain_two = jnp.clip(1.0 + 0.1 * jax.random.normal(arg_keys[11], (D,), jnp.float32), 0.5, 1.5).astype(jnp.bfloat16)
    shift_two = normal_values(arg_keys[12], (D,), 0.5, 3.0)
    w_up = normal_values(arg_keys[13], (D, FF), D ** -0.5, 0.21875, ((1, 2),))
    bias_up = normal_values(arg_keys[14], (FF,), 0.5, 3.0, ((0, 2),))
    w_down = normal_values(arg_keys[15], (FF, D), FF ** -0.5, 0.109375, ((0, 2),))
    bias_down = normal_values(arg_keys[16], (D,), 0.3, 2.0)
    cotangent = normal_values(arg_keys[17], (TOKENS, D), 1.0, 6.0, ((0, 32),))
    return dict(tokens=tokens, image_ids=image_ids, rel_index=rel_index, gain_one=gain_one, shift_one=shift_one, w_qkv=w_qkv, bias_query=bias_query, bias_value=bias_value, bias_table=bias_table, w_proj=w_proj, bias_proj=bias_proj, gain_two=gain_two, shift_two=shift_two, w_up=w_up, bias_up=bias_up, w_down=w_down, bias_down=bias_down, cotangent=cotangent)


norm_eps = 1e-05
mask_fill = -1000000000.0

@jax.custom_vjp
def low(v):
    return lax.optimization_barrier(v.astype(jnp.bfloat16)).astype(jnp.float32)

@jax.custom_vjp
def low_back(v):
    return v

def low_keep(v):
    return (low(v), None)

def low_pass(kept, grad):
    return (grad,)

def back_keep(v):
    return (v, None)

def back_low(kept, grad):
    return (low(grad),)
low.defvjp(low_keep, low_pass)
low_back.defvjp(back_keep, back_low)

def product(left, right):
    return jnp.dot(left, right, precision=lax.Precision.HIGHEST, preferred_element_type=jnp.float32)

def layer_norm(values_in, gain_in, shift_in):
    row_mean = lax.optimization_barrier(jnp.mean(values_in, axis=-1, keepdims=True))
    centred = values_in - row_mean
    spread = lax.optimization_barrier(jnp.mean(centred * centred, axis=-1, keepdims=True))
    return centred * lax.rsqrt(spread + norm_eps) * gain_in + shift_in

def window_block(pos_bias, packet):
    qkv_block, labels = packet
    query_part = qkv_block[..., 0, :]
    key_part = qkv_block[..., 1, :]
    value_part = qkv_block[..., 2, :]
    raw_scores = jnp.einsum('wqhd,wkhd->whqk', query_part, key_part, precision=lax.Precision.HIGHEST)
    scores = low_back(raw_scores * HEAD_DIM ** (-0.5) + pos_bias[None])
    same_image = labels[:, :, None] == labels[:, None, :]
    diagonal_ok = jnp.eye(SLOTS, dtype=bool)[None]
    allowed = same_image & ((labels[:, None, :] >= 0) | diagonal_ok)
    scores = jnp.where(allowed[:, None], scores, mask_fill)
    probability = low(jax.nn.softmax(scores, axis=-1))
    return jnp.einsum('whqk,wkhd->wqhd', probability, value_part, precision=lax.Precision.HIGHEST)

def forward(tokens, gain_one, shift_one, w_qkv, bias_query, bias_value, bias_table, w_proj, bias_proj, gain_two, shift_two, w_up, bias_up, w_down, bias_down, image_ids, rel_index):
    row_count = tokens.shape[0]
    normed_one = low(layer_norm(tokens, gain_one, shift_one))
    qkv = product(normed_one, w_qkv).reshape(row_count, HEADS, 3, HEAD_DIM)
    zero_block = jnp.zeros((HEADS, HEAD_DIM), jnp.float32)
    qkv_bias = jnp.stack([bias_query.reshape(HEADS, HEAD_DIM), zero_block, bias_value.reshape(HEADS, HEAD_DIM)], axis=1)
    qkv = low_back(low(qkv + qkv_bias[None]))
    pos_bias = jnp.transpose(bias_table[rel_index], (2, 0, 1))
    windows = row_count // SLOTS
    grouped = qkv.reshape(windows // 64, 64, SLOTS, HEADS, 3, HEAD_DIM)
    label_groups = image_ids.reshape(windows // 64, 64, SLOTS)
    checked = jax.checkpoint(window_block)
    attended = lax.map(lambda packet: checked(pos_bias, packet), (grouped, label_groups))
    attended = low_back(low(attended.reshape(row_count, HEADS * HEAD_DIM)))
    branch = low_back(product(attended, w_proj) + bias_proj)
    middle = tokens + branch
    normed_two = low(layer_norm(middle, gain_two, shift_two))
    pre_act = low_back(product(normed_two, w_up) + bias_up)
    hidden = low(jax.nn.gelu(pre_act, approximate=False))
    mlp_out = low_back(product(hidden, w_down) + bias_down)
    return middle + mlp_out

def reference(tokens, image_ids, rel_index, gain_one, shift_one, w_qkv, bias_query, bias_value, bias_table, w_proj, bias_proj, gain_two, shift_two, w_up, bias_up, w_down, bias_down, cotangent):
    floats = [item.astype(jnp.float32) for item in (tokens, gain_one, shift_one, w_qkv, bias_query, bias_value, bias_table, w_proj, bias_proj, gain_two, shift_two, w_up, bias_up, w_down, bias_down)]
    result, backward = jax.vjp(lambda *params: forward(*params, image_ids, rel_index), *floats)
    grads = backward(cotangent.astype(jnp.float32))
    return (result.astype(jnp.bfloat16), grads[0].astype(jnp.bfloat16), grads[1], grads[2], grads[3], grads[4], grads[5], grads[6], grads[7], grads[8], grads[9], grads[10], grads[11], grads[12], grads[13], grads[14])
```

```python
import functools

import jax
import jax.numpy as jnp
from jax import lax
from jax.experimental import pallas as pl
from jax.experimental.pallas import tpu as pltpu
from jax.sharding import PartitionSpec as P

HEAD_DIM = 32
SLOTS = 49
PAD = 64
KEYS = 56
GROUP = 4
SPARE = 16
norm_eps = 1e-05
mask_fill = -1000000000.0
f32 = jnp.float32
bf16 = jnp.bfloat16
MIB = 1024 * 1024


def params(limit=56):
    return pltpu.CompilerParams(vmem_limit_bytes=limit * MIB)


def whole(shape):
    return pl.BlockSpec(shape, lambda *_: (0,) * len(shape))


def dot(left, right, dims=((1,), (0,))):
    return lax.dot_general(left, right, (dims, ((), ())), preferred_element_type=f32)


NT = ((1,), (1,))
TN = ((0,), (0,))


def norm_parts(values):
    mean = jnp.mean(values, axis=-1, keepdims=True)
    centred = values - mean
    spread = jnp.mean(centred * centred, axis=-1, keepdims=True)
    return centred, lax.rsqrt(spread + norm_eps)


def norm_back(values, gain, grad):
    centred, inverse = norm_parts(values)
    unit = centred * inverse
    scaled = grad * gain
    first = jnp.mean(scaled, axis=-1, keepdims=True)
    second = jnp.mean(scaled * unit, axis=-1, keepdims=True)
    return inverse * (scaled - first - unit * second), grad * unit


def col_sum(values):
    return jnp.sum(values, axis=0, keepdims=True)


def row_blocks(rows):
    size = 256 if rows % 16 == 0 else rows
    starts = list(range(0, rows, size))
    if len(starts) > 1 and rows - starts[-1] < 128:
        starts.pop()
    return [(s, (starts[i + 1] if i + 1 < len(starts) else rows) - s) for i, s in enumerate(starts)]


def diagonal(rows_of_heads):
    lane = lax.broadcasted_iota(jnp.int32, (PAD, 128), 1)
    out = rows_of_heads[3 * PAD :]
    for head in (2, 1, 0):
        out = jnp.where(lane < (head + 1) * HEAD_DIM, rows_of_heads[head * PAD : (head + 1) * PAD], out)
    return out


def spread(rows, block_mask):
    return jnp.concatenate([rows] * GROUP, axis=0) * block_mask


def block_mask_of():
    row = lax.broadcasted_iota(jnp.int32, (GROUP * PAD, 128), 0) // PAD
    lane = lax.broadcasted_iota(jnp.int32, (GROUP * PAD, 128), 1) // HEAD_DIM
    return (row == lane).astype(f32).astype(bf16)


def window_rows_mask(rows, cols):
    return lax.rem(lax.broadcasted_iota(jnp.int32, (rows, cols), 0), PAD) < SLOTS


def batch_of(windows):
    return 8 if windows % 8 == 0 else windows


def step_rows(ref, step, batch):
    if batch % 8:
        return ref
    return ref.at[pl.ds(pl.multiple_of(step * batch * SLOTS, 8), batch * SLOTS + SPARE)]


def pad_windows(src, dst, step, batch):
    view = step_rows(src, step, batch)
    for j in range(batch):
        dst[j * PAD : (j + 1) * PAD, :] = view[j * SLOTS : j * SLOTS + PAD, :].astype(bf16)


def fwd_kernel(groups, tokens, gain, shift, w, bias, pos, mask, qkv, probs, att, wp, padded, normed, att_s):
    step = pl.program_id(0)
    rows = tokens.shape[0]

    @pl.when(step == 0)
    def _():
        centred, inverse = norm_parts(tokens[...].astype(f32))
        value = (centred * inverse * gain[...] + shift[...]).astype(bf16)
        normed[0:rows, :] = value.astype(f32)
        normed[rows:, :] = jnp.zeros_like(normed[rows:, :])
        order = group_order()
        for g in range(groups):
            wp[:, g * 384 : (g + 1) * 384] = dot(w[:, g * 384 : (g + 1) * 384], order).astype(bf16)

    batch = mask.shape[0]
    pad_windows(normed, padded, step, batch)
    att_view = step_rows(att_s, step, batch)
    block_mask = block_mask_of()
    keep = window_rows_mask(batch * PAD, 384)
    left = padded[...]
    for g in range(groups):
        cols = slice(g * 384, (g + 1) * 384)
        value = dot(left, wp[:, cols]) + bias[:, cols]
        qkv[:, cols] = jnp.where(keep, value, 0.0).astype(bf16)
    for j in range(batch):
        rows_at = slice(j * PAD, (j + 1) * PAD)
        allowed = mask[j] > 0.0
        allowed = jnp.concatenate([allowed, allowed], axis=1)
        for g in range(groups):
            at = g * 384
            query = qkv[rows_at, at : at + 128]
            key = qkv[rows_at, at + 128 : at + 256]
            value = qkv[rows_at, at + 256 : at + 384]
            raw = dot(key, spread(query, block_mask), NT)[:KEYS]
            scores = raw * HEAD_DIM ** (-0.5) + pos[:, g * 256 : (g + 1) * 256]
            scores = jnp.where(allowed, scores, mask_fill)
            top = jnp.max(scores, axis=0, keepdims=True)
            power = jnp.exp(scores - top)
            total = jnp.sum(power, axis=0, keepdims=True)
            prob = power * (1.0 / total)
            prob = jnp.concatenate([prob, jnp.zeros((PAD - KEYS, 256), f32)], axis=0).astype(bf16)
            probs[j, :, g * 256 : (g + 1) * 256] = prob
            out = diagonal(dot(prob, value, TN))
            att_view[j * SLOTS : j * SLOTS + KEYS, g * 128 : (g + 1) * 128] = out[:KEYS]

    @pl.when(step == pl.num_programs(0) - 1)
    def _():
        windows = pl.num_programs(0) * batch
        value = att_s[0:rows, :]
        real = lax.broadcasted_iota(jnp.int32, value.shape, 0) < windows * SLOTS
        att[...] = jnp.where(real, value, 0.0).astype(bf16)


def attention_forward(tokens, gain, shift, w, bias, pos, mask):
    rows, width = tokens.shape
    windows = mask.shape[0]
    cols = w.shape[1]
    groups = cols // 384
    heads = groups * GROUP
    batch = batch_of(windows)
    steps = windows // batch
    quad_rows = batch * PAD
    out_shape = (
        jax.ShapeDtypeStruct((windows * PAD, cols), bf16),
        jax.ShapeDtypeStruct((windows, PAD, heads * PAD), bf16),
        jax.ShapeDtypeStruct((rows, heads * HEAD_DIM), bf16),
        jax.ShapeDtypeStruct((width, cols), bf16),
        jax.ShapeDtypeStruct((windows * PAD, width), bf16),
    )
    return pl.pallas_call(
        functools.partial(fwd_kernel, groups),
        grid=(steps,),
        in_specs=[
            whole((rows, width)),
            whole((1, width)),
            whole((1, width)),
            whole((width, cols)),
            whole((1, cols)),
            whole((KEYS, heads * PAD)),
            pl.BlockSpec((batch, KEYS, 128), lambda i: (i, 0, 0)),
        ],
        out_specs=[
            pl.BlockSpec((quad_rows, cols), lambda i: (i, 0)),
            pl.BlockSpec((batch, PAD, heads * PAD), lambda i: (i, 0, 0)),
            whole((rows, heads * HEAD_DIM)),
            whole((width, cols)),
            pl.BlockSpec((quad_rows, width), lambda i: (i, 0)),
        ],
        out_shape=out_shape,
        scratch_shapes=[
            pltpu.VMEM((rows + SPARE, width), f32),
            pltpu.VMEM((rows + SPARE, heads * HEAD_DIM), f32),
        ],
        compiler_params=params(),
        cost_estimate=pl.CostEstimate(
            flops=2 * windows * PAD * width * cols + 16 * windows * groups * 256 * 256 * 64,
            bytes_accessed=windows * PAD * cols * 4 + width * cols * 4,
            transcendentals=0,
        ),
        name="attention_forward",
    )(tokens, gain, shift, w, bias, pos, mask)


def proj_kernel(parts, *refs):
    atts, ws = refs[:parts], refs[parts : 2 * parts]
    tokens, bias, gain, shift, middle, low = refs[2 * parts :]
    for start, size in row_blocks(tokens.shape[0]):
        at = slice(start, start + size)
        value = tokens[at, :].astype(f32) + bias[...]
        for a, w in zip(atts, ws):
            value = value + dot(a[at, :], w[...])
        middle[at, :] = value
        centred, inverse = norm_parts(value)
        low[at, :] = (centred * inverse * gain[...] + shift[...]).astype(bf16)


def project(atts, ws, tokens, bias, gain, shift):
    rows, width = tokens.shape
    return pl.pallas_call(
        functools.partial(proj_kernel, len(atts)),
        out_shape=(jax.ShapeDtypeStruct((rows, width), f32), jax.ShapeDtypeStruct((rows, width), bf16)),
        compiler_params=params(),
        cost_estimate=pl.CostEstimate(flops=2 * rows * width * width, bytes_accessed=rows * width * 10, transcendentals=0),
        name="project",
    )(*atts, *ws, tokens, bias, gain, shift)


def gelu_parts(x):
    z = jnp.abs(x) * 0.7071067811865476
    t = 1.0 / (1.0 + 0.3275911 * z)
    e = jnp.exp(-z * z)
    half = t * (0.127414796 + t * (-0.142248368 + t * (0.7107068705 + t * (-0.7265760135 + t * 0.5307027145)))) * e
    cdf = jnp.where(x >= 0.0, 1.0 - half, half)
    return cdf, e * 0.3989422804014327


def mlp_kernel(first, last, order, *refs):
    low, dy, up, bias, down = refs[:5]
    refs = refs[5:]
    if not first:
        out_in, two_in = refs[:2]
        refs = refs[2:]
    if last:
        middle, bias_down, gain = refs[:3]
        refs = refs[3:]
        hidden, gpre, gbias, block_out, grad_middle, branch, sums, acc_out, acc_two = refs
    else:
        hidden, gpre, gbias, acc_out, acc_two = refs
    step = pl.program_id(0)
    rows = low.shape[0]

    @pl.when(step == 0)
    def _():
        if first:
            acc_out[...] = jnp.zeros_like(acc_out)
            acc_two[...] = jnp.zeros_like(acc_two)
        else:
            acc_out[...] = out_in[...]
            acc_two[...] = two_in[...]

    total = jnp.zeros(gbias.shape[1:], f32)
    for start, size in row_blocks(rows):
        at = slice(start, start + size)
        pre = dot(low[at, :], up[...], NT) + bias[0]
        back = dot(dy[at, :], down[...], NT)
        cdf, pdf = gelu_parts(pre)
        hid = (pre * cdf).astype(bf16)
        gp = (back * (cdf + pre * pdf)).astype(bf16)
        hidden[at, :] = hid
        gpre[at, :] = gp
        total = total + col_sum(gp.astype(f32))
        acc_out[at, :] += dot(hid, down[...])
        acc_two[at, :] += dot(gp, up[...])
    gbias[0] = total

    if last:

        @pl.when(step == pl.num_programs(0) - 1)
        def _():
            s_gain = s_shift = s_branch = s_down = jnp.zeros((1, low.shape[1]), f32)
            for start, size in row_blocks(rows):
                at = slice(start, start + size)
                mid = middle[at, :]
                block_out[at, :] = (mid + acc_out[at, :] + bias_down[...]).astype(bf16)
                two = acc_two[at, :]
                up_grad = dy[at, :].astype(f32)
                grad, for_gain = norm_back(mid, gain[...], two)
                grad = grad + up_grad
                grad_middle[at, :] = grad
                low_grad = grad.astype(bf16)
                branch[at, :] = low_grad
                s_gain += col_sum(for_gain)
                s_shift += col_sum(two)
                s_branch += col_sum(low_grad.astype(f32))
                s_down += col_sum(up_grad)
            sums[...] = jnp.concatenate([s_gain, s_shift, s_branch, s_down], axis=0)


def mlp(order, low, dy, up, bias, down, carried=None, finish=None):
    rows, width = low.shape
    units = up.shape[0]
    piece = bias.shape[2]
    steps = units // piece
    first, last = carried is None, finish is not None
    ins = [low, dy, up, bias, down]
    specs = [
        whole((rows, width)),
        whole((rows, width)),
        pl.BlockSpec((piece, width), lambda i, o: (i, 0)),
        pl.BlockSpec((1, 1, piece), lambda i, o: (o[i], 0, 0)),
        pl.BlockSpec((piece, width), lambda i, o: (i, 0)),
    ]
    outs = [
        jax.ShapeDtypeStruct((rows, units), bf16),
        jax.ShapeDtypeStruct((rows, units), bf16),
        jax.ShapeDtypeStruct(bias.shape, f32),
    ]
    out_specs = [
        pl.BlockSpec((rows, piece), lambda i, o: (0, i)),
        pl.BlockSpec((rows, piece), lambda i, o: (0, i)),
        pl.BlockSpec((1, 1, piece), lambda i, o: (o[i], 0, 0)),
    ]
    scratch = []
    if not first:
        ins += list(carried)
        specs += [whole((rows, width))] * 2
    if last:
        ins += list(finish)
        specs += [whole((rows, width)), whole((1, width)), whole((1, width))]
        outs += [
            jax.ShapeDtypeStruct((rows, width), bf16),
            jax.ShapeDtypeStruct((rows, width), f32),
            jax.ShapeDtypeStruct((rows, width), bf16),
            jax.ShapeDtypeStruct((4, width), f32),
        ]
        out_specs += [whole((rows, width))] * 3 + [whole((4, width))]
        scratch = [pltpu.VMEM((rows, width), f32)] * 2
    else:
        outs += [jax.ShapeDtypeStruct((rows, width), f32)] * 2
        out_specs += [whole((rows, width))] * 2
    return pl.pallas_call(
        functools.partial(mlp_kernel, first, last),
        grid_spec=pltpu.PrefetchScalarGridSpec(
            num_scalar_prefetch=1, grid=(steps,), in_specs=specs, out_specs=out_specs, scratch_shapes=scratch
        ),
        out_shape=tuple(outs),
        compiler_params=params(),
        cost_estimate=pl.CostEstimate(flops=8 * rows * width * units, bytes_accessed=rows * units * 4, transcendentals=0),
        name="mlp",
    )(order, *ins)


def bwd_kernel(groups, branch, wproj, qkv, probs, gqkv, bias_sum, col_sums, wide, padded):
    step = pl.program_id(0)
    rows = branch.shape[0]

    @pl.when(step == 0)
    def _():
        wide[0:rows, :] = branch[...].astype(f32)
        wide[rows:, :] = jnp.zeros_like(wide[rows:, :])
        bias_sum[...] = jnp.zeros_like(bias_sum)
        col_sums[...] = jnp.zeros_like(col_sums)

    batch = probs.shape[0]
    pad_windows(wide, padded, step, batch)
    block_mask = block_mask_of()
    scale = HEAD_DIM ** (-0.5)
    grads = dot(padded[...], wproj[...], NT)
    grads = jnp.where(window_rows_mask(batch * PAD, grads.shape[1]), grads, 0.0).astype(bf16)
    for g in range(groups):
        at = g * 384
        bias_total = jnp.zeros((KEYS, 256), f32)
        col_total = [jnp.zeros((1, 128), f32)] * 2
        for j in range(batch):
            rows_at = slice(j * PAD, (j + 1) * PAD)
            query = qkv[rows_at, at : at + 128]
            key = qkv[rows_at, at + 128 : at + 256]
            value = qkv[rows_at, at + 256 : at + 384]
            prob_low = probs[j, :, g * 256 : (g + 1) * 256]
            grad = spread(grads[rows_at, g * 128 : (g + 1) * 128], block_mask)
            prob = prob_low.astype(f32)[:KEYS]
            prob_grad = dot(value, grad, NT)[:KEYS]
            both = prob * prob_grad
            score_grad = both - prob * jnp.sum(both, axis=0, keepdims=True)
            score_grad = jnp.concatenate([score_grad, jnp.zeros((PAD - KEYS, 256), f32)], axis=0).astype(bf16)
            bias_total = bias_total + score_grad.astype(f32)[:KEYS]
            grad_value = dot(prob_low, grad).astype(bf16)
            grad_key = (dot(score_grad, spread(query, block_mask)) * scale).astype(bf16)
            grad_query = (diagonal(dot(score_grad, key, TN)) * scale).astype(bf16)
            gqkv[rows_at, at : at + 128] = grad_query
            gqkv[rows_at, at + 128 : at + 256] = grad_key
            gqkv[rows_at, at + 256 : at + 384] = grad_value
            col_total[0] = col_total[0] + col_sum(grad_query.astype(f32))
            col_total[1] = col_total[1] + col_sum(grad_value.astype(f32))
        bias_sum[:, g * 256 : (g + 1) * 256] += bias_total
        col_sums[0:1, g * 128 : (g + 1) * 128] += col_total[0]
        col_sums[1:2, g * 128 : (g + 1) * 128] += col_total[1]


def attention_backward(branch, wproj, qkv, probs):
    rows, width = branch.shape
    windows = probs.shape[0]
    cols = qkv.shape[1]
    groups = cols // 384
    heads = groups * GROUP
    batch = batch_of(windows)
    quad_rows = batch * PAD
    return pl.pallas_call(
        functools.partial(bwd_kernel, groups),
        grid=(windows // batch,),
        in_specs=[
            whole((rows, width)),
            whole((heads * HEAD_DIM, width)),
            pl.BlockSpec((quad_rows, cols), lambda i: (i, 0)),
            pl.BlockSpec((batch, PAD, heads * PAD), lambda i: (i, 0, 0)),
        ],
        out_specs=[
            pl.BlockSpec((quad_rows, cols), lambda i: (i, 0)),
            whole((KEYS, heads * PAD)),
            whole((2, heads * HEAD_DIM)),
        ],
        out_shape=(
            jax.ShapeDtypeStruct((windows * PAD, cols), bf16),
            jax.ShapeDtypeStruct((KEYS, heads * PAD), f32),
            jax.ShapeDtypeStruct((2, heads * HEAD_DIM), f32),
        ),
        scratch_shapes=[pltpu.VMEM((rows + SPARE, width), f32), pltpu.VMEM((quad_rows, width), bf16)],
        compiler_params=params(),
        cost_estimate=pl.CostEstimate(
            flops=2 * windows * PAD * width * heads * 32 + 32 * windows * groups * 256 * 256 * 64,
            bytes_accessed=windows * PAD * cols * 6,
            transcendentals=0,
        ),
        name="attention_backward",
    )(branch, wproj, qkv, probs)


def input_kernel(parts, *refs):
    gqkvs, ws = refs[:parts], refs[parts : 2 * parts]
    tokens, grad_middle, gain, grad_tokens, sums, compact = refs[2 * parts :]
    step = pl.program_id(0)
    total = dot(gqkvs[0][...], ws[0][...], NT)
    for a, w in zip(gqkvs[1:], ws[1:]):
        total = total + dot(a[...], w[...], NT)
    batch = total.shape[0] // PAD
    view = step_rows(compact, step, batch)
    for j in range(batch):
        view[j * SLOTS : j * SLOTS + KEYS, :] = total[j * PAD : j * PAD + KEYS]

    @pl.when(step == pl.num_programs(0) - 1)
    def _():
        rows = tokens.shape[0]
        windows = pl.num_programs(0) * batch
        s_gain = s_shift = jnp.zeros((1, tokens.shape[1]), f32)
        for start, size in row_blocks(rows):
            at = slice(start, start + size)
            one = compact[at, :]
            if start + size == rows:
                real = start + lax.broadcasted_iota(jnp.int32, one.shape, 0) < windows * SLOTS
                one = jnp.where(real, one, 0.0)
            grad, for_gain = norm_back(tokens[at, :].astype(f32), gain[...], one)
            grad_tokens[at, :] = (grad_middle[at, :] + grad).astype(bf16)
            s_gain += col_sum(for_gain)
            s_shift += col_sum(one)
        sums[...] = jnp.concatenate([s_gain, s_shift], axis=0)


def input_backward(gqkvs, ws, tokens, grad_middle, gain):
    rows, width = tokens.shape
    quad_rows = batch_of(gqkvs[0].shape[0] // PAD) * PAD
    steps = gqkvs[0].shape[0] // quad_rows
    return pl.pallas_call(
        functools.partial(input_kernel, len(ws)),
        grid=(steps,),
        in_specs=[pl.BlockSpec((quad_rows, a.shape[1]), lambda i: (i, 0)) for a in gqkvs]
        + [whole(w.shape) for w in ws]
        + [whole((rows, width)), whole((rows, width)), whole((1, width))],
        out_specs=[whole((rows, width)), whole((2, width))],
        out_shape=(jax.ShapeDtypeStruct((rows, width), bf16), jax.ShapeDtypeStruct((2, width), f32)),
        scratch_shapes=[pltpu.VMEM((rows + SPARE, width), f32)],
        compiler_params=params(),
        cost_estimate=pl.CostEstimate(
            flops=2 * gqkvs[0].shape[0] * width * sum(w.shape[1] for w in ws), bytes_accessed=rows * width * 10, transcendentals=0
        ),
        name="input_backward",
    )(*gqkvs, *ws, tokens, grad_middle, gain)


def weight_kernel(adds, idx, left, right, *refs):
    value = dot(left[...], right[...], TN)
    for ref in refs[:adds]:
        value = value + ref[...].astype(f32)
    refs[adds][...] = value.astype(refs[adds].dtype)


def weight_split_kernel(relative, idx, left, right, near, far, send, keep, total):
    half = keep.shape[0]
    here = idx[2]
    total[...] = dot(left[...], right[...], TN) + near[...].astype(f32)
    for out, place, at in ((send, 1 - here, 1), (keep, here, 0)):
        rows = pl.ds(pl.multiple_of(place * half, 16), half)
        if relative:
            came = far[at * half : (at + 1) * half, :]
        else:
            came = far[rows, :]
        out[...] = (total[rows, :] + came.astype(f32)).astype(bf16)


def weight_grad(idx, left, left_width, right, right_width, adds=(), split=None, dtype=bf16):
    rows = left.shape[0]
    out = (left_width, right_width)
    step = left_width // 2 if split is None and left_width % 256 == 0 else left_width
    in_specs = [
        pl.BlockSpec((rows, step), lambda i, s: (0, s[0] * (left_width // step) + i)),
        pl.BlockSpec((rows, right_width), lambda i, s: (0, s[1])),
    ] + [pl.BlockSpec((step, right_width), lambda i, s: (i, 0)) for _ in adds]
    scratch = []
    if split is None:
        kernel = functools.partial(weight_kernel, len(adds))
        out_shape = jax.ShapeDtypeStruct(out, dtype)
        out_specs = pl.BlockSpec((step, right_width), lambda i, s: (i, 0))
    else:
        kernel = functools.partial(weight_split_kernel, split == "relative")
        half = (left_width // 2, right_width)
        out_shape = (jax.ShapeDtypeStruct(half, bf16),) * 2
        out_specs = [whole(half)] * 2
        scratch = [pltpu.VMEM(out, f32)]
    return pl.pallas_call(
        kernel,
        grid_spec=pltpu.PrefetchScalarGridSpec(
            num_scalar_prefetch=1, grid=(left_width // step,), in_specs=in_specs, out_specs=out_specs, scratch_shapes=scratch
        ),
        out_shape=out_shape,
        compiler_params=params(),
        cost_estimate=pl.CostEstimate(
            flops=2 * rows * left_width * right_width, bytes_accessed=2 * rows * (left_width + right_width), transcendentals=0
        ),
        name="weight_grad",
    )(idx, left, right, *adds)


def group_order():
    at = lax.broadcasted_iota(jnp.int32, (384, 384), 1)
    source = (at % 128) // 32 * 96 + at // 128 * 32 + at % 32
    return (lax.broadcasted_iota(jnp.int32, (384, 384), 0) == source).astype(f32).astype(bf16)


def as_given(piece):
    return piece.astype(f32)


def turned(piece):
    return piece.astype(f32).T


def head_order(piece):
    order = group_order()
    groups = [dot(piece[:, g : g + 384], order, NT) for g in range(0, piece.shape[1], 384)]
    return jnp.concatenate(groups, axis=1)


def place_kernel(change, places, *refs):
    step = pl.program_id(0)
    for i, ref in enumerate(refs[:-1]):

        @pl.when(step == i)
        def _(ref=ref):
            refs[-1][...] = change(ref[...])


def place(places, pieces, shape, change=as_given):
    if change is turned:
        block = pieces[0].shape[::-1]
    else:
        block = pieces[0].shape
    return pl.pallas_call(
        functools.partial(place_kernel, change),
        grid_spec=pltpu.PrefetchScalarGridSpec(
            num_scalar_prefetch=1,
            grid=(len(pieces),),
            in_specs=[whole(p.shape) for p in pieces],
            out_specs=pl.BlockSpec(block, lambda i, s: (s[2 * i], s[2 * i + 1])),
        ),
        out_shape=jax.ShapeDtypeStruct(shape, f32),
        compiler_params=params(),
        cost_estimate=pl.CostEstimate(flops=0, bytes_accessed=shape[0] * shape[1] * 6, transcendentals=0),
        name="place",
    )(places, *pieces)


def gather_kernel(places, *refs):
    pieces, out, sems = refs[:-2], refs[-2], refs[-1]
    rows = pieces[0].shape[0]
    copies = []
    for i, piece in enumerate(pieces):
        start = pl.multiple_of(places[i] * rows, 16)
        copies.append(pltpu.make_async_copy(piece, out.at[pl.ds(start, rows)], sems.at[i]))
    for copy in copies:
        copy.start()
    for copy in copies:
        copy.wait()


def gather_rows(places, pieces):
    rows, cols = pieces[0].shape
    return pl.pallas_call(
        gather_kernel,
        grid_spec=pltpu.PrefetchScalarGridSpec(
            num_scalar_prefetch=1,
            grid=(1,),
            in_specs=[pl.BlockSpec(memory_space=pl.ANY)] * len(pieces),
            out_specs=pl.BlockSpec(memory_space=pl.ANY),
            scratch_shapes=[pltpu.SemaphoreType.DMA((len(pieces),))],
        ),
        out_shape=jax.ShapeDtypeStruct((rows * len(pieces), cols), pieces[0].dtype),
        cost_estimate=pl.CostEstimate(flops=0, bytes_accessed=rows * cols * 16, transcendentals=0),
        name="gather_rows",
    )(places, *pieces)


def pair_onehot(rel_index, table_rows):
    turned_index = jnp.pad(rel_index.T, ((0, KEYS - SLOTS), (0, PAD - SLOTS)), constant_values=-1)
    offsets = jnp.arange(table_rows, dtype=jnp.int32)
    return (turned_index[None] == offsets[:, None, None]).astype(bf16)


def position_rows(onehot, table):
    rows, heads = table.shape
    flat = dot(onehot.reshape(rows, KEYS * PAD), table, TN)
    value = jnp.transpose(flat.reshape(KEYS, PAD, heads), (0, 2, 1)).reshape(KEYS, heads * PAD)
    return jnp.where(jnp.arange(KEYS)[:, None] < SLOTS, value, 2 * mask_fill)


def table_grad(onehot, sums):
    rows = onehot.shape[0]
    heads = sums.shape[1] // PAD
    flat = jnp.transpose(sums.reshape(KEYS, heads, PAD), (0, 2, 1)).reshape(KEYS * PAD, heads)
    high = flat.astype(bf16)
    rest = (flat - high.astype(f32)).astype(bf16)
    low = (flat - high.astype(f32) - rest.astype(f32)).astype(bf16)
    both = dot(onehot.reshape(rows, KEYS * PAD), jnp.concatenate([high, rest, low], axis=1))
    return both[:, :heads] + both[:, heads : 2 * heads] + both[:, 2 * heads :]


def window_mask(labels):
    shaped = labels.reshape(-1, SLOTS)
    keys = jnp.pad(shaped, ((0, 0), (0, KEYS - SLOTS)), constant_values=-2)[:, :, None]
    queries = jnp.pad(shaped, ((0, 0), (0, PAD - SLOTS)), constant_values=-3)
    queries = jnp.concatenate([queries, queries], axis=1)[:, None, :]
    key_at = jnp.arange(KEYS)[None, :, None]
    query_at = (jnp.arange(128) % PAD)[None, None, :]
    allowed = (keys == queries) & ((keys >= 0) | (key_at == query_at))
    outside = (key_at >= SLOTS) | (query_at >= SLOTS)
    return (allowed | outside).astype(f32)


def qkv_bias_row(bias_query, bias_value):
    groups = bias_query.shape[0] // 128
    query = bias_query.astype(f32).reshape(groups, 128)
    value = bias_value.astype(f32).reshape(groups, 128)
    return jnp.stack([query, jnp.zeros_like(query), value], axis=1).reshape(1, -1)


def row(vector):
    return vector.astype(f32).reshape(1, -1)


class Links:
    def __init__(self):
        at = lax.axis_index("dp")
        self.core = at % 2
        self.x = at // 2 % 2
        self.z = at // 4
        self.inner = (self.z == 1) | (self.z == 2)

    def y_swap(self, value):
        return lax.ppermute(value, "mp", [(0, 1), (1, 0)])

    def flip(self, value, bit):
        return lax.ppermute(value, "dp", [(i, i ^ bit) for i in range(16)])

    def core_swap(self, value):
        return self.flip(value, 1)

    def x_swap(self, value):
        return self.flip(value, 2)

    def z_pairs(self, value):
        return self.flip(value, 4)

    def z_move(self, value, pairs):
        return lax.ppermute(value, "dp", [(s * 4 + i, d * 4 + i) for s, d in pairs for i in range(4)])

    def z_sum(self, value):
        value = value + self.z_move(value, [(0, 1), (3, 2)])
        value = value + self.z_move(value, [(1, 2), (2, 1)])
        return jnp.where(self.inner, value, self.z_move(value, [(1, 0), (2, 3)]))

    def order(self):
        places = [2 * (self.core ^ (r >> 1)) + (self.x ^ (r & 1)) for r in range(4)]
        return jnp.stack(places).astype(jnp.int32)


def index_of(*items):
    return jnp.stack([jnp.asarray(i, jnp.int32) for i in items])


def step_grads(links, family):
    first = family("rem", False, (), None)
    second = family("rem", True, (links.core_swap(first),), None)
    far = links.y_swap(second)
    third = family("loc", False, (), None)
    send, keep = family("loc", True, (links.core_swap(third), far), True)
    piece = links.z_sum(keep + links.x_swap(send))
    beside = links.x_swap(piece)
    return [piece, beside, links.core_swap(piece), links.core_swap(beside)]


def on_device(
    direct,
    tokens,
    image_ids,
    rel_index,
    gain_one,
    shift_one,
    w_qkv,
    bias_query,
    bias_value,
    bias_table,
    w_proj,
    bias_proj,
    gain_two,
    shift_two,
    w_up,
    bias_up,
    w_down,
    bias_down,
    cotangent,
):
    mp = lax.axis_index("mp")
    real_rows = tokens.shape[0]
    labels = lax.dynamic_slice(image_ids, (mp * real_rows,), (real_rows,))
    spare = -real_rows % 16
    tokens = jnp.pad(tokens, ((0, spare), (0, 0)))
    cotangent = jnp.pad(cotangent, ((0, spare), (0, 0)))
    width = tokens.shape[1]
    table_rows = bias_table.shape[0]
    onehot = pair_onehot(rel_index, table_rows)
    mask = window_mask(labels)
    zero = jnp.zeros((), jnp.int32)

    local = (w_qkv, bias_query, bias_value, bias_table, w_proj, w_up.T, bias_up, w_down)
    if direct:
        links = Links()
        core, x = links.core, links.x
        order = links.order()
        heads_cols = bias_query.shape[0]
        units = bias_up.shape[0]
        small = jnp.concatenate([bias_query, bias_value, bias_up, bias_table.reshape(-1)])
        small = links.y_swap(small)
        query_rem = small[:heads_cols]
        value_rem = small[heads_cols : 2 * heads_cols]
        up_bias_rem = small[2 * heads_cols : 2 * heads_cols + units]
        table_rem = small[2 * heads_cols + units :].reshape(bias_table.shape)

        def fetch(weight):
            rows = weight.shape[0] // 4
            piece = lax.dynamic_slice(weight, (order[0] * rows, 0), (rows, weight.shape[1]))
            piece = links.y_swap(piece)
            beside = links.x_swap(piece)
            return gather_rows(order, (piece, beside, links.core_swap(piece), links.core_swap(beside)))

        qkv_rem = fetch(w_qkv)
        proj_rem = fetch(w_proj)
        piece_rows = units // 4
        own = [lax.dynamic_slice(w, (order[0] * piece_rows, 0), (piece_rows, width)) for w in (local[5], w_down)]
        even = links.z % 2 == 0
        came = links.y_swap(jnp.where(even, own[0], own[1]))
        swapped = links.z_pairs(came)
        both = []
        for piece in (jnp.where(even, came, swapped), jnp.where(even, swapped, came)):
            beside = links.x_swap(piece)
            both.append(jnp.concatenate([piece, beside, links.core_swap(piece), links.core_swap(beside)], axis=0))
        remote = (qkv_rem, query_rem, value_rem, table_rem, proj_rem, both[0], up_bias_rem, both[1])
        names = ("loc", "rem")
        parts = dict(loc=local, rem=remote)
        orders = dict(loc=jnp.arange(4, dtype=jnp.int32), rem=order)
    else:
        axes = (1, 0, 0, 1, 0, 0, 0, 0)
        names = ("all",)
        parts = dict(all=tuple(lax.all_gather(w, "mp", axis=a, tiled=True) for w, a in zip(local, axes)))
        orders = dict(all=jnp.arange(parts["all"][6].shape[0] // 384, dtype=jnp.int32))

    gain_first, shift_first = row(gain_one), row(shift_one)
    gain_second = row(gain_two)
    qkv, probs, att, w_in, pos = {}, {}, {}, {}, {}
    for name in names:
        w, b_query, b_value, table = parts[name][:4]
        qkv[name], probs[name], att[name], w_in[name], normed = attention_forward(
            tokens, gain_first, shift_first, w, qkv_bias_row(b_query, b_value), position_rows(onehot, table), mask
        )
    w_projs = {n: parts[n][4] for n in names}
    middle, low_two = project(
        [att[n] for n in names], [w_projs[n] for n in names], tokens, row(bias_proj), gain_second, row(shift_two)
    )
    hidden, gpre, up_bias_grad = {}, {}, {}
    carried = None
    for i, name in enumerate(reversed(names)):
        w_up_t, b_up, w_dn = parts[name][5:]
        finish = (middle, row(bias_down), gain_second) if i == len(names) - 1 else None
        bias = b_up.astype(f32).reshape(-1, 1, 384)
        got = mlp(orders[name], low_two, cotangent, w_up_t, bias, w_dn, carried, finish)
        hidden[name], gpre[name], up_bias_grad[name] = got[:3]
        carried = got[3:5]
    block_out, grad_middle, branch, sums_two = got[3:7]

    gqkv, bias_sums, col_sums = {}, {}, {}
    for name in reversed(names):
        gqkv[name], bias_sums[name], col_sums[name] = attention_backward(branch, w_projs[name], qkv[name], probs[name])
    grad_tokens, sums_one = input_backward(
        [gqkv[n] for n in names], [w_in[n] for n in names], tokens, grad_middle, gain_first
    )
    table_sums = {n: table_grad(onehot, bias_sums[n]) for n in names}

    if direct:

        def down_family(part, mine, adds, split):
            block = (0 if mine else 1) if part == "rem" else (core if mine else 1 - core)
            return weight_grad(
                index_of(block, 0, x), hidden[part], units // 2, cotangent, width, adds, "relative" if split else None
            )

        def up_family(part, mine, adds, split):
            block = (0 if mine else 1) if part == "rem" else (core if mine else 1 - core)
            return weight_grad(
                index_of(block, 0, x), gpre[part], units // 2, low_two, width, adds, "relative" if split else None
            )

        def proj_family(part, mine, adds, split):
            block = core if mine else 1 - core
            return weight_grad(
                index_of(0, block, x), att[part], att[part].shape[1], branch, width // 2, adds, "natural" if split else None
            )

        def qkv_family(part, mine, adds, split):
            block = core if mine else 1 - core
            return weight_grad(
                index_of(block, 0, x), normed, width // 2, gqkv[part], gqkv[part].shape[1], adds, "natural" if split else None
            )

        row_places = jnp.stack([order, jnp.zeros_like(order)], axis=1).reshape(-1)
        col_places = jnp.stack([jnp.zeros_like(order), order], axis=1).reshape(-1)
        proj_places = jnp.stack([order % 2, order // 2], axis=1).reshape(-1)
        grad_down = place(row_places, step_grads(links, down_family), w_down.shape)
        grad_up = place(col_places, step_grads(links, up_family), w_up.shape, turned)
        grad_proj = place(proj_places, step_grads(links, proj_family), w_proj.shape)
        grad_qkv = place(row_places, step_grads(links, qkv_family), w_qkv.shape, head_order)

        def reduce_small(shared, loc, rem):
            value = jnp.concatenate([shared, loc, rem])
            value = value + links.core_swap(value)
            value = value + links.x_swap(value)
            value = links.z_sum(value)
            n, m = shared.shape[0], loc.shape[0]
            far = links.y_swap(jnp.concatenate([value[:n], value[n + m :]]))
            return value[: n + m] + far

        def flat(name):
            return [col_sums[name].reshape(-1), up_bias_grad[name].reshape(-1), table_sums[name].reshape(-1)]

        shared = sums_two.reshape(-1)
        early = reduce_small(shared, jnp.concatenate(flat("loc")), jnp.concatenate(flat("rem")))
        late = reduce_small(sums_one.reshape(-1), jnp.zeros((0,), f32), jnp.zeros((0,), f32)).reshape(2, width)
        two = early[: 4 * width].reshape(4, width)
        early = early[4 * width :]
        grad_query_b, grad_value_b = early[:heads_cols], early[heads_cols : 2 * heads_cols]
        grad_up_bias = early[2 * heads_cols : 2 * heads_cols + units]
        grad_table = early[2 * heads_cols + units :].reshape(bias_table.shape)
    else:
        none = index_of(0, 0, 0)

        def summed(value, axis):
            value = lax.psum_scatter(value, "mp", scatter_dimension=axis, tiled=True)
            return lax.psum(value, "dp")

        def wide(value, axis):
            return summed(value.astype(bf16), axis).astype(f32)

        def full(left, right):
            return weight_grad(none, left, left.shape[1], right, right.shape[1])

        h, g, q = hidden["all"], gpre["all"], gqkv["all"]
        grad_down = wide(full(h, cotangent), 0)
        grad_up = wide(full(g, low_two).T, 1)
        grad_proj = wide(full(att["all"], branch), 0)
        by_group = full(normed, q).reshape(width, -1, 384)
        natural = dot(by_group.reshape(-1, 384), group_order(), NT).reshape(width, -1)
        grad_qkv = wide(natural, 1)
        grad_query_b = summed(col_sums["all"][0], 0)
        grad_value_b = summed(col_sums["all"][1], 0)
        grad_up_bias = summed(up_bias_grad["all"].reshape(-1), 0)
        grad_table = summed(table_sums["all"], 1)
        two, late = lax.psum((sums_two, sums_one), ("dp", "mp"))
    return (
        block_out[:real_rows],
        grad_tokens[:real_rows],
        late[0],
        late[1],
        grad_qkv,
        grad_query_b,
        grad_value_b,
        grad_table,
        grad_proj,
        two[2],
        two[0],
        two[1],
        grad_up,
        grad_up_bias,
        grad_down,
        two[3],
    )


def solution(mesh):
    direct = mesh.shape["dp"] == 16 and mesh.shape["mp"] == 2
    return jax.shard_map(
        functools.partial(on_device, direct),
        mesh=mesh,
        in_specs=(
            P(("dp", "mp"), None),
            P("dp"),
            P(),
            P(),
            P(),
            P(None, "mp"),
            P("mp"),
            P("mp"),
            P(None, "mp"),
            P("mp", None),
            P(),
            P(),
            P(),
            P(None, "mp"),
            P("mp"),
            P("mp", None),
            P(),
            P(("dp", "mp"), None),
        ),
        out_specs=(
            P(("dp", "mp"), None),
            P(("dp", "mp"), None),
            P(),
            P(),
            P(None, "mp"),
            P("mp"),
            P("mp"),
            P(None, "mp"),
            P("mp", None),
            P(),
            P(),
            P(),
            P(None, "mp"),
            P("mp"),
            P("mp", None),
            P(),
        ),
        check_vma=False,
    )
```

```python
import functools

import jax
import jax.numpy as jnp
from jax import lax
from jax.experimental import pallas as pl
from jax.experimental.pallas import tpu as pltpu
from jax.sharding import PartitionSpec as P

HEAD_DIM = 32
SLOTS = 49
PAD = 64
KEYS = 56
PIECE = 384
GROUP = 4
SPARE = 16
norm_eps = 1e-05
mask_fill = -1000000000.0
f32 = jnp.float32
bf16 = jnp.bfloat16
MIB = 1024 * 1024


def cost(micros):
    return pl.CostEstimate(flops=int(micros * 1.0e9), bytes_accessed=int(micros * 1.0e5), transcendentals=0)


def params(limit=56):
    return pltpu.CompilerParams(vmem_limit_bytes=limit * MIB)


def whole(shape):
    return pl.BlockSpec(shape, lambda *_: (0,) * len(shape))


def dot(left, right, dims=((1,), (0,))):
    return lax.dot_general(left, right, (dims, ((), ())), preferred_element_type=f32)


NT = ((1,), (1,))
TN = ((0,), (0,))


def norm_parts(values):
    mean = jnp.mean(values, axis=-1, keepdims=True)
    centred = values - mean
    spread = jnp.mean(centred * centred, axis=-1, keepdims=True)
    return centred, lax.rsqrt(spread + norm_eps)


def norm_back(values, gain, grad):
    centred, inverse = norm_parts(values)
    unit = centred * inverse
    scaled = grad * gain
    first = jnp.mean(scaled, axis=-1, keepdims=True)
    second = jnp.mean(scaled * unit, axis=-1, keepdims=True)
    return inverse * (scaled - first - unit * second), grad * unit


def col_sum(values):
    return jnp.sum(values, axis=0, keepdims=True)


def row_blocks(rows):
    size = 256 if rows % 16 == 0 else rows
    starts = list(range(0, rows, size))
    if len(starts) > 1 and rows - starts[-1] < 128:
        starts.pop()
    return [(s, (starts[i + 1] if i + 1 < len(starts) else rows) - s) for i, s in enumerate(starts)]


def diagonal(rows_of_heads):
    lane = lax.broadcasted_iota(jnp.int32, (PAD, 128), 1)
    out = rows_of_heads[3 * PAD :]
    for head in (2, 1, 0):
        out = jnp.where(lane < (head + 1) * HEAD_DIM, rows_of_heads[head * PAD : (head + 1) * PAD], out)
    return out


def spread(rows, block_mask):
    return jnp.concatenate([rows] * GROUP, axis=0) * block_mask


def block_mask_of():
    row = lax.broadcasted_iota(jnp.int32, (GROUP * PAD, 128), 0) // PAD
    lane = lax.broadcasted_iota(jnp.int32, (GROUP * PAD, 128), 1) // HEAD_DIM
    return (row == lane).astype(f32).astype(bf16)


def window_rows_mask(rows, cols):
    return lax.rem(lax.broadcasted_iota(jnp.int32, (rows, cols), 0), PAD) < SLOTS


def batch_of(windows):
    return 8 if windows % 8 == 0 else windows


def step_rows(ref, step, batch):
    if batch % 8:
        return ref
    return ref.at[pl.ds(pl.multiple_of(step * batch * SLOTS, 8), batch * SLOTS + SPARE)]


def pad_windows(src, dst, step, batch):
    view = step_rows(src, step, batch)
    for j in range(batch):
        dst[j * PAD : (j + 1) * PAD, :] = view[j * SLOTS : j * SLOTS + PAD, :].astype(bf16)


def fwd_kernel(groups, pieces, places, tokens, rows8, small, pos, mask, *refs):
    ws, refs = refs[: max(pieces, 1)], refs[max(pieces, 1) :]
    qkv, probs, att, wp, padded = refs[:5]
    normed, att_s, pos_s = refs[-3:]
    step = pl.program_id(0)
    rows = tokens.shape[0]

    @pl.when(step == 0)
    def _():
        centred, inverse = norm_parts(tokens[...].astype(f32))
        value = (centred * inverse * rows8[0:1, :] + rows8[1:2, :]).astype(bf16)
        normed[0:rows, :] = value.astype(f32)
        normed[rows:, :] = jnp.zeros_like(normed[rows:, :])
        order = group_order()
        for r, w in enumerate(ws):
            if pieces:
                size = w.shape[0]
                at = pl.ds(pl.multiple_of(places[r] * size, 16), size)
            else:
                at = slice(0, w.shape[0])
            for g in range(groups):
                cols = slice(g * 384, (g + 1) * 384)
                wp[at, cols] = dot(w[:, cols], order).astype(bf16)
        slot = lax.broadcasted_iota(jnp.int32, (KEYS, 128), 0) < SLOTS
        for h in range(0, groups * GROUP, 2):
            both = jnp.concatenate([pos[h], pos[h + 1]], axis=1)
            pos_s[:, h * PAD : (h + 2) * PAD] = jnp.where(slot, both, 2 * mask_fill)

    batch = mask.shape[0]
    pad_windows(normed, padded, step, batch)
    att_view = step_rows(att_s, step, batch)
    block_mask = block_mask_of()
    keep = window_rows_mask(batch * PAD, 128)
    left = padded[...]
    for g in range(groups):
        value = dot(left, wp[:, g * 384 : (g + 1) * 384])
        for part, bias in enumerate((small[g], None, small[groups + g])):
            piece = value[:, part * 128 : (part + 1) * 128]
            if bias is not None:
                piece = piece + bias
            qkv[:, g * 384 + part * 128 : g * 384 + (part + 1) * 128] = jnp.where(keep, piece, 0.0).astype(bf16)
    for j in range(batch):
        rows_at = slice(j * PAD, (j + 1) * PAD)
        allowed = mask[j] > 0.0
        allowed = jnp.concatenate([allowed, allowed], axis=1)
        for g in range(groups):
            at = g * 384
            query = qkv[rows_at, at : at + 128]
            key = qkv[rows_at, at + 128 : at + 256]
            value = qkv[rows_at, at + 256 : at + 384]
            raw = dot(key, spread(query, block_mask), NT)[:KEYS]
            scores = raw * HEAD_DIM ** (-0.5) + pos_s[:, g * 256 : (g + 1) * 256]
            scores = jnp.where(allowed, scores, mask_fill)
            top = jnp.max(scores, axis=0, keepdims=True)
            power = jnp.exp(scores - top)
            total = jnp.sum(power, axis=0, keepdims=True)
            prob = power * (1.0 / total)
            prob = jnp.concatenate([prob, jnp.zeros((PAD - KEYS, 256), f32)], axis=0).astype(bf16)
            probs[j, :, g * 256 : (g + 1) * 256] = prob
            out = diagonal(dot(prob, value, TN))
            att_view[j * SLOTS : j * SLOTS + KEYS, g * 128 : (g + 1) * 128] = out[:KEYS]

    @pl.when(step == pl.num_programs(0) - 1)
    def _():
        windows = pl.num_programs(0) * batch
        value = att_s[0:rows, :]
        real = lax.broadcasted_iota(jnp.int32, value.shape, 0) < windows * SLOTS
        att[...] = jnp.where(real, value, 0.0).astype(bf16)


def attention_forward(places, tokens, rows8, small, pos, mask, ws):
    rows, width = tokens.shape
    windows = mask.shape[0]
    pieces = len(ws) if len(ws) > 1 else 0
    heads = pos.shape[0]
    groups = heads // GROUP
    cols = groups * 384
    batch = batch_of(windows)
    steps = windows // batch
    quad_rows = batch * PAD
    out_shape = [
        jax.ShapeDtypeStruct((windows * PAD, cols), bf16),
        jax.ShapeDtypeStruct((windows, PAD, heads * PAD), bf16),
        jax.ShapeDtypeStruct((rows, heads * HEAD_DIM), bf16),
        jax.ShapeDtypeStruct((width, cols), bf16),
        jax.ShapeDtypeStruct((windows * PAD, width), bf16),
    ]
    out_specs = [
        pl.BlockSpec((quad_rows, cols), lambda i, s: (i, 0)),
        pl.BlockSpec((batch, PAD, heads * PAD), lambda i, s: (i, 0, 0)),
        whole((rows, heads * HEAD_DIM)),
        whole((width, cols)),
        pl.BlockSpec((quad_rows, width), lambda i, s: (i, 0)),
    ]
    return pl.pallas_call(
        functools.partial(fwd_kernel, groups, pieces),
        grid_spec=pltpu.PrefetchScalarGridSpec(
            num_scalar_prefetch=1,
            grid=(steps,),
            in_specs=[
                whole((rows, width)),
                whole(rows8.shape),
                whole(small.shape),
                whole(pos.shape),
                pl.BlockSpec((batch, KEYS, 128), lambda i, s: (i, 0, 0)),
            ]
            + [whole(w.shape) for w in ws],
            out_specs=out_specs,
            scratch_shapes=[
                pltpu.VMEM((rows + SPARE, width), f32),
                pltpu.VMEM((rows + SPARE, heads * HEAD_DIM), f32),
                pltpu.VMEM((KEYS, heads * PAD), f32),
            ],
        ),
        out_shape=tuple(out_shape),
        compiler_params=params(),
        cost_estimate=cost(11 * groups / 3),
        name="attention_forward",
    )(places, tokens, rows8, small, pos, mask, *ws)


def proj_kernel(parts, pieces, places, *refs):
    atts, ws = refs[:parts], list(refs[parts : 2 * parts - (1 if pieces else 0)])
    refs = refs[parts + len(ws) :]
    tokens, rows8, middle, low = refs[pieces : pieces + 4]
    if pieces:
        joined = refs[pieces + 4]
        for r, piece in enumerate(refs[:pieces]):
            size = piece.shape[1]
            joined[:, pl.ds(pl.multiple_of(places[r] * size, 128), size)] = piece[...]
        ws.append(joined)
    for start, size in row_blocks(tokens.shape[0]):
        at = slice(start, start + size)
        value = tokens[at, :].astype(f32) + rows8[2:3, :]
        for a, w in zip(atts, ws):
            value = value + dot(a[at, :], w[...])
        middle[at, :] = value
        centred, inverse = norm_parts(value)
        low[at, :] = (centred * inverse * rows8[3:4, :] + rows8[4:5, :]).astype(bf16)


def project(places, atts, ws, pieces, tokens, rows8):
    rows, width = tokens.shape
    ins = [*atts, *ws, *pieces, tokens, rows8]
    out_shape = [jax.ShapeDtypeStruct((rows, width), f32), jax.ShapeDtypeStruct((rows, width), bf16)]
    if pieces:
        out_shape.append(jax.ShapeDtypeStruct((pieces[0].shape[0], width), bf16))
    return pl.pallas_call(
        functools.partial(proj_kernel, len(atts), len(pieces)),
        grid_spec=pltpu.PrefetchScalarGridSpec(
            num_scalar_prefetch=1,
            grid=(1,),
            in_specs=[whole(v.shape) for v in ins],
            out_specs=[whole(o.shape) for o in out_shape],
        ),
        out_shape=tuple(out_shape),
        compiler_params=params(),
        cost_estimate=cost(5),
        name="project",
    )(places, *ins)


def gelu_parts(x):
    z = jnp.abs(x) * 0.7071067811865476
    t = 1.0 / (1.0 + 0.3275911 * z)
    e = jnp.exp(-z * z)
    half = t * (0.127414796 + t * (-0.142248368 + t * (0.7107068705 + t * (-0.7265760135 + t * 0.5307027145)))) * e
    cdf = jnp.where(x >= 0.0, 1.0 - half, half)
    return cdf, e * 0.3989422804014327


def mlp_kernel(first, last, held_pieces, base, order, *refs):
    low, dy, small, rows8 = refs[:4]
    ws, refs = refs[4 : 8 if held_pieces else 6], refs[8 if held_pieces else 6 :]
    if not first:
        out_in, two_in = refs[:2]
        refs = refs[2:]
    if last:
        middle, own, other, gbias, block_out, grad_middle, branch, sums = refs[:8]
        acc_out, acc_two, hid_s, gp_s = refs[8:12]
        refs = refs[12:]
    else:
        own, other, gbias, acc_out, acc_two, hid_s, gp_s = refs[:7]
        refs = refs[7:]
    step = pl.program_id(0)
    rows = low.shape[0]
    if held_pieces:
        held, sems = refs
        copies = []
        for i, w in enumerate(ws):
            r, k = i // 2, i % 2
            copies.append(pltpu.make_async_copy(w, held.at[k, r * PIECE : (r + 1) * PIECE], sems.at[i]))
        for copy in copies:
            copy.start()
        for copy in copies:
            copy.wait()
        up, down = held.at[0], held.at[1]
        up_dims, back_dims = NT, ((1,), (0,))
    else:
        up, down = ws
        up_dims, back_dims = ((1,), (0,)), NT

    @pl.when(step == 0)
    def _():
        if first:
            acc_out[...] = jnp.zeros_like(acc_out)
            acc_two[...] = jnp.zeros_like(acc_two)
        else:
            acc_out[...] = out_in[...]
            acc_two[...] = two_in[...]

    bias = [small[base + 3 * order[2 * step + t // 3] + t % 3] for t in range(6)]
    bias = jnp.concatenate(bias, axis=1)
    total = jnp.zeros(bias.shape, f32)
    for start, size in row_blocks(rows):
        at = slice(start, start + size)
        pre = dot(low[at, :], up[...], up_dims) + bias
        back = dot(dy[at, :], down[...], NT)
        cdf, pdf = gelu_parts(pre)
        hid = (pre * cdf).astype(bf16)
        gp = (back * (cdf + pre * pdf)).astype(bf16)
        hid_s[at, :] = hid
        gp_s[at, :] = gp
        total = total + col_sum(gp.astype(f32))
        acc_out[at, :] += dot(hid, down[...])
        acc_two[at, :] += dot(gp, up[...], back_dims)
    gbias[0] = total
    grad_down = dot(hid_s[...], dy[...], TN).astype(bf16)
    grad_up = dot(gp_s[...], low[...], TN).astype(bf16)
    if held_pieces:
        for out, at in ((own, 0), (other, PIECE)):
            out[0:PIECE, :] = grad_down[at : at + PIECE]
            out[PIECE:, :] = grad_up[at : at + PIECE]
    else:
        for out, now in ((own, step < pl.num_programs(0) // 2), (other, step >= pl.num_programs(0) // 2)):

            @pl.when(now)
            def _(out=out):
                for t in range(2):
                    at, end = 2 * t * PIECE, (2 * t + 1) * PIECE
                    out[at:end, :] = grad_down[t * PIECE : (t + 1) * PIECE]
                    out[end : end + PIECE, :] = grad_up[t * PIECE : (t + 1) * PIECE]

    if last:

        @pl.when(step == pl.num_programs(0) - 1)
        def _():
            s_gain = s_shift = s_branch = s_down = jnp.zeros((1, low.shape[1]), f32)
            for start, size in row_blocks(rows):
                at = slice(start, start + size)
                mid = middle[at, :]
                block_out[at, :] = (mid + acc_out[at, :] + rows8[5:6, :]).astype(bf16)
                two = acc_two[at, :]
                up_grad = dy[at, :].astype(f32)
                grad, for_gain = norm_back(mid, rows8[3:4, :], two)
                grad = grad + up_grad
                grad_middle[at, :] = grad
                low_grad = grad.astype(bf16)
                branch[at, :] = low_grad
                s_gain += col_sum(for_gain)
                s_shift += col_sum(two)
                s_branch += col_sum(low_grad.astype(f32))
                s_down += col_sum(up_grad)
            sums[...] = jnp.concatenate([s_gain, s_shift, s_branch, s_down], axis=0)


def mlp(order, low, dy, small, base, rows8, ws, carried=None, middle=None):
    rows, width = low.shape
    held = isinstance(ws, list)
    units = 2 * PIECE if held else ws[1].shape[0]
    steps = units // (2 * PIECE)
    first, last = carried is None, middle is not None
    ins = [low, dy, small, rows8, *ws]
    specs = [whole((rows, width)), whole((rows, width)), whole(small.shape), whole(rows8.shape)]
    if held:
        specs += [pl.BlockSpec(memory_space=pl.ANY)] * 4
        grads = [jax.ShapeDtypeStruct((2 * PIECE, width), bf16)] * 2
        grad_specs = [whole((2 * PIECE, width))] * 2
    else:
        specs += [
            pl.BlockSpec((width, 2 * PIECE), lambda i, o: (0, o[2 * i] // 2)),
            pl.BlockSpec((2 * PIECE, width), lambda i, o: (o[2 * i] // 2, 0)),
        ]
        many = steps // 2
        grads = [jax.ShapeDtypeStruct((many * 4 * PIECE, width), bf16)] * 2
        grad_specs = [
            pl.BlockSpec((4 * PIECE, width), lambda i, o: (jnp.minimum(i, many - 1), 0)),
            pl.BlockSpec((4 * PIECE, width), lambda i, o: (jnp.maximum(i - many, 0), 0)),
        ]
    outs = [*grads, jax.ShapeDtypeStruct((steps, 1, 2 * PIECE), f32)]
    out_specs = [*grad_specs, pl.BlockSpec((1, 1, 2 * PIECE), lambda i, o: (i, 0, 0))]
    scratch = []
    if not first:
        ins += list(carried)
        specs += [whole((rows, width))] * 2
    if last:
        ins.append(middle)
        specs.append(whole((rows, width)))
        outs += [
            jax.ShapeDtypeStruct((rows, width), bf16),
            jax.ShapeDtypeStruct((rows, width), f32),
            jax.ShapeDtypeStruct((rows, width), bf16),
            jax.ShapeDtypeStruct((4, width), f32),
        ]
        out_specs += [whole((rows, width))] * 3 + [whole((4, width))]
        scratch = [pltpu.VMEM((rows, width), f32)] * 2
    else:
        outs += [jax.ShapeDtypeStruct((rows, width), f32)] * 2
        out_specs += [whole((rows, width))] * 2
    scratch += [pltpu.VMEM((rows, 2 * PIECE), bf16)] * 2
    if held:
        scratch += [pltpu.VMEM((2, 2 * PIECE, width), bf16), pltpu.SemaphoreType.DMA((4,))]
    return pl.pallas_call(
        functools.partial(mlp_kernel, first, last, held, base),
        grid_spec=pltpu.PrefetchScalarGridSpec(
            num_scalar_prefetch=1, grid=(steps,), in_specs=specs, out_specs=out_specs, scratch_shapes=scratch
        ),
        out_shape=tuple(outs),
        compiler_params=params(),
        cost_estimate=cost(11 * steps),
        name="mlp",
    )(order, *ins)


def bwd_kernel(parts, each, with_proj, core, branch, normed, *refs):
    units = parts * each
    atts, refs = refs[: parts * with_proj], refs[parts * with_proj :]
    wprojs, qkvs, probs = refs[:units], refs[units : 2 * units], refs[2 * units : 3 * units]
    gqkv, bias_sum, col_sums, theirs = refs[3 * units : 3 * units + 4]
    mine, (wide, padded, wcat, total) = refs[3 * units + 4 : -4], refs[-4:]
    step = pl.program_id(0)
    rows = branch.shape[0]
    half = normed.shape[1] // 2

    @pl.when(step == 0)
    def _():
        wide[0:rows, :] = branch[...].astype(f32)
        wide[rows:, :] = jnp.zeros_like(wide[rows:, :])
        bias_sum[...] = jnp.zeros_like(bias_sum)
        col_sums[...] = jnp.zeros_like(col_sums)
        for u in range(units):
            wcat[u * 128 : (u + 1) * 128, :] = wprojs[u][...]
        if with_proj:
            for out_at, place in ((mine, core[0]), (None, 1 - core[0])):
                right = branch[:, pl.ds(pl.multiple_of(place * half, 128), half)]
                for p in range(parts):
                    value = dot(atts[p][...], right, TN).astype(bf16)
                    if out_at is None:
                        theirs[p, :, each * 384 :] = value
                    else:
                        mine[p][:, each * 384 :] = value

    batch = probs[0].shape[0]
    pad_windows(wide, padded, step, batch)
    block_mask = block_mask_of()
    scale = HEAD_DIM ** (-0.5)
    grads = dot(padded[...], wcat[...], NT)
    grads = jnp.where(window_rows_mask(batch * PAD, grads.shape[1]), grads, 0.0).astype(bf16)
    for u in range(units):
        qkv, at = qkvs[u], u * 384
        bias_total = jnp.zeros((KEYS, 256), f32)
        col_total = [jnp.zeros((1, 128), f32)] * 2
        for j in range(batch):
            rows_at = slice(j * PAD, (j + 1) * PAD)
            query = qkv[rows_at, 0:128]
            key = qkv[rows_at, 128:256]
            value = qkv[rows_at, 256:384]
            prob_low = probs[u][j]
            grad = spread(grads[rows_at, u * 128 : (u + 1) * 128], block_mask)
            prob = prob_low.astype(f32)[:KEYS]
            prob_grad = dot(value, grad, NT)[:KEYS]
            both = prob * prob_grad
            score_grad = both - prob * jnp.sum(both, axis=0, keepdims=True)
            score_grad = jnp.concatenate([score_grad, jnp.zeros((PAD - KEYS, 256), f32)], axis=0).astype(bf16)
            bias_total = bias_total + score_grad.astype(f32)[:KEYS]
            grad_value = dot(prob_low, grad).astype(bf16)
            grad_key = (dot(score_grad, spread(query, block_mask)) * scale).astype(bf16)
            grad_query = (diagonal(dot(score_grad, key, TN)) * scale).astype(bf16)
            gqkv[rows_at, at : at + 128] = grad_query
            gqkv[rows_at, at + 128 : at + 256] = grad_key
            gqkv[rows_at, at + 256 : at + 384] = grad_value
            col_total[0] = col_total[0] + col_sum(grad_query.astype(f32))
            col_total[1] = col_total[1] + col_sum(grad_value.astype(f32))
        bias_sum[:, u * 256 : (u + 1) * 256] += bias_total
        col_sums[0:1, u * 128 : (u + 1) * 128] += col_total[0]
        col_sums[1:2, u * 128 : (u + 1) * 128] += col_total[1]
    grad = dot(normed[...], gqkv[...], TN)

    @pl.when(step == 0)
    def _():
        total[...] = grad

    @pl.when(step > 0)
    def _():
        total[...] += grad

    @pl.when(step == pl.num_programs(0) - 1)
    def _():
        for p in range(parts):
            cols = slice(p * each * 384, (p + 1) * each * 384)
            mine[p][:, 0 : each * 384] = total[pl.ds(pl.multiple_of(core[0] * half, 16), half), cols].astype(bf16)
            other = pl.ds(pl.multiple_of((1 - core[0]) * half, 16), half)
            theirs[p, :, 0 : each * 384] = total[other, cols].astype(bf16)


def attention_backward(core, branch, normed, parts, atts=()):
    rows, width = branch.shape
    units = [u for part in parts for u in part]
    windows = units[0][2].shape[0]
    count, each = len(units), len(parts[0])
    batch = batch_of(windows)
    quad_rows = batch * PAD
    half = (width // 2, each * 384 + (width // 2 if atts else 0))
    in_specs = [whole((rows, width)), pl.BlockSpec((quad_rows, width), lambda i, s: (i, 0))]
    in_specs += [whole(a.shape) for a in atts]
    in_specs += [pl.BlockSpec((128, width), lambda i, s, g=g: (g, 0)) for _, _, _, g in units]
    in_specs += [pl.BlockSpec((quad_rows, 384), lambda i, s, g=g: (i, g)) for _, _, _, g in units]
    in_specs += [pl.BlockSpec((batch, PAD, 256), lambda i, s, g=g: (i, 0, g)) for _, _, _, g in units]
    return pl.pallas_call(
        functools.partial(bwd_kernel, len(parts), each, 1 if atts else 0),
        grid_spec=pltpu.PrefetchScalarGridSpec(
            num_scalar_prefetch=1,
            grid=(windows // batch,),
            in_specs=in_specs,
            out_specs=[
                pl.BlockSpec((quad_rows, count * 384), lambda i, s: (i, 0)),
                whole((KEYS, count * 256)),
                whole((2, count * 128)),
                whole((len(parts), *half)),
            ]
            + [whole(half)] * len(parts),
            scratch_shapes=[
                pltpu.VMEM((rows + SPARE, width), f32),
                pltpu.VMEM((quad_rows, width), bf16),
                pltpu.VMEM((count * 128, width), bf16),
                pltpu.VMEM((width, count * 384), f32),
            ],
        ),
        out_shape=(
            jax.ShapeDtypeStruct((windows * PAD, count * 384), bf16),
            jax.ShapeDtypeStruct((KEYS, count * 256), f32),
            jax.ShapeDtypeStruct((2, count * 128), f32),
            jax.ShapeDtypeStruct((len(parts), *half), bf16),
        )
        + (jax.ShapeDtypeStruct(half, bf16),) * len(parts),
        compiler_params=params(),
        cost_estimate=cost(5 * count),
        name="attention_backward",
    )(core, branch, normed, *atts, *[u[0] for u in units], *[u[1] for u in units], *[u[2] for u in units])


def input_kernel(plan, arrays, *refs):
    gqkvs, refs = refs[:arrays], refs[arrays:]
    ws, refs = refs[: -6], refs[-6:]
    tokens, grad_middle, rows8, grad_tokens, sums, compact = refs
    step = pl.program_id(0)
    total = None
    for a, a_at, w, w_at, size in plan:
        term = dot(gqkvs[a][:, a_at : a_at + size], ws[w][:, w_at : w_at + size], NT)
        total = term if total is None else total + term
    batch = total.shape[0] // PAD
    view = step_rows(compact, step, batch)
    for j in range(batch):
        view[j * SLOTS : j * SLOTS + KEYS, :] = total[j * PAD : j * PAD + KEYS]

    @pl.when(step == pl.num_programs(0) - 1)
    def _():
        rows = tokens.shape[0]
        windows = pl.num_programs(0) * batch
        s_gain = s_shift = jnp.zeros((1, tokens.shape[1]), f32)
        for start, size in row_blocks(rows):
            at = slice(start, start + size)
            one = compact[at, :]
            if start + size == rows:
                real = start + lax.broadcasted_iota(jnp.int32, one.shape, 0) < windows * SLOTS
                one = jnp.where(real, one, 0.0)
            grad, for_gain = norm_back(tokens[at, :].astype(f32), rows8[0:1, :], one)
            grad_tokens[at, :] = (grad_middle[at, :] + grad).astype(bf16)
            s_gain += col_sum(for_gain)
            s_shift += col_sum(one)
        sums[...] = jnp.concatenate([s_gain, s_shift], axis=0)


def input_backward(plan, gqkvs, ws, tokens, grad_middle, rows8):
    rows, width = tokens.shape
    quad_rows = batch_of(gqkvs[0].shape[0] // PAD) * PAD
    steps = gqkvs[0].shape[0] // quad_rows
    return pl.pallas_call(
        functools.partial(input_kernel, plan, len(gqkvs)),
        grid=(steps,),
        in_specs=[pl.BlockSpec((quad_rows, a.shape[1]), lambda i: (i, 0)) for a in gqkvs]
        + [whole(w.shape) for w in ws]
        + [whole((rows, width)), whole((rows, width)), whole(rows8.shape)],
        out_specs=[whole((rows, width)), whole((2, width))],
        out_shape=(jax.ShapeDtypeStruct((rows, width), bf16), jax.ShapeDtypeStruct((2, width), f32)),
        scratch_shapes=[pltpu.VMEM((rows + SPARE, width), f32)],
        compiler_params=params(),
        cost_estimate=cost(11),
        name="input_backward",
    )(*gqkvs, *ws, tokens, grad_middle, rows8)


def stack_kernel(count, *refs):
    rows8, small = refs[-2:]
    rows8[...] = jnp.zeros_like(rows8)
    for i, ref in enumerate(refs[:count]):
        rows8[i : i + 1, :] = ref[...].astype(f32).reshape(1, -1)
    at = 0
    for ref in refs[count:-2]:
        value = ref[...].astype(f32)
        for start in range(0, ref.shape[0], 128):
            small[at] = value[start : start + 128].reshape(1, 128)
            at += 1


def stack_rows(vectors, others):
    count = sum(v.shape[0] for v in others) // 128
    return pl.pallas_call(
        functools.partial(stack_kernel, len(vectors)),
        out_shape=(
            jax.ShapeDtypeStruct((8, vectors[0].shape[0]), f32),
            jax.ShapeDtypeStruct((count, 1, 128), f32),
        ),
        cost_estimate=cost(1),
        name="stack_rows",
    )(*vectors, *others)


def pack_kernel(core, source, out):
    out[...] = source[...]


def pack_half(core, weight, axis):
    out = tuple(n // 2 if i == axis else n for i, n in enumerate(weight.shape))
    return pl.pallas_call(
        pack_kernel,
        grid_spec=pltpu.PrefetchScalarGridSpec(
            num_scalar_prefetch=1,
            grid=(1,),
            in_specs=[pl.BlockSpec(out, lambda i, s: (s[0], 0) if axis == 0 else (0, s[0]))],
            out_specs=whole(out),
        ),
        out_shape=jax.ShapeDtypeStruct(out, weight.dtype),
        compiler_params=params(16),
        cost_estimate=cost(2),
        name="pack_half",
    )(core, weight)


def pack_two_kernel(places, up_0, up_1, down_0, down_1, *outs):
    for t, (up, down) in enumerate(((up_0, down_0), (up_1, down_1))):
        outs[2 * t][...] = up[...].astype(f32).T.astype(bf16)
        outs[2 * t + 1][...] = down[...]


def pack_second(core, w_up, w_down):
    width = w_up.shape[0]
    return pl.pallas_call(
        pack_two_kernel,
        grid_spec=pltpu.PrefetchScalarGridSpec(
            num_scalar_prefetch=1,
            grid=(1,),
            in_specs=[pl.BlockSpec((width, PIECE), lambda i, s, t=t: (0, 2 * s[0] + t)) for t in range(2)]
            + [pl.BlockSpec((PIECE, width), lambda i, s, t=t: (2 * s[0] + t, 0)) for t in range(2)],
            out_specs=[whole((PIECE, width))] * 4,
        ),
        out_shape=(jax.ShapeDtypeStruct((PIECE, width), bf16),) * 4,
        compiler_params=params(32),
        cost_estimate=cost(5),
        name="pack_second",
    )(core, w_up, w_up, w_down, w_down)


def group_order():
    at = lax.broadcasted_iota(jnp.int32, (384, 384), 1)
    source = (at % 128) // 32 * 96 + at // 128 * 32 + at % 32
    return (lax.broadcasted_iota(jnp.int32, (384, 384), 0) == source).astype(f32).astype(bf16)


def place_mlp_kernel(places, *refs):
    step = pl.program_id(0)
    grad_down, grad_up = refs[-2:]
    for i in range(4):
        for x in range(2):

            @pl.when((step == i) & (places[4] == x))
            def _(down=refs[2 * i + x], up=refs[2 * i + 1 - x]):
                grad_down[...] = down[...].astype(f32)
                grad_up[...] = up[...].astype(f32).T


def place_mlp(places, pieces, down_shape, up_shape):
    size = pieces[0].shape[0]
    return pl.pallas_call(
        place_mlp_kernel,
        grid_spec=pltpu.PrefetchScalarGridSpec(
            num_scalar_prefetch=1,
            grid=(4,),
            in_specs=[whole(p.shape) for p in pieces],
            out_specs=[
                pl.BlockSpec((size, down_shape[1]), lambda i, s: (s[i], 0)),
                pl.BlockSpec((up_shape[0], size), lambda i, s: (0, s[i])),
            ],
        ),
        out_shape=(jax.ShapeDtypeStruct(down_shape, f32), jax.ShapeDtypeStruct(up_shape, f32)),
        compiler_params=params(),
        cost_estimate=cost(8),
        name="place_mlp",
    )(places, *pieces)


def place_two_kernel(places, *refs):
    step = pl.program_id(0)
    grad_qkv, grad_proj = refs[-2:]
    for i in range(4):

        @pl.when(step == i)
        def _(first=refs[2 * i], second=refs[2 * i + 1]):
            order = group_order()
            grad_qkv[:, 0:384] = dot(first[:, 0:384], order, NT)
            grad_qkv[:, 384:768] = dot(first[:, 384:768], order, NT)
            grad_qkv[:, 768:1152] = dot(second[...], order, NT)
            grad_proj[...] = first[:, 768:1152].astype(f32)


def place_two(places, firsts, seconds, qkv_shape, proj_shape):
    pieces = [p for pair in zip(firsts, seconds) for p in pair]
    rows = firsts[0].shape[0]
    return pl.pallas_call(
        place_two_kernel,
        grid_spec=pltpu.PrefetchScalarGridSpec(
            num_scalar_prefetch=1,
            grid=(4,),
            in_specs=[whole(p.shape) for p in pieces],
            out_specs=[
                pl.BlockSpec((rows, qkv_shape[1]), lambda i, s: (s[i], 0)),
                pl.BlockSpec((rows, proj_shape[1] // 2), lambda i, s: (s[i] % 2, s[i] // 2)),
            ],
        ),
        out_shape=(jax.ShapeDtypeStruct(qkv_shape, f32), jax.ShapeDtypeStruct(proj_shape, f32)),
        compiler_params=params(),
        cost_estimate=cost(5),
        name="place_two",
    )(places, *pieces)


def pair_onehot(rel_index, table_rows):
    turned_index = jnp.pad(rel_index.T, ((0, KEYS - SLOTS), (0, PAD - SLOTS)), constant_values=-1)
    offsets = jnp.arange(table_rows, dtype=jnp.int32)
    return (turned_index[None] == offsets[:, None, None]).astype(bf16)


def position_rows(onehot, table):
    return dot(table, onehot.reshape(onehot.shape[0], KEYS * PAD), TN).reshape(table.shape[1], KEYS, PAD)


def table_grad(onehot, sums):
    rows = onehot.shape[0]
    heads = sums.shape[1] // PAD
    flat = jnp.transpose(sums.reshape(KEYS, heads, PAD), (0, 2, 1)).reshape(KEYS * PAD, heads)
    high = flat.astype(bf16)
    rest = (flat - high.astype(f32)).astype(bf16)
    low = (flat - high.astype(f32) - rest.astype(f32)).astype(bf16)
    both = dot(onehot.reshape(rows, KEYS * PAD), jnp.concatenate([high, rest, low], axis=1))
    return both[:, :heads] + both[:, heads : 2 * heads] + both[:, 2 * heads :]


def window_mask(labels):
    shaped = labels.reshape(-1, SLOTS)
    keys = jnp.pad(shaped, ((0, 0), (0, KEYS - SLOTS)), constant_values=-2)[:, :, None]
    queries = jnp.pad(shaped, ((0, 0), (0, PAD - SLOTS)), constant_values=-3)
    queries = jnp.concatenate([queries, queries], axis=1)[:, None, :]
    key_at = jnp.arange(KEYS)[None, :, None]
    query_at = (jnp.arange(128) % PAD)[None, None, :]
    allowed = (keys == queries) & ((keys >= 0) | (key_at == query_at))
    outside = (key_at >= SLOTS) | (query_at >= SLOTS)
    return (allowed | outside).astype(f32)


class Links:
    def __init__(self):
        at = lax.axis_index("dp")
        self.core = at % 2
        self.x = at // 2 % 2
        self.z = at // 4
        self.inner = (self.z == 1) | (self.z == 2)

    def y_swap(self, value):
        return lax.ppermute(value, "mp", [(0, 1), (1, 0)])

    def flip(self, value, bit):
        return lax.ppermute(value, "dp", [(i, i ^ bit) for i in range(16)])

    def core_swap(self, value):
        return self.flip(value, 1)

    def x_swap(self, value):
        return self.flip(value, 2)

    def z_pairs(self, value):
        return self.flip(value, 4)

    def z_move(self, value, pairs):
        return lax.ppermute(value, "dp", [(s * 4 + i, d * 4 + i) for s, d in pairs for i in range(4)])

    def z_sum(self, value):
        value = value + self.z_move(value, [(0, 1), (3, 2)])
        value = value + self.z_move(value, [(1, 2), (2, 1)])
        return jnp.where(self.inner, value, self.z_move(value, [(1, 0), (2, 3)]))

    def order(self):
        places = [2 * (self.core ^ (r >> 1)) + (self.x ^ (r & 1)) for r in range(4)]
        return jnp.stack(places).astype(jnp.int32)


def tie(value, *others):
    return lax.optimization_barrier((value, *others))[0]


class Sequence:
    def __init__(self):
        self.last = None

    def __call__(self, value):
        return value if self.last is None else tie(value, self.last)

    def mark(self, value):
        self.last = value
        return value


class Chain:
    def __init__(self, links, seq, rows, terms, halves=None):
        self.links, self.seq = links, seq
        half = rows // 2

        def at(place):
            cut = [lax.dynamic_slice(t, (start + place * half, 0), (half, t.shape[1])).astype(f32) for t, start in terms]
            if halves:
                cut.append(jnp.where(place == 0, halves[0], halves[1]).astype(f32))
            return sum(cut[1:], cut[0]).astype(bf16)

        terms = [(seq(terms[0][0]), terms[0][1]), *terms[1:]]
        send = seq.mark(at(1 - links.x))
        self.came = links.x_swap(send)
        self.value = at(links.x)
        self.step = 0

    def next(self):
        links, seq = self.links, self.seq
        pairs = ([(0, 1), (3, 2)], [(1, 2), (2, 1)], [(1, 0), (2, 3)])
        if self.step < 3:
            self.value = seq.mark(seq(self.value) + self.came)
            self.came = links.z_move(self.value, pairs[self.step])
        elif self.step == 3:
            self.value = seq.mark(jnp.where(links.inner, seq(self.value), self.came))
            self.came = links.x_swap(self.value)
            self.core = links.core_swap(self.value)
        else:
            self.beside = seq(self.came)
            self.pieces = [self.value, self.beside, self.core, links.core_swap(self.beside)]
        self.step += 1


class SmallChain:
    def __init__(self, links, seq, value, shared, mine):
        self.links, self.seq, self.value = links, seq, seq(value)
        self.shared, self.mine = shared, mine
        self.came = links.core_swap(self.value)
        self.step = 0

    def next(self):
        links = self.links
        if self.step < 4:
            self.value = self.seq.mark(self.seq(self.value) + self.came)
            pairs = ([], [(0, 1), (3, 2)], [(1, 2), (2, 1)], [(1, 0), (2, 3)])[self.step]
            self.came = links.z_move(self.value, pairs) if pairs else links.x_swap(self.value)
        elif self.step == 4:
            self.value = self.seq.mark(jnp.where(links.inner, self.seq(self.value), self.came))
            n = self.shared + self.mine
            self.came = links.y_swap(jnp.concatenate([self.value[: self.shared], self.value[n:]]))
            self.value = self.value[:n]
        else:
            self.value = self.value + self.came
        self.step += 1


def on_device(
    direct,
    tokens,
    image_ids,
    rel_index,
    gain_one,
    shift_one,
    w_qkv,
    bias_query,
    bias_value,
    bias_table,
    w_proj,
    bias_proj,
    gain_two,
    shift_two,
    w_up,
    bias_up,
    w_down,
    bias_down,
    cotangent,
):
    mp = lax.axis_index("mp")
    real_rows = tokens.shape[0]
    labels = lax.dynamic_slice(image_ids, (mp * real_rows,), (real_rows,))
    spare = -real_rows % 16
    tokens = jnp.pad(tokens, ((0, spare), (0, 0)))
    cotangent = jnp.pad(cotangent, ((0, spare), (0, 0)))
    width = tokens.shape[1]
    small_size = bias_query.shape[0] + bias_value.shape[0] + bias_up.shape[0]
    biases = [bias_query, bias_value, bias_up]
    onehot = pair_onehot(rel_index, bias_table.shape[0])
    mask = window_mask(labels)

    if direct:
        links = Links()
        core, x = links.core, links.x
        half = width // 2
        core_at = core.astype(jnp.int32).reshape(1)
        first_own = pack_half(core_at, w_qkv, 0)
        first = links.y_swap(first_own)
        names = ("loc", "rem")
        inputs = dict(loc=[w_qkv], rem=None)
        small = dict(rem=None)
        tables = dict(loc=bias_table, rem=links.y_swap(bias_table))
        w_projs = dict(loc=w_proj)
        by_core = jnp.stack([2 * core, 2 * core + 1, 2 - 2 * core, 3 - 2 * core]).astype(jnp.int32)
        orders = dict(loc=core_at, rem=jnp.stack([core, 1 - core]).astype(jnp.int32))
        halves = [("loc", by_core, (w_up, w_down))] + [("rem", 2 * orders["rem"] + t, None) for t in range(2)]
        tokens_first = tie(tokens, first_own)
    else:
        names = ("all",)

        def whole_of(value, axis):
            return lax.all_gather(value, "mp", axis=axis, tiled=True)

        inputs = dict(all=[whole_of(w_qkv, 1)])
        up_all, down_all = whole_of(w_up, 1), whole_of(w_down, 0)
        biases = [whole_of(b, 0) for b in biases]
        small = {}
        tables = dict(all=whole_of(bias_table, 1))
        w_projs = dict(all=whole_of(w_proj, 0))
        core_at = jnp.zeros((1,), jnp.int32)
        orders = dict(all=core_at)
        halves = [("all", jnp.arange(down_all.shape[0] // PIECE, dtype=jnp.int32), (up_all, down_all))]

    rows8, small[names[0]] = stack_rows([gain_one, shift_one, bias_proj, gain_two, shift_two, bias_down], biases)
    if direct:
        small["rem"] = links.y_swap(small["loc"])
    small_pieces = sum(places.shape[0] for name, places, _ in halves if name == names[0]) * 3
    qkv, probs, att, w_in = {}, {}, {}, {}
    for name in names:
        positions = position_rows(onehot, tables[name])
        if inputs[name] is None:
            proj_own = pack_half(core_at, tie(w_proj, qkv["loc"]), 1)
            sent = list(pack_second(core_at, tie(w_up, qkv["loc"]), w_down))
            first = tie(first, qkv["loc"], positions, proj_own, *sent)
            inputs[name] = [first, links.core_swap(first)]
            proj_far = links.y_swap(tie(proj_own, first))
            came = [links.y_swap(tie(sent[0], first))]
        got = attention_forward(
            orders[name], tokens_first if name == "loc" else tokens, rows8, small[name], positions, mask, inputs[name]
        )
        qkv[name], probs[name], att[name], w_in[name], normed = got[:5]
    pieces = []
    if direct:
        proj_far = tie(proj_far, qkv["rem"])
        pieces = [proj_far, links.core_swap(proj_far)]
    got = project(orders[names[-1]], [att[n] for n in names], [w_projs[n] for n in w_projs], pieces, tokens, rows8)
    middle, low_two = got[:2]
    if direct:
        w_projs["rem"] = got[2]
    own, other, up_bias_grad = [], [], []
    carried = None
    for i, (name, places, ws) in enumerate(halves):
        last = i == len(halves) - 1
        low_now = low_two
        base = small[name].shape[0] - small_pieces
        if direct and i == 0:
            fence = (low_two, came[0])
            came = [tie(came[0], *fence)]
            came += [links.y_swap(tie(piece, *fence)) for piece in sent[1:3]]
            swapped = [links.core_swap(came[0])]
            low_now = tie(low_two, *fence)
        if direct and i == 1:
            fence = (own[0], came[1], came[2], swapped[0])
            came[1:3] = [tie(piece, *fence) for piece in came[1:3]]
            came.append(links.y_swap(tie(sent[3], *fence)))
            swapped += [links.core_swap(piece) for piece in came[1:3]]
            ws = [came[0], came[1], swapped[0], swapped[1]]
            theirs_hidden = links.core_swap(tie(other[0], swapped[1]))
        if direct and i == 2:
            came[3] = tie(came[3], own[1], theirs_hidden)
            theirs_0 = links.core_swap(tie(other[1], came[3]))
            swapped.append(links.core_swap(came[3]))
            ws = [came[2], came[3], swapped[2], swapped[3]]
            far_0 = [own[1][r : r + PIECE] + theirs_0[r : r + PIECE] for r in (0, PIECE)]
            got_0 = [links.y_swap(far_0[0])]
            low_now = tie(low_two, *far_0)
        got = mlp(places, low_now, cotangent, small[name], base, rows8, ws, carried, middle if last else None)
        own.append(got[0])
        other.append(got[1])
        up_bias_grad.append(got[2])
        carried = got[3:5]
    block_out, grad_middle, branch, sums_two = got[3:7]

    def unit(name, group):
        return (w_projs[name], qkv[name], probs[name], group)

    if direct:
        seq = Sequence()
        seq.mark(tie(branch, got_0[0]))
        theirs_1 = links.core_swap(seq(other[2]))
        got_0.append(links.y_swap(seq(far_0[1])))
        rows = 2 * PIECE
        far_1 = seq.mark(seq(own[2]) + theirs_1)
        got_1 = links.y_swap(far_1)
        got = attention_backward(
            core_at,
            seq(branch),
            normed,
            [[unit(name, g) for g in range(2)] for name in ("rem", "loc")],
            [att["rem"], att["loc"]],
        )
        gqkv_a, bias_a, cols_a, theirs_a, rem_a, loc_a = got
        seq.mark(tie(gqkv_a, got_0[1], got_1))
        theirs_a = links.core_swap(seq(theirs_a))
        chain_0 = Chain(links, seq, rows, [(own[0], 0), (theirs_hidden, 0)], got_0)
        low, high = slice(0, half // 2), slice(half // 2, half)
        far_a = [seq.mark(seq(rem_a)[at] + theirs_a[0][at]) for at in (low, high)]
        got_a = [links.y_swap(far_a[0])]
        got = attention_backward(core_at, seq(branch), normed, [[unit(name, 2)] for name in ("rem", "loc")])
        gqkv_b, bias_b, cols_b, theirs_b, rem_b, loc_b = got
        seq.mark(tie(gqkv_b, chain_0.came, got_a[0]))
        theirs_b = links.core_swap(seq(theirs_b))
        got_a.append(links.y_swap(seq(far_a[1])))
        chain_0.next()
        chain_1 = Chain(links, seq, rows, [(own[0], rows), (theirs_hidden, rows), (got_1, 0)])
        far_b = seq.mark(seq(rem_b) + theirs_b[0])
        got_b = links.y_swap(far_b)
        theirs_a, theirs_b = theirs_a.reshape(-1, theirs_a.shape[2]), theirs_b.reshape(-1, theirs_b.shape[2])
        plan = ((0, 0, 1, 0, 768), (0, 768, 0, 0, 768), (1, 0, 1, 768, 384), (1, 384, 0, 768, 384))
        grad_tokens, sums_one = input_backward(
            plan, [gqkv_a, gqkv_b], [w_in["loc"], w_in["rem"]], tokens, grad_middle, seq(rows8)
        )
        seq.mark(tie(sums_one, got_a[1], chain_0.came, chain_1.came))
        bias_a, bias_b, cols_a, cols_b = [seq(v) for v in (bias_a, bias_b, cols_a, cols_b)]
        up_bias_grad = [seq(v) for v in up_bias_grad]
        chain_a = Chain(links, seq, half, [(loc_a, 0), (theirs_a, half)], got_a)
        chain_0.next()
        chain_1.next()
        seq.mark(tie(seq.last, got_b))
        chain_b = Chain(links, seq, half, [(loc_b, 0), (theirs_b, half), (got_b, 0)])

        def by_place(first, second):
            return jnp.where(core == 0, jnp.concatenate([first, second]), jnp.concatenate([second, first]))

        rem = [jnp.concatenate([up_bias_grad[t][0, 0, at : at + PIECE] for t in (1, 2)]) for at in (0, PIECE)]
        bias_up_parts = [by_place(*rem), by_place(up_bias_grad[0][0, 0], up_bias_grad[0][1, 0])]

        def of_part(at):
            sums = [bias_a[:, at * 512 : (at + 1) * 512], bias_b[:, at * 256 : (at + 1) * 256]]
            cols = [cols_a[:, at * 256 : (at + 1) * 256], cols_b[:, at * 128 : (at + 1) * 128]]
            table = table_grad(onehot, jnp.concatenate(sums, axis=1))
            return [jnp.concatenate(cols, axis=1).reshape(-1), bias_up_parts[at], table.reshape(-1)]

        values = [sums_two.reshape(-1), sums_one.reshape(-1), *of_part(1), *of_part(0)]
        small_chain = SmallChain(links, seq, jnp.concatenate(values), 6 * width, small_size + bias_table.size)
        waves = (
            (chain_b, chain_a, small_chain, chain_0, chain_1),
            (chain_b, small_chain, chain_a, chain_0, chain_1),
            (chain_b, small_chain, chain_a, chain_1, chain_0),
            (chain_b, small_chain, chain_a, chain_1),
        )
        for wave in waves:
            for chain in wave:
                chain.next()
        small_chain.next()
        pieces_t = [chain_0.pieces, chain_1.pieces]
        pairs = [p for ends in (0, 2) for pieces in pieces_t for p in pieces[ends : ends + 2]]
        places = jnp.concatenate([by_core, x.astype(jnp.int32).reshape(1)])
        small_chain.next()
        grad_down, grad_up = place_mlp(places, pairs, w_down.shape, w_up.shape)
        seq.mark(grad_down)
        chain_b.next()
        chain_a.next()
        grad_qkv, grad_proj = place_two(links.order(), chain_a.pieces, chain_b.pieces, w_qkv.shape, w_proj.shape)
        got = small_chain.value
        two = got[: 4 * width].reshape(4, width)
        late = got[4 * width : 6 * width].reshape(2, width)
        got = got[6 * width :]
        cols = bias_query.shape[0]
        grad_query_b, grad_value_b = got[:cols], got[cols : 2 * cols]
        grad_up_bias = got[2 * cols : small_size]
        grad_table = got[small_size:].reshape(bias_table.shape)
    else:
        groups = tables["all"].shape[1] // GROUP
        got = attention_backward(core_at, branch, normed, [[unit("all", g) for g in range(groups)]])
        gqkv, bias_sums, col_sums, second_half, first_half = got
        grad_tokens, sums_one = input_backward(
            ((0, 0, 0, 0, gqkv.shape[1]),), [gqkv], [w_in["all"]], tokens, grad_middle, rows8
        )

        def summed(value, axis):
            value = lax.psum_scatter(value, "mp", scatter_dimension=axis, tiled=True)
            return lax.psum(value, "dp")

        hidden_grads = jnp.concatenate([own[0], other[0]]).reshape(-1, 2, PIECE, width)
        grad_down = summed(hidden_grads[:, 0].reshape(-1, width), 0).astype(f32)
        grad_up = summed(hidden_grads[:, 1].reshape(-1, width).T, 1).astype(f32)
        cols = gqkv.shape[1]
        grad_proj = summed(dot(att["all"], branch, TN).astype(bf16), 0).astype(f32)
        in_order = jnp.concatenate([first_half, second_half[0]], axis=0).reshape(-1, 384)
        natural = dot(in_order, group_order(), NT).reshape(width, cols).astype(bf16)
        grad_qkv = summed(natural, 1).astype(f32)
        grad_query_b = summed(col_sums[0], 0)
        grad_value_b = summed(col_sums[1], 0)
        grad_up_bias = summed(up_bias_grad[0].reshape(-1), 0)
        grad_table = summed(table_grad(onehot, bias_sums), 1)
        two, late = lax.psum((sums_two, sums_one), ("dp", "mp"))
    return (
        block_out[:real_rows],
        grad_tokens[:real_rows],
        late[0],
        late[1],
        grad_qkv,
        grad_query_b,
        grad_value_b,
        grad_table,
        grad_proj,
        two[2],
        two[0],
        two[1],
        grad_up,
        grad_up_bias,
        grad_down,
        two[3],
    )


def solution(mesh):
    direct = mesh.shape["dp"] == 16 and mesh.shape["mp"] == 2
    return jax.shard_map(
        functools.partial(on_device, direct),
        mesh=mesh,
        in_specs=(
            P(("dp", "mp"), None),
            P("dp"),
            P(),
            P(),
            P(),
            P(None, "mp"),
            P("mp"),
            P("mp"),
            P(None, "mp"),
            P("mp", None),
            P(),
            P(),
            P(),
            P(None, "mp"),
            P("mp"),
            P("mp", None),
            P(),
            P(("dp", "mp"), None),
        ),
        out_specs=(
            P(("dp", "mp"), None),
            P(("dp", "mp"), None),
            P(),
            P(),
            P(None, "mp"),
            P("mp"),
            P("mp"),
            P(None, "mp"),
            P("mp", None),
            P(),
            P(),
            P(),
            P(None, "mp"),
            P("mp"),
            P("mp", None),
            P(),
        ),
        check_vma=False,
    )
```

```python
import functools

import jax
import jax.numpy as jnp
from jax import lax
from jax.experimental import pallas as pl
from jax.experimental.pallas import tpu as pltpu
from jax.sharding import PartitionSpec as P

HEAD_DIM = 32
SLOTS = 49
PAD = 64
KEYS = 56
PIECE = 384
GROUP = 4
SPARE = 16
norm_eps = 1e-05
mask_fill = -1000000000.0
f32 = jnp.float32
bf16 = jnp.bfloat16
MIB = 1024 * 1024


def cost(micros):
    return pl.CostEstimate(flops=int(micros * 1.0e9), bytes_accessed=int(micros * 1.0e5), transcendentals=0)


def params(limit=56):
    return pltpu.CompilerParams(vmem_limit_bytes=limit * MIB)


def whole(shape):
    return pl.BlockSpec(shape, lambda *_: (0,) * len(shape))


def dot(left, right, dims=((1,), (0,))):
    return lax.dot_general(left, right, (dims, ((), ())), preferred_element_type=f32)


NT = ((1,), (1,))
TN = ((0,), (0,))


def norm_parts(values):
    mean = jnp.mean(values, axis=-1, keepdims=True)
    centred = values - mean
    spread = jnp.mean(centred * centred, axis=-1, keepdims=True)
    return centred, lax.rsqrt(spread + norm_eps)


def norm_back(values, gain, grad):
    centred, inverse = norm_parts(values)
    unit = centred * inverse
    scaled = grad * gain
    first = jnp.mean(scaled, axis=-1, keepdims=True)
    second = jnp.mean(scaled * unit, axis=-1, keepdims=True)
    return inverse * (scaled - first - unit * second), grad * unit


def col_sum(values):
    return jnp.sum(values, axis=0, keepdims=True)


def row_blocks(rows):
    size = 256 if rows % 16 == 0 else rows
    starts = list(range(0, rows, size))
    if len(starts) > 1 and rows - starts[-1] < 128:
        starts.pop()
    return [(s, (starts[i + 1] if i + 1 < len(starts) else rows) - s) for i, s in enumerate(starts)]


def diagonal(rows_of_heads):
    lane = lax.broadcasted_iota(jnp.int32, (PAD, 128), 1)
    out = rows_of_heads[3 * PAD :]
    for head in (2, 1, 0):
        out = jnp.where(lane < (head + 1) * HEAD_DIM, rows_of_heads[head * PAD : (head + 1) * PAD], out)
    return out


def spread(rows, block_mask):
    return jnp.concatenate([rows] * GROUP, axis=0) * block_mask


def block_mask_of():
    row = lax.broadcasted_iota(jnp.int32, (GROUP * PAD, 128), 0) // PAD
    lane = lax.broadcasted_iota(jnp.int32, (GROUP * PAD, 128), 1) // HEAD_DIM
    return (row == lane).astype(f32).astype(bf16)


def window_rows_mask(rows, cols):
    return lax.rem(lax.broadcasted_iota(jnp.int32, (rows, cols), 0), PAD) < SLOTS


def batch_of(windows):
    return 8 if windows % 8 == 0 else windows


def step_rows(ref, step, batch):
    if batch % 8:
        return ref
    return ref.at[pl.ds(pl.multiple_of(step * batch * SLOTS, 8), batch * SLOTS + SPARE)]


def pad_windows(src, dst, step, batch):
    view = step_rows(src, step, batch)
    for j in range(batch):
        dst[j * PAD : (j + 1) * PAD, :] = view[j * SLOTS : j * SLOTS + PAD, :].astype(bf16)


def fwd_kernel(groups, pieces, places, tokens, rows8, small, pos, mask, *refs):
    ws, refs = refs[: max(pieces, 1)], refs[max(pieces, 1) :]
    qkv, probs, att, wp, padded = refs[:5]
    normed, att_s, pos_s = refs[-3:]
    step = pl.program_id(0)
    rows = tokens.shape[0]

    @pl.when(step == 0)
    def _():
        centred, inverse = norm_parts(tokens[...].astype(f32))
        value = (centred * inverse * rows8[0:1, :] + rows8[1:2, :]).astype(bf16)
        normed[0:rows, :] = value.astype(f32)
        normed[rows:, :] = jnp.zeros_like(normed[rows:, :])
        order = group_order()
        for r, w in enumerate(ws):
            if pieces:
                size = w.shape[0]
                at = pl.ds(pl.multiple_of(places[r] * size, 16), size)
            else:
                at = slice(0, w.shape[0])
            for g in range(groups):
                cols = slice(g * 384, (g + 1) * 384)
                wp[at, cols] = dot(w[:, cols], order).astype(bf16)
        slot = lax.broadcasted_iota(jnp.int32, (KEYS, 128), 0) < SLOTS
        for h in range(0, groups * GROUP, 2):
            both = jnp.concatenate([pos[h], pos[h + 1]], axis=1)
            pos_s[:, h * PAD : (h + 2) * PAD] = jnp.where(slot, both, 2 * mask_fill)

    batch = mask.shape[0]
    pad_windows(normed, padded, step, batch)
    att_view = step_rows(att_s, step, batch)
    block_mask = block_mask_of()
    keep = window_rows_mask(batch * PAD, 128)
    left = padded[...]
    for g in range(groups):
        value = dot(left, wp[:, g * 384 : (g + 1) * 384])
        for part, bias in enumerate((small[g], None, small[groups + g])):
            piece = value[:, part * 128 : (part + 1) * 128]
            if bias is not None:
                piece = piece + bias
            qkv[:, g * 384 + part * 128 : g * 384 + (part + 1) * 128] = jnp.where(keep, piece, 0.0).astype(bf16)
    for j in range(batch):
        rows_at = slice(j * PAD, (j + 1) * PAD)
        allowed = mask[j] > 0.0
        allowed = jnp.concatenate([allowed, allowed], axis=1)
        for g in range(groups):
            at = g * 384
            query = qkv[rows_at, at : at + 128]
            key = qkv[rows_at, at + 128 : at + 256]
            value = qkv[rows_at, at + 256 : at + 384]
            raw = dot(key, spread(query, block_mask), NT)[:KEYS]
            scores = raw * HEAD_DIM ** (-0.5) + pos_s[:, g * 256 : (g + 1) * 256]
            scores = jnp.where(allowed, scores, mask_fill)
            top = jnp.max(scores, axis=0, keepdims=True)
            power = jnp.exp(scores - top)
            total = jnp.sum(power, axis=0, keepdims=True)
            prob = power * (1.0 / total)
            prob = jnp.concatenate([prob, jnp.zeros((PAD - KEYS, 256), f32)], axis=0).astype(bf16)
            probs[j, :, g * 256 : (g + 1) * 256] = prob
            out = diagonal(dot(prob, value, TN))
            att_view[j * SLOTS : j * SLOTS + KEYS, g * 128 : (g + 1) * 128] = out[:KEYS]

    @pl.when(step == pl.num_programs(0) - 1)
    def _():
        windows = pl.num_programs(0) * batch
        value = att_s[0:rows, :]
        real = lax.broadcasted_iota(jnp.int32, value.shape, 0) < windows * SLOTS
        att[...] = jnp.where(real, value, 0.0).astype(bf16)


def attention_forward(places, tokens, rows8, small, pos, mask, ws):
    rows, width = tokens.shape
    windows = mask.shape[0]
    pieces = len(ws) if len(ws) > 1 else 0
    heads = pos.shape[0]
    groups = heads // GROUP
    cols = groups * 384
    batch = batch_of(windows)
    steps = windows // batch
    quad_rows = batch * PAD
    out_shape = [
        jax.ShapeDtypeStruct((windows * PAD, cols), bf16),
        jax.ShapeDtypeStruct((windows, PAD, heads * PAD), bf16),
        jax.ShapeDtypeStruct((rows, heads * HEAD_DIM), bf16),
        jax.ShapeDtypeStruct((width, cols), bf16),
        jax.ShapeDtypeStruct((windows * PAD, width), bf16),
    ]
    out_specs = [
        pl.BlockSpec((quad_rows, cols), lambda i, s: (i, 0)),
        pl.BlockSpec((batch, PAD, heads * PAD), lambda i, s: (i, 0, 0)),
        whole((rows, heads * HEAD_DIM)),
        whole((width, cols)),
        pl.BlockSpec((quad_rows, width), lambda i, s: (i, 0)),
    ]
    return pl.pallas_call(
        functools.partial(fwd_kernel, groups, pieces),
        grid_spec=pltpu.PrefetchScalarGridSpec(
            num_scalar_prefetch=1,
            grid=(steps,),
            in_specs=[
                whole((rows, width)),
                whole(rows8.shape),
                whole(small.shape),
                whole(pos.shape),
                pl.BlockSpec((batch, KEYS, 128), lambda i, s: (i, 0, 0)),
            ]
            + [whole(w.shape) for w in ws],
            out_specs=out_specs,
            scratch_shapes=[
                pltpu.VMEM((rows + SPARE, width), f32),
                pltpu.VMEM((rows + SPARE, heads * HEAD_DIM), f32),
                pltpu.VMEM((KEYS, heads * PAD), f32),
            ],
        ),
        out_shape=tuple(out_shape),
        compiler_params=params(),
        cost_estimate=cost(11 * groups / 3),
        name="attention_forward",
    )(places, tokens, rows8, small, pos, mask, *ws)


def proj_kernel(parts, pieces, places, *refs):
    atts, ws = refs[:parts], list(refs[parts : 2 * parts - (1 if pieces else 0)])
    refs = refs[parts + len(ws) :]
    tokens, rows8, middle, low = refs[pieces : pieces + 4]
    if pieces:
        joined = refs[pieces + 4]
        for r, piece in enumerate(refs[:pieces]):
            size = piece.shape[1]
            joined[:, pl.ds(pl.multiple_of(places[r] * size, 128), size)] = piece[...]
        ws.append(joined)
    for start, size in row_blocks(tokens.shape[0]):
        at = slice(start, start + size)
        value = tokens[at, :].astype(f32) + rows8[2:3, :]
        for a, w in zip(atts, ws):
            value = value + dot(a[at, :], w[...])
        middle[at, :] = value
        centred, inverse = norm_parts(value)
        low[at, :] = (centred * inverse * rows8[3:4, :] + rows8[4:5, :]).astype(bf16)


def project(places, atts, ws, pieces, tokens, rows8):
    rows, width = tokens.shape
    ins = [*atts, *ws, *pieces, tokens, rows8]
    out_shape = [jax.ShapeDtypeStruct((rows, width), f32), jax.ShapeDtypeStruct((rows, width), bf16)]
    if pieces:
        out_shape.append(jax.ShapeDtypeStruct((pieces[0].shape[0], width), bf16))
    return pl.pallas_call(
        functools.partial(proj_kernel, len(atts), len(pieces)),
        grid_spec=pltpu.PrefetchScalarGridSpec(
            num_scalar_prefetch=1,
            grid=(1,),
            in_specs=[whole(v.shape) for v in ins],
            out_specs=[whole(o.shape) for o in out_shape],
        ),
        out_shape=tuple(out_shape),
        compiler_params=params(),
        cost_estimate=cost(5),
        name="project",
    )(places, *ins)


def gelu_parts(x):
    z = jnp.abs(x) * 0.7071067811865476
    t = 1.0 / (1.0 + 0.3275911 * z)
    e = jnp.exp(-z * z)
    half = t * (0.127414796 + t * (-0.142248368 + t * (0.7107068705 + t * (-0.7265760135 + t * 0.5307027145)))) * e
    cdf = jnp.where(x >= 0.0, 1.0 - half, half)
    return cdf, e * 0.3989422804014327


def mlp_kernel(first, last, held_pieces, base, order, *refs):
    low, dy, small, rows8 = refs[:4]
    ws, refs = refs[4 : 8 if held_pieces else 6], refs[8 if held_pieces else 6 :]
    if not first:
        out_in, two_in = refs[:2]
        refs = refs[2:]
    if last:
        middle, own, other, gbias, block_out, grad_middle, branch, sums = refs[:8]
        acc_out, acc_two, hid_s, gp_s = refs[8:12]
        refs = refs[12:]
    else:
        own, other, gbias, acc_out, acc_two, hid_s, gp_s = refs[:7]
        refs = refs[7:]
    step = pl.program_id(0)
    rows = low.shape[0]
    if held_pieces:
        held, sems = refs
        copies = []
        for i, w in enumerate(ws):
            r, k = i // 2, i % 2
            copies.append(pltpu.make_async_copy(w, held.at[k, r * PIECE : (r + 1) * PIECE], sems.at[i]))
        for copy in copies:
            copy.start()
        for copy in copies:
            copy.wait()
        up, down = held.at[0], held.at[1]
        up_dims, back_dims = NT, ((1,), (0,))
    else:
        up, down = ws
        up_dims, back_dims = ((1,), (0,)), NT

    @pl.when(step == 0)
    def _():
        if first:
            acc_out[...] = jnp.zeros_like(acc_out)
            acc_two[...] = jnp.zeros_like(acc_two)
        else:
            acc_out[...] = out_in[...]
            acc_two[...] = two_in[...]

    bias = [small[base + 3 * order[2 * step + t // 3] + t % 3] for t in range(6)]
    bias = jnp.concatenate(bias, axis=1)
    total = jnp.zeros(bias.shape, f32)
    for start, size in row_blocks(rows):
        at = slice(start, start + size)
        pre = dot(low[at, :], up[...], up_dims) + bias
        back = dot(dy[at, :], down[...], NT)
        cdf, pdf = gelu_parts(pre)
        hid = (pre * cdf).astype(bf16)
        gp = (back * (cdf + pre * pdf)).astype(bf16)
        hid_s[at, :] = hid
        gp_s[at, :] = gp
        total = total + col_sum(gp.astype(f32))
        acc_out[at, :] += dot(hid, down[...])
        acc_two[at, :] += dot(gp, up[...], back_dims)
    gbias[0] = total
    grad_down = dot(hid_s[...], dy[...], TN).astype(bf16)
    grad_up = dot(gp_s[...], low[...], TN).astype(bf16)
    if held_pieces:
        for out, at in ((own, 0), (other, PIECE)):
            out[0:PIECE, :] = grad_down[at : at + PIECE]
            out[PIECE:, :] = grad_up[at : at + PIECE]
    else:
        for out, now in ((own, step < pl.num_programs(0) // 2), (other, step >= pl.num_programs(0) // 2)):

            @pl.when(now)
            def _(out=out):
                for t in range(2):
                    at, end = 2 * t * PIECE, (2 * t + 1) * PIECE
                    out[at:end, :] = grad_down[t * PIECE : (t + 1) * PIECE]
                    out[end : end + PIECE, :] = grad_up[t * PIECE : (t + 1) * PIECE]

    if last:

        @pl.when(step == pl.num_programs(0) - 1)
        def _():
            s_gain = s_shift = s_branch = s_down = jnp.zeros((1, low.shape[1]), f32)
            for start, size in row_blocks(rows):
                at = slice(start, start + size)
                mid = middle[at, :]
                block_out[at, :] = (mid + acc_out[at, :] + rows8[5:6, :]).astype(bf16)
                two = acc_two[at, :]
                up_grad = dy[at, :].astype(f32)
                grad, for_gain = norm_back(mid, rows8[3:4, :], two)
                grad = grad + up_grad
                grad_middle[at, :] = grad
                low_grad = grad.astype(bf16)
                branch[at, :] = low_grad
                s_gain += col_sum(for_gain)
                s_shift += col_sum(two)
                s_branch += col_sum(low_grad.astype(f32))
                s_down += col_sum(up_grad)
            sums[...] = jnp.concatenate([s_gain, s_shift, s_branch, s_down], axis=0)


def mlp(order, low, dy, small, base, rows8, ws, carried=None, middle=None):
    rows, width = low.shape
    held = isinstance(ws, list)
    units = 2 * PIECE if held else ws[1].shape[0]
    steps = units // (2 * PIECE)
    first, last = carried is None, middle is not None
    ins = [low, dy, small, rows8, *ws]
    specs = [whole((rows, width)), whole((rows, width)), whole(small.shape), whole(rows8.shape)]
    if held:
        specs += [pl.BlockSpec(memory_space=pl.ANY)] * 4
        grads = [jax.ShapeDtypeStruct((2 * PIECE, width), bf16)] * 2
        grad_specs = [whole((2 * PIECE, width))] * 2
    else:
        specs += [
            pl.BlockSpec((width, 2 * PIECE), lambda i, o: (0, o[2 * i] // 2)),
            pl.BlockSpec((2 * PIECE, width), lambda i, o: (o[2 * i] // 2, 0)),
        ]
        many = steps // 2
        grads = [jax.ShapeDtypeStruct((many * 4 * PIECE, width), bf16)] * 2
        grad_specs = [
            pl.BlockSpec((4 * PIECE, width), lambda i, o: (jnp.minimum(i, many - 1), 0)),
            pl.BlockSpec((4 * PIECE, width), lambda i, o: (jnp.maximum(i - many, 0), 0)),
        ]
    outs = [*grads, jax.ShapeDtypeStruct((steps, 1, 2 * PIECE), f32)]
    out_specs = [*grad_specs, pl.BlockSpec((1, 1, 2 * PIECE), lambda i, o: (i, 0, 0))]
    scratch = []
    if not first:
        ins += list(carried)
        specs += [whole((rows, width))] * 2
    if last:
        ins.append(middle)
        specs.append(whole((rows, width)))
        outs += [
            jax.ShapeDtypeStruct((rows, width), bf16),
            jax.ShapeDtypeStruct((rows, width), f32),
            jax.ShapeDtypeStruct((rows, width), bf16),
            jax.ShapeDtypeStruct((4, width), f32),
        ]
        out_specs += [whole((rows, width))] * 3 + [whole((4, width))]
        scratch = [pltpu.VMEM((rows, width), f32)] * 2
    else:
        outs += [jax.ShapeDtypeStruct((rows, width), f32)] * 2
        out_specs += [whole((rows, width))] * 2
    scratch += [pltpu.VMEM((rows, 2 * PIECE), bf16)] * 2
    if held:
        scratch += [pltpu.VMEM((2, 2 * PIECE, width), bf16), pltpu.SemaphoreType.DMA((4,))]
    return pl.pallas_call(
        functools.partial(mlp_kernel, first, last, held, base),
        grid_spec=pltpu.PrefetchScalarGridSpec(
            num_scalar_prefetch=1, grid=(steps,), in_specs=specs, out_specs=out_specs, scratch_shapes=scratch
        ),
        out_shape=tuple(outs),
        compiler_params=params(),
        cost_estimate=cost(11 * steps),
        name="mlp",
    )(order, *ins)


def bwd_kernel(parts, each, with_proj, core, branch, normed, *refs):
    units = parts * each
    atts, refs = refs[: parts * with_proj], refs[parts * with_proj :]
    wprojs, qkvs, probs = refs[:units], refs[units : 2 * units], refs[2 * units : 3 * units]
    gqkv, bias_sum, col_sums, theirs = refs[3 * units : 3 * units + 4]
    mine, (wide, padded, wcat, total) = refs[3 * units + 4 : -4], refs[-4:]
    step = pl.program_id(0)
    rows = branch.shape[0]
    half = normed.shape[1] // 2

    @pl.when(step == 0)
    def _():
        wide[0:rows, :] = branch[...].astype(f32)
        wide[rows:, :] = jnp.zeros_like(wide[rows:, :])
        bias_sum[...] = jnp.zeros_like(bias_sum)
        col_sums[...] = jnp.zeros_like(col_sums)
        for u in range(units):
            wcat[u * 128 : (u + 1) * 128, :] = wprojs[u][...]
        if with_proj:
            for out_at, place in ((mine, core[0]), (None, 1 - core[0])):
                right = branch[:, pl.ds(pl.multiple_of(place * half, 128), half)]
                for p in range(parts):
                    value = dot(atts[p][...], right, TN).astype(bf16)
                    if out_at is None:
                        theirs[p, :, each * 384 :] = value
                    else:
                        mine[p][:, each * 384 :] = value

    batch = probs[0].shape[0]
    pad_windows(wide, padded, step, batch)
    block_mask = block_mask_of()
    scale = HEAD_DIM ** (-0.5)
    grads = dot(padded[...], wcat[...], NT)
    grads = jnp.where(window_rows_mask(batch * PAD, grads.shape[1]), grads, 0.0).astype(bf16)
    for u in range(units):
        qkv, at = qkvs[u], u * 384
        bias_total = jnp.zeros((KEYS, 256), f32)
        col_total = [jnp.zeros((1, 128), f32)] * 2
        for j in range(batch):
            rows_at = slice(j * PAD, (j + 1) * PAD)
            query = qkv[rows_at, 0:128]
            key = qkv[rows_at, 128:256]
            value = qkv[rows_at, 256:384]
            prob_low = probs[u][j]
            grad = spread(grads[rows_at, u * 128 : (u + 1) * 128], block_mask)
            prob = prob_low.astype(f32)[:KEYS]
            prob_grad = dot(value, grad, NT)[:KEYS]
            both = prob * prob_grad
            score_grad = both - prob * jnp.sum(both, axis=0, keepdims=True)
            score_grad = jnp.concatenate([score_grad, jnp.zeros((PAD - KEYS, 256), f32)], axis=0).astype(bf16)
            bias_total = bias_total + score_grad.astype(f32)[:KEYS]
            grad_value = dot(prob_low, grad).astype(bf16)
            grad_key = (dot(score_grad, spread(query, block_mask)) * scale).astype(bf16)
            grad_query = (diagonal(dot(score_grad, key, TN)) * scale).astype(bf16)
            gqkv[rows_at, at : at + 128] = grad_query
            gqkv[rows_at, at + 128 : at + 256] = grad_key
            gqkv[rows_at, at + 256 : at + 384] = grad_value
            col_total[0] = col_total[0] + col_sum(grad_query.astype(f32))
            col_total[1] = col_total[1] + col_sum(grad_value.astype(f32))
        bias_sum[:, u * 256 : (u + 1) * 256] += bias_total
        col_sums[0:1, u * 128 : (u + 1) * 128] += col_total[0]
        col_sums[1:2, u * 128 : (u + 1) * 128] += col_total[1]
    grad = dot(normed[...], gqkv[...], TN)

    @pl.when(step == 0)
    def _():
        total[...] = grad

    @pl.when(step > 0)
    def _():
        total[...] += grad

    @pl.when(step == pl.num_programs(0) - 1)
    def _():
        for p in range(parts):
            cols = slice(p * each * 384, (p + 1) * each * 384)
            mine[p][:, 0 : each * 384] = total[pl.ds(pl.multiple_of(core[0] * half, 16), half), cols].astype(bf16)
            other = pl.ds(pl.multiple_of((1 - core[0]) * half, 16), half)
            theirs[p, :, 0 : each * 384] = total[other, cols].astype(bf16)


def attention_backward(core, branch, normed, parts, atts=()):
    rows, width = branch.shape
    units = [u for part in parts for u in part]
    windows = units[0][2].shape[0]
    count, each = len(units), len(parts[0])
    batch = batch_of(windows)
    quad_rows = batch * PAD
    half = (width // 2, each * 384 + (width // 2 if atts else 0))
    in_specs = [whole((rows, width)), pl.BlockSpec((quad_rows, width), lambda i, s: (i, 0))]
    in_specs += [whole(a.shape) for a in atts]
    in_specs += [pl.BlockSpec((128, width), lambda i, s, g=g: (g, 0)) for _, _, _, g in units]
    in_specs += [pl.BlockSpec((quad_rows, 384), lambda i, s, g=g: (i, g)) for _, _, _, g in units]
    in_specs += [pl.BlockSpec((batch, PAD, 256), lambda i, s, g=g: (i, 0, g)) for _, _, _, g in units]
    return pl.pallas_call(
        functools.partial(bwd_kernel, len(parts), each, 1 if atts else 0),
        grid_spec=pltpu.PrefetchScalarGridSpec(
            num_scalar_prefetch=1,
            grid=(windows // batch,),
            in_specs=in_specs,
            out_specs=[
                pl.BlockSpec((quad_rows, count * 384), lambda i, s: (i, 0)),
                whole((KEYS, count * 256)),
                whole((2, count * 128)),
                whole((len(parts), *half)),
            ]
            + [whole(half)] * len(parts),
            scratch_shapes=[
                pltpu.VMEM((rows + SPARE, width), f32),
                pltpu.VMEM((quad_rows, width), bf16),
                pltpu.VMEM((count * 128, width), bf16),
                pltpu.VMEM((width, count * 384), f32),
            ],
        ),
        out_shape=(
            jax.ShapeDtypeStruct((windows * PAD, count * 384), bf16),
            jax.ShapeDtypeStruct((KEYS, count * 256), f32),
            jax.ShapeDtypeStruct((2, count * 128), f32),
            jax.ShapeDtypeStruct((len(parts), *half), bf16),
        )
        + (jax.ShapeDtypeStruct(half, bf16),) * len(parts),
        compiler_params=params(),
        cost_estimate=cost(5 * count),
        name="attention_backward",
    )(core, branch, normed, *atts, *[u[0] for u in units], *[u[1] for u in units], *[u[2] for u in units])


def input_kernel(plan, arrays, *refs):
    gqkvs, refs = refs[:arrays], refs[arrays:]
    ws, refs = refs[: -6], refs[-6:]
    tokens, grad_middle, rows8, grad_tokens, sums, compact = refs
    step = pl.program_id(0)
    total = None
    for a, a_at, w, w_at, size in plan:
        term = dot(gqkvs[a][:, a_at : a_at + size], ws[w][:, w_at : w_at + size], NT)
        total = term if total is None else total + term
    batch = total.shape[0] // PAD
    view = step_rows(compact, step, batch)
    for j in range(batch):
        view[j * SLOTS : j * SLOTS + KEYS, :] = total[j * PAD : j * PAD + KEYS]

    @pl.when(step == pl.num_programs(0) - 1)
    def _():
        rows = tokens.shape[0]
        windows = pl.num_programs(0) * batch
        s_gain = s_shift = jnp.zeros((1, tokens.shape[1]), f32)
        for start, size in row_blocks(rows):
            at = slice(start, start + size)
            one = compact[at, :]
            if start + size == rows:
                real = start + lax.broadcasted_iota(jnp.int32, one.shape, 0) < windows * SLOTS
                one = jnp.where(real, one, 0.0)
            grad, for_gain = norm_back(tokens[at, :].astype(f32), rows8[0:1, :], one)
            grad_tokens[at, :] = (grad_middle[at, :] + grad).astype(bf16)
            s_gain += col_sum(for_gain)
            s_shift += col_sum(one)
        sums[...] = jnp.concatenate([s_gain, s_shift], axis=0)


def input_backward(plan, gqkvs, ws, tokens, grad_middle, rows8):
    rows, width = tokens.shape
    quad_rows = batch_of(gqkvs[0].shape[0] // PAD) * PAD
    steps = gqkvs[0].shape[0] // quad_rows
    return pl.pallas_call(
        functools.partial(input_kernel, plan, len(gqkvs)),
        grid=(steps,),
        in_specs=[pl.BlockSpec((quad_rows, a.shape[1]), lambda i: (i, 0)) for a in gqkvs]
        + [whole(w.shape) for w in ws]
        + [whole((rows, width)), whole((rows, width)), whole(rows8.shape)],
        out_specs=[whole((rows, width)), whole((2, width))],
        out_shape=(jax.ShapeDtypeStruct((rows, width), bf16), jax.ShapeDtypeStruct((2, width), f32)),
        scratch_shapes=[pltpu.VMEM((rows + SPARE, width), f32)],
        compiler_params=params(),
        cost_estimate=cost(11),
        name="input_backward",
    )(*gqkvs, *ws, tokens, grad_middle, rows8)


def stack_kernel(count, *refs):
    rows8, small = refs[-2:]
    rows8[...] = jnp.zeros_like(rows8)
    for i, ref in enumerate(refs[:count]):
        rows8[i : i + 1, :] = ref[...].astype(f32).reshape(1, -1)
    at = 0
    for ref in refs[count:-2]:
        value = ref[...].astype(f32)
        for start in range(0, ref.shape[0], 128):
            small[at] = value[start : start + 128].reshape(1, 128)
            at += 1


def stack_rows(vectors, others):
    count = sum(v.shape[0] for v in others) // 128
    return pl.pallas_call(
        functools.partial(stack_kernel, len(vectors)),
        out_shape=(
            jax.ShapeDtypeStruct((8, vectors[0].shape[0]), f32),
            jax.ShapeDtypeStruct((count, 1, 128), f32),
        ),
        cost_estimate=cost(1),
        name="stack_rows",
    )(*vectors, *others)


def pack_kernel(core, source, out):
    out[...] = source[...]


def pack_half(core, weight, axis):
    out = tuple(n // 2 if i == axis else n for i, n in enumerate(weight.shape))
    return pl.pallas_call(
        pack_kernel,
        grid_spec=pltpu.PrefetchScalarGridSpec(
            num_scalar_prefetch=1,
            grid=(1,),
            in_specs=[pl.BlockSpec(out, lambda i, s: (s[0], 0) if axis == 0 else (0, s[0]))],
            out_specs=whole(out),
        ),
        out_shape=jax.ShapeDtypeStruct(out, weight.dtype),
        compiler_params=params(16),
        cost_estimate=cost(2),
        name="pack_half",
    )(core, weight)


def pack_piece_kernel(place, up, down, up_out, down_out):
    up_out[...] = up[...].astype(f32).T.astype(bf16)
    down_out[...] = down[...]


def pack_piece(place, w_up, w_down):
    width = w_up.shape[0]
    return pl.pallas_call(
        pack_piece_kernel,
        grid_spec=pltpu.PrefetchScalarGridSpec(
            num_scalar_prefetch=1,
            grid=(1,),
            in_specs=[
                pl.BlockSpec((width, PIECE), lambda i, s: (0, s[0])),
                pl.BlockSpec((PIECE, width), lambda i, s: (s[0], 0)),
            ],
            out_specs=[whole((PIECE, width))] * 2,
        ),
        out_shape=(jax.ShapeDtypeStruct((PIECE, width), bf16),) * 2,
        compiler_params=params(32),
        cost_estimate=cost(3),
        name="pack_piece",
    )(place, w_up, w_down)


def group_order():
    at = lax.broadcasted_iota(jnp.int32, (384, 384), 1)
    source = (at % 128) // 32 * 96 + at // 128 * 32 + at % 32
    return (lax.broadcasted_iota(jnp.int32, (384, 384), 0) == source).astype(f32).astype(bf16)


def place_mlp_kernel(places, *refs):
    step = pl.program_id(0)
    grad_down, grad_up = refs[-2:]
    for i in range(4):

        @pl.when(step == i)
        def _(down=refs[2 * i], up=refs[2 * i + 1]):
            grad_down[...] = down[...].astype(f32)
            grad_up[...] = up[...].astype(f32).T


def place_mlp(places, pieces, down_shape, up_shape):
    size = pieces[0].shape[0]
    return pl.pallas_call(
        place_mlp_kernel,
        grid_spec=pltpu.PrefetchScalarGridSpec(
            num_scalar_prefetch=1,
            grid=(4,),
            in_specs=[whole(p.shape) for p in pieces],
            out_specs=[
                pl.BlockSpec((size, down_shape[1]), lambda i, s: (s[i], 0)),
                pl.BlockSpec((up_shape[0], size), lambda i, s: (0, s[i])),
            ],
        ),
        out_shape=(jax.ShapeDtypeStruct(down_shape, f32), jax.ShapeDtypeStruct(up_shape, f32)),
        compiler_params=params(),
        cost_estimate=cost(8),
        name="place_mlp",
    )(places, *pieces)


def place_two_kernel(places, *refs):
    step = pl.program_id(0)
    grad_qkv, grad_proj = refs[-2:]
    for i in range(4):

        @pl.when(step == i)
        def _(first=refs[2 * i], second=refs[2 * i + 1]):
            order = group_order()
            grad_qkv[:, 0:384] = dot(first[:, 0:384], order, NT)
            grad_qkv[:, 384:768] = dot(first[:, 384:768], order, NT)
            grad_qkv[:, 768:1152] = dot(second[...], order, NT)
            grad_proj[...] = first[:, 768:1152].astype(f32)


def place_two(places, firsts, seconds, qkv_shape, proj_shape):
    pieces = [p for pair in zip(firsts, seconds) for p in pair]
    rows = firsts[0].shape[0]
    return pl.pallas_call(
        place_two_kernel,
        grid_spec=pltpu.PrefetchScalarGridSpec(
            num_scalar_prefetch=1,
            grid=(4,),
            in_specs=[whole(p.shape) for p in pieces],
            out_specs=[
                pl.BlockSpec((rows, qkv_shape[1]), lambda i, s: (s[i], 0)),
                pl.BlockSpec((rows, proj_shape[1] // 2), lambda i, s: (s[i] % 2, s[i] // 2)),
            ],
        ),
        out_shape=(jax.ShapeDtypeStruct(qkv_shape, f32), jax.ShapeDtypeStruct(proj_shape, f32)),
        compiler_params=params(),
        cost_estimate=cost(5),
        name="place_two",
    )(places, *pieces)


def pair_onehot(rel_index, table_rows):
    turned_index = jnp.pad(rel_index.T, ((0, KEYS - SLOTS), (0, PAD - SLOTS)), constant_values=-1)
    offsets = jnp.arange(table_rows, dtype=jnp.int32)
    return (turned_index[None] == offsets[:, None, None]).astype(bf16)


def position_rows(onehot, table):
    return dot(table, onehot.reshape(onehot.shape[0], KEYS * PAD), TN).reshape(table.shape[1], KEYS, PAD)


def table_grad(onehot, sums):
    rows = onehot.shape[0]
    heads = sums.shape[1] // PAD
    flat = jnp.transpose(sums.reshape(KEYS, heads, PAD), (0, 2, 1)).reshape(KEYS * PAD, heads)
    high = flat.astype(bf16)
    rest = (flat - high.astype(f32)).astype(bf16)
    low = (flat - high.astype(f32) - rest.astype(f32)).astype(bf16)
    both = dot(onehot.reshape(rows, KEYS * PAD), jnp.concatenate([high, rest, low], axis=1))
    return both[:, :heads] + both[:, heads : 2 * heads] + both[:, 2 * heads :]


def window_mask(labels):
    shaped = labels.reshape(-1, SLOTS)
    keys = jnp.pad(shaped, ((0, 0), (0, KEYS - SLOTS)), constant_values=-2)[:, :, None]
    queries = jnp.pad(shaped, ((0, 0), (0, PAD - SLOTS)), constant_values=-3)
    queries = jnp.concatenate([queries, queries], axis=1)[:, None, :]
    key_at = jnp.arange(KEYS)[None, :, None]
    query_at = (jnp.arange(128) % PAD)[None, None, :]
    allowed = (keys == queries) & ((keys >= 0) | (key_at == query_at))
    outside = (key_at >= SLOTS) | (query_at >= SLOTS)
    return (allowed | outside).astype(f32)


class Links:
    def __init__(self):
        at = lax.axis_index("dp")
        self.core = at % 2
        self.x = at // 2 % 2
        self.z = at // 4
        self.inner = (self.z == 1) | (self.z == 2)

    def y_swap(self, value):
        return lax.ppermute(value, "mp", [(0, 1), (1, 0)])

    def flip(self, value, bit):
        return lax.ppermute(value, "dp", [(i, i ^ bit) for i in range(16)])

    def core_swap(self, value):
        return self.flip(value, 1)

    def x_swap(self, value):
        return self.flip(value, 2)

    def z_pairs(self, value):
        return self.flip(value, 4)

    def z_all(self, value):
        return [self.flip(value, 4), self.flip(value, 8), self.flip(value, 12)]

    def z_total(self, value, others):
        pair, far = value.astype(f32) + others[0].astype(f32), others[1].astype(f32) + others[2].astype(f32)
        return (pair + far).astype(value.dtype)

    def z_move(self, value, pairs):
        return lax.ppermute(value, "dp", [(s * 4 + i, d * 4 + i) for s, d in pairs for i in range(4)])

    def z_sum(self, value):
        value = value + self.z_move(value, [(0, 1), (3, 2)])
        value = value + self.z_move(value, [(1, 2), (2, 1)])
        return jnp.where(self.inner, value, self.z_move(value, [(1, 0), (2, 3)]))

    def order(self):
        places = [2 * (self.core ^ (r >> 1)) + (self.x ^ (r & 1)) for r in range(4)]
        return jnp.stack(places).astype(jnp.int32)


def tie(value, *others):
    return lax.optimization_barrier((value, *others))[0]


class Sequence:
    def __init__(self):
        self.last = None

    def __call__(self, value):
        return value if self.last is None else tie(value, self.last)

    def mark(self, value):
        self.last = value
        return value

    def fence(self, value, *others):
        return self.mark(tie(value, *others))


def cut_sum(place, rows, terms):
    cut = [lax.dynamic_slice(t, (start + place * rows, 0), (rows, t.shape[1])).astype(f32) for t, start in terms]
    return sum(cut[1:], cut[0]).astype(bf16)


class Chain:
    def __init__(self, links, seq, value, came=None):
        self.links, self.seq, self.value, self.came = links, seq, value, came
        self.step = 0
        if came is None:
            self.came = links.z_move(seq.mark(value), [(0, 1), (3, 2)])
            self.step = 1

    def next(self):
        links, seq = self.links, self.seq
        pairs = ([(0, 1), (3, 2)], [(1, 2), (2, 1)], [(1, 0), (2, 3)])
        if self.step < 3:
            self.value = seq.mark(seq(self.value) + self.came)
            self.came = links.z_move(self.value, pairs[self.step])
        elif self.step == 3:
            self.value = seq.mark(jnp.where(links.inner, seq(self.value), self.came))
            self.came = links.x_swap(self.value)
            self.core = links.core_swap(self.value)
        else:
            self.beside = seq.mark(seq(self.came))
            self.pieces = [self.value, self.beside, self.core, links.core_swap(self.beside)]
        self.step += 1


class SmallChain:
    def __init__(self, links, seq, value, shared, mine):
        self.links, self.seq, self.value = links, seq, seq(value)
        self.shared, self.mine = shared, mine
        self.came = links.core_swap(self.value)
        self.step = 0

    def next(self):
        links = self.links
        if self.step == 0:
            self.value = self.seq.mark(self.seq(self.value) + self.came)
            self.came = links.x_swap(self.value)
        elif self.step == 1:
            self.value = self.seq.mark(self.seq(self.value) + self.came)
            self.came = links.z_all(self.value)
        elif self.step == 2:
            self.value = self.seq.mark(links.z_total(self.seq(self.value), self.came))
            n = self.shared + self.mine
            self.came = links.y_swap(jnp.concatenate([self.value[: self.shared], self.value[n:]]))
            self.value = self.value[:n]
        else:
            self.value = self.seq.mark(self.seq(self.value) + self.came)
        self.step += 1


def on_device(
    direct,
    tokens,
    image_ids,
    rel_index,
    gain_one,
    shift_one,
    w_qkv,
    bias_query,
    bias_value,
    bias_table,
    w_proj,
    bias_proj,
    gain_two,
    shift_two,
    w_up,
    bias_up,
    w_down,
    bias_down,
    cotangent,
):
    mp = lax.axis_index("mp")
    real_rows = tokens.shape[0]
    labels = lax.dynamic_slice(image_ids, (mp * real_rows,), (real_rows,))
    spare = -real_rows % 16
    tokens = jnp.pad(tokens, ((0, spare), (0, 0)))
    cotangent = jnp.pad(cotangent, ((0, spare), (0, 0)))
    width = tokens.shape[1]
    small_size = bias_query.shape[0] + bias_value.shape[0] + bias_up.shape[0]
    biases = [bias_query, bias_value, bias_up]
    onehot = pair_onehot(rel_index, bias_table.shape[0])
    mask = window_mask(labels)

    if direct:
        links = Links()
        core, x = links.core, links.x
        half = width // 2
        core_at = core.astype(jnp.int32).reshape(1)
        first_own = pack_half(core_at, w_qkv, 0)
        first = links.y_swap(first_own)
        names = ("loc", "rem")
        inputs = dict(loc=[w_qkv], rem=None)
        small = dict(rem=None)
        tables = dict(loc=bias_table, rem=links.y_swap(bias_table))
        w_projs = dict(loc=w_proj)
        by_core_x = (2 * core + x).astype(jnp.int32).reshape(1)
        by_core = jnp.stack([2 * core, 2 * core + 1, 2 - 2 * core, 3 - 2 * core]).astype(jnp.int32)
        orders = dict(loc=core_at, rem=jnp.stack([core, 1 - core]).astype(jnp.int32))
        halves = [("loc", by_core, (w_up, w_down))] + [
            ("rem", 2 * orders["rem"] + t, None) for t in (x, 1 - x)
        ]
        halves = [halves[1], halves[0], halves[2]]
        tokens_first = tie(tokens, first_own)
    else:
        names = ("all",)

        def whole_of(value, axis):
            return lax.all_gather(value, "mp", axis=axis, tiled=True)

        inputs = dict(all=[whole_of(w_qkv, 1)])
        up_all, down_all = whole_of(w_up, 1), whole_of(w_down, 0)
        biases = [whole_of(b, 0) for b in biases]
        small = {}
        tables = dict(all=whole_of(bias_table, 1))
        w_projs = dict(all=whole_of(w_proj, 0))
        core_at = jnp.zeros((1,), jnp.int32)
        orders = dict(all=core_at)
        halves = [("all", jnp.arange(down_all.shape[0] // PIECE, dtype=jnp.int32), (up_all, down_all))]

    rows8, small[names[0]] = stack_rows([gain_one, shift_one, bias_proj, gain_two, shift_two, bias_down], biases)
    if direct:
        small["rem"] = links.y_swap(small["loc"])
    small_pieces = sum(places.shape[0] for name, places, _ in halves if name == names[0]) * 3
    qkv, probs, att, w_in = {}, {}, {}, {}
    for name in names:
        positions = position_rows(onehot, tables[name])
        if inputs[name] is None:
            first = tie(first, qkv["loc"], positions)
            inputs[name] = [first, links.core_swap(first)]
            proj_own = pack_half(core_at, tie(w_proj, first), 1)
            sent = list(pack_piece(by_core_x, tie(w_up, first), w_down))
            proj_far = links.y_swap(tie(proj_own, first))
            came = [links.y_swap(tie(sent[0], first))]
        got = attention_forward(
            orders[name], tokens_first if name == "loc" else tokens, rows8, small[name], positions, mask, inputs[name]
        )
        qkv[name], probs[name], att[name], w_in[name], normed = got[:5]
    pieces = []
    if direct:
        proj_far, came[0] = tie(proj_far, qkv["rem"], came[0]), tie(came[0], qkv["rem"], proj_far)
        pieces = [proj_far, links.core_swap(proj_far)]
        came.append(links.y_swap(tie(sent[1], came[0])))
    got = project(orders[names[-1]], [att[n] for n in names], [w_projs[n] for n in w_projs], pieces, tokens, rows8)
    middle, low_two = got[:2]
    if direct:
        w_projs["rem"] = got[2]
    own, other, up_bias_grad = [], [], []
    carried = None
    for i, (name, places, ws) in enumerate(halves):
        last = i == len(halves) - 1
        low_now = low_two
        base = small[name].shape[0] - small_pieces
        if direct and i == 0:
            came = [tie(piece, low_two, *came) for piece in came]
            beside = [links.x_swap(came[0])]
            ws = came + [links.core_swap(piece) for piece in came]
        if direct and i == 1:
            fence = (own[0], beside[0])
            theirs_f = links.core_swap(tie(other[0], *fence))
            beside.append(links.x_swap(tie(came[1], *fence)))
            swapped = [links.core_swap(tie(beside[0], *fence))]
            far_f = own[0] + theirs_f
            got_f = links.y_swap(far_f)
            low_now = tie(low_two, far_f)
        if direct and i == 2:
            fence = (own[1], beside[1], got_f, swapped[0])
            beside[1] = tie(beside[1], *fence)
            swapped.append(links.core_swap(beside[1]))
            theirs_hidden = links.core_swap(tie(other[1], beside[1]))
            ws = beside + swapped
        got = mlp(places, low_now, cotangent, small[name], base, rows8, ws, carried, middle if last else None)
        own.append(got[0])
        other.append(got[1])
        up_bias_grad.append(got[2])
        carried = got[3:5]
    block_out, grad_middle, branch, sums_two = got[3:7]

    def unit(name, group):
        return (w_projs[name], qkv[name], probs[name], group)

    if direct:
        seq = Sequence()
        branch = seq.fence(branch, theirs_hidden)
        rows = 2 * PIECE
        theirs_s = links.core_swap(seq(other[2]))
        send_f = seq.mark(cut_sum(x, rows, [(seq(own[1]), 0), (theirs_hidden, 0), (tie(got_f, branch), -x * rows)]))
        beside_f = links.x_swap(send_f)
        far_s = seq.mark(seq(own[2]) + theirs_s)
        got_s = links.y_swap(far_s)
        got = attention_backward(
            core_at,
            seq(branch),
            normed,
            [[unit(name, g) for g in range(2)] for name in ("rem", "loc")],
            [att["rem"], att["loc"]],
        )
        gqkv_a, bias_a, cols_a, theirs_a, rem_a, loc_a = got
        gqkv_a = seq.fence(gqkv_a, beside_f, got_s)
        theirs_a = links.core_swap(seq(theirs_a))

        def kept(at):
            start = (1 - x) * rows + at
            cut = [lax.dynamic_slice(t, (start, 0), (PIECE, width)) for t in (seq(own[1]), theirs_hidden)]
            cut = [t.astype(f32) for t in (*cut, got_s[at : at + PIECE], beside_f[at : at + PIECE])]
            return sum(cut[1:], cut[0]).astype(bf16)

        chain_0 = Chain(links, seq, kept(0))
        far_a = seq.mark(seq(rem_a) + theirs_a[0])
        got_a = links.y_swap(far_a)
        chain_1_value = seq.mark(kept(PIECE))
        got = attention_backward(core_at, seq(branch), normed, [[unit(name, 2)] for name in ("rem", "loc")])
        gqkv_b, bias_b, cols_b, theirs_b, rem_b, loc_b = got
        gqkv_b = seq.fence(gqkv_b, chain_0.came, got_a)
        theirs_b = links.core_swap(seq(theirs_b))
        chain_0.next()
        chain_1 = Chain(links, seq, seq(chain_1_value))
        theirs_a = theirs_a.reshape(-1, theirs_a.shape[2])
        def along_x(loc, theirs, got):
            quarter = half // 2
            terms = [(seq(loc), 0), (theirs, half), (got, 0)]
            send = seq.mark(cut_sum(1 - x, quarter, terms))
            return Chain(links, seq, cut_sum(x, quarter, terms), links.x_swap(send))

        chain_a = along_x(loc_a, theirs_a, got_a)
        far_b = seq.mark(seq(rem_b) + theirs_b[0])
        got_b = links.y_swap(far_b)
        theirs_b = theirs_b.reshape(-1, theirs_b.shape[2])
        plan = ((0, 0, 1, 0, 768), (0, 768, 0, 0, 768), (1, 0, 1, 768, 384), (1, 384, 0, 768, 384))
        grad_tokens, sums_one = input_backward(
            plan, [gqkv_a, gqkv_b], [w_in["loc"], w_in["rem"]], tokens, grad_middle, seq(rows8)
        )
        sums_one = seq.fence(sums_one, chain_0.came, chain_1.came, chain_a.came, got_b)
        chain_a.next()
        bias_a, bias_b, cols_a, cols_b = [seq(v) for v in (bias_a, bias_b, cols_a, cols_b)]
        up_bias_grad = [seq(v) for v in up_bias_grad]

        chain_0.next()
        chain_1.next()
        chain_b = along_x(loc_b, theirs_b, got_b)

        def by_place(first, second):
            return jnp.where(core == 0, jnp.concatenate([first, second]), jnp.concatenate([second, first]))

        by_t = [jnp.where(x == t, up_bias_grad[0], up_bias_grad[2]) for t in range(2)]
        rem = [jnp.concatenate([grad[0, 0, at : at + PIECE] for grad in by_t]) for at in (0, PIECE)]
        bias_up_parts = [by_place(*rem), by_place(up_bias_grad[1][0, 0], up_bias_grad[1][1, 0])]

        def of_part(at):
            sums = [bias_a[:, at * 512 : (at + 1) * 512], bias_b[:, at * 256 : (at + 1) * 256]]
            cols = [cols_a[:, at * 256 : (at + 1) * 256], cols_b[:, at * 128 : (at + 1) * 128]]
            table = table_grad(onehot, jnp.concatenate(sums, axis=1))
            return [jnp.concatenate(cols, axis=1).reshape(-1), bias_up_parts[at], table.reshape(-1)]

        values = [sums_two.reshape(-1), sums_one.reshape(-1), *of_part(1), *of_part(0)]
        small_chain = SmallChain(links, seq, jnp.concatenate(values), 6 * width, small_size + bias_table.size)
        waves = (
            (chain_a, chain_b, chain_0, chain_1, small_chain),
            (chain_a, chain_b, chain_1, chain_0, small_chain),
            (chain_a, chain_1, chain_b, small_chain),
        )
        for wave in waves:
            for chain in wave:
                chain.next()
        pairs = [p for pair in zip(chain_0.pieces, chain_1.pieces) for p in pair]
        places = jnp.stack([2 * c + t for c in (core, 1 - core) for t in (1 - x, x)]).astype(jnp.int32)
        grad_down, grad_up = place_mlp(tie(places, seq.last), pairs, w_down.shape, w_up.shape)
        grad_down = seq.mark(grad_down)
        for chain in (chain_b, chain_a, small_chain, chain_b):
            chain.next()
        grad_qkv, grad_proj = place_two(links.order(), chain_a.pieces, chain_b.pieces, w_qkv.shape, w_proj.shape)
        got = small_chain.value
        two = got[: 4 * width].reshape(4, width)
        late = got[4 * width : 6 * width].reshape(2, width)
        got = got[6 * width :]
        cols = bias_query.shape[0]
        grad_query_b, grad_value_b = got[:cols], got[cols : 2 * cols]
        grad_up_bias = got[2 * cols : small_size]
        grad_table = got[small_size:].reshape(bias_table.shape)
    else:
        groups = tables["all"].shape[1] // GROUP
        got = attention_backward(core_at, branch, normed, [[unit("all", g) for g in range(groups)]])
        gqkv, bias_sums, col_sums, second_half, first_half = got
        grad_tokens, sums_one = input_backward(
            ((0, 0, 0, 0, gqkv.shape[1]),), [gqkv], [w_in["all"]], tokens, grad_middle, rows8
        )

        def summed(value, axis):
            value = lax.psum_scatter(value, "mp", scatter_dimension=axis, tiled=True)
            return lax.psum(value, "dp")

        hidden_grads = jnp.concatenate([own[0], other[0]]).reshape(-1, 2, PIECE, width)
        grad_down = summed(hidden_grads[:, 0].reshape(-1, width), 0).astype(f32)
        grad_up = summed(hidden_grads[:, 1].reshape(-1, width).T, 1).astype(f32)
        cols = gqkv.shape[1]
        grad_proj = summed(dot(att["all"], branch, TN).astype(bf16), 0).astype(f32)
        in_order = jnp.concatenate([first_half, second_half[0]], axis=0).reshape(-1, 384)
        natural = dot(in_order, group_order(), NT).reshape(width, cols).astype(bf16)
        grad_qkv = summed(natural, 1).astype(f32)
        grad_query_b = summed(col_sums[0], 0)
        grad_value_b = summed(col_sums[1], 0)
        grad_up_bias = summed(up_bias_grad[0].reshape(-1), 0)
        grad_table = summed(table_grad(onehot, bias_sums), 1)
        two, late = lax.psum((sums_two, sums_one), ("dp", "mp"))
    return (
        block_out[:real_rows],
        grad_tokens[:real_rows],
        late[0],
        late[1],
        grad_qkv,
        grad_query_b,
        grad_value_b,
        grad_table,
        grad_proj,
        two[2],
        two[0],
        two[1],
        grad_up,
        grad_up_bias,
        grad_down,
        two[3],
    )


def solution(mesh):
    direct = mesh.shape["dp"] == 16 and mesh.shape["mp"] == 2
    return jax.shard_map(
        functools.partial(on_device, direct),
        mesh=mesh,
        in_specs=(
            P(("dp", "mp"), None),
            P("dp"),
            P(),
            P(),
            P(),
            P(None, "mp"),
            P("mp"),
            P("mp"),
            P(None, "mp"),
            P("mp", None),
            P(),
            P(),
            P(),
            P(None, "mp"),
            P("mp"),
            P("mp", None),
            P(),
            P(("dp", "mp"), None),
        ),
        out_specs=(
            P(("dp", "mp"), None),
            P(("dp", "mp"), None),
            P(),
            P(),
            P(None, "mp"),
            P("mp"),
            P("mp"),
            P(None, "mp"),
            P("mp", None),
            P(),
            P(),
            P(),
            P(None, "mp"),
            P("mp"),
            P("mp", None),
            P(),
        ),
        check_vma=False,
    )
```

```python
import functools

import jax
import jax.numpy as jnp
from jax import lax
from jax.experimental import pallas as pl
from jax.experimental.pallas import tpu as pltpu
from jax.sharding import PartitionSpec as P

HEAD_DIM = 32
SLOTS = 49
PAD = 64
KEYS = 56
PIECE = 384
GROUP = 4
SPARE = 16
norm_eps = 1e-05
mask_fill = -1000000000.0
f32 = jnp.float32
bf16 = jnp.bfloat16
MIB = 1024 * 1024


def cost(micros):
    return pl.CostEstimate(flops=int(micros * 1.0e9), bytes_accessed=int(micros * 1.0e5), transcendentals=0)


def params(limit=56):
    return pltpu.CompilerParams(vmem_limit_bytes=limit * MIB)


def whole(shape):
    return pl.BlockSpec(shape, lambda *_: (0,) * len(shape))


def dot(left, right, dims=((1,), (0,))):
    return lax.dot_general(left, right, (dims, ((), ())), preferred_element_type=f32)


NT = ((1,), (1,))
TN = ((0,), (0,))


def norm_parts(values):
    mean = jnp.mean(values, axis=-1, keepdims=True)
    centred = values - mean
    spread = jnp.mean(centred * centred, axis=-1, keepdims=True)
    return centred, lax.rsqrt(spread + norm_eps)


def norm_back(values, gain, grad):
    centred, inverse = norm_parts(values)
    unit = centred * inverse
    scaled = grad * gain
    first = jnp.mean(scaled, axis=-1, keepdims=True)
    second = jnp.mean(scaled * unit, axis=-1, keepdims=True)
    return inverse * (scaled - first - unit * second), grad * unit


def col_sum(values):
    return jnp.sum(values, axis=0, keepdims=True)


def row_blocks(rows):
    size = 256 if rows % 16 == 0 else rows
    starts = list(range(0, rows, size))
    if len(starts) > 1 and rows - starts[-1] < 128:
        starts.pop()
    return [(s, (starts[i + 1] if i + 1 < len(starts) else rows) - s) for i, s in enumerate(starts)]


def diagonal(rows_of_heads):
    lane = lax.broadcasted_iota(jnp.int32, (PAD, 128), 1)
    out = rows_of_heads[3 * PAD :]
    for head in (2, 1, 0):
        out = jnp.where(lane < (head + 1) * HEAD_DIM, rows_of_heads[head * PAD : (head + 1) * PAD], out)
    return out


def spread(rows, block_mask):
    return jnp.concatenate([rows] * GROUP, axis=0) * block_mask


def block_mask_of():
    row = lax.broadcasted_iota(jnp.int32, (GROUP * PAD, 128), 0) // PAD
    lane = lax.broadcasted_iota(jnp.int32, (GROUP * PAD, 128), 1) // HEAD_DIM
    return (row == lane).astype(f32).astype(bf16)


def window_rows_mask(rows, cols):
    return lax.rem(lax.broadcasted_iota(jnp.int32, (rows, cols), 0), PAD) < SLOTS


def batch_of(windows):
    return 8 if windows % 8 == 0 else windows


def step_rows(ref, step, batch):
    if batch % 8:
        return ref
    return ref.at[pl.ds(pl.multiple_of(step * batch * SLOTS, 8), batch * SLOTS + SPARE)]


def pad_windows(src, dst, step, batch):
    view = step_rows(src, step, batch)
    for j in range(batch):
        dst[j * PAD : (j + 1) * PAD, :] = view[j * SLOTS : j * SLOTS + PAD, :].astype(bf16)


def fwd_kernel(groups, pieces, places, tokens, rows8, small, pos, mask, *refs):
    ws, refs = refs[: max(pieces, 1)], refs[max(pieces, 1) :]
    qkv, probs, att, wp, padded = refs[:5]
    normed, att_s, pos_s = refs[-3:]
    step = pl.program_id(0)
    rows = tokens.shape[0]

    @pl.when(step == 0)
    def _():
        centred, inverse = norm_parts(tokens[...].astype(f32))
        value = (centred * inverse * rows8[0:1, :] + rows8[1:2, :]).astype(bf16)
        normed[0:rows, :] = value.astype(f32)
        normed[rows:, :] = jnp.zeros_like(normed[rows:, :])
        order = group_order()
        for r, w in enumerate(ws):
            if pieces:
                size = w.shape[0]
                at = pl.ds(pl.multiple_of(places[r] * size, 16), size)
            else:
                at = slice(0, w.shape[0])
            for g in range(groups):
                cols = slice(g * 384, (g + 1) * 384)
                wp[at, cols] = dot(w[:, cols], order).astype(bf16)
        slot = lax.broadcasted_iota(jnp.int32, (KEYS, 128), 0) < SLOTS
        for h in range(0, groups * GROUP, 2):
            both = jnp.concatenate([pos[h], pos[h + 1]], axis=1)
            pos_s[:, h * PAD : (h + 2) * PAD] = jnp.where(slot, both, 2 * mask_fill)

    batch = mask.shape[0]
    pad_windows(normed, padded, step, batch)
    att_view = step_rows(att_s, step, batch)
    block_mask = block_mask_of()
    keep = window_rows_mask(batch * PAD, 128)
    left = padded[...]
    for g in range(groups):
        value = dot(left, wp[:, g * 384 : (g + 1) * 384])
        for part, bias in enumerate((small[g], None, small[groups + g])):
            piece = value[:, part * 128 : (part + 1) * 128]
            if bias is not None:
                piece = piece + bias
            qkv[:, g * 384 + part * 128 : g * 384 + (part + 1) * 128] = jnp.where(keep, piece, 0.0).astype(bf16)
    for j in range(batch):
        rows_at = slice(j * PAD, (j + 1) * PAD)
        allowed = mask[j] > 0.0
        allowed = jnp.concatenate([allowed, allowed], axis=1)
        for g in range(groups):
            at = g * 384
            query = qkv[rows_at, at : at + 128]
            key = qkv[rows_at, at + 128 : at + 256]
            value = qkv[rows_at, at + 256 : at + 384]
            raw = dot(key, spread(query, block_mask), NT)[:KEYS]
            scores = raw * HEAD_DIM ** (-0.5) + pos_s[:, g * 256 : (g + 1) * 256]
            scores = jnp.where(allowed, scores, mask_fill)
            top = jnp.max(scores, axis=0, keepdims=True)
            power = jnp.exp(scores - top)
            total = jnp.sum(power, axis=0, keepdims=True)
            prob = power * (1.0 / total)
            prob = jnp.concatenate([prob, jnp.zeros((PAD - KEYS, 256), f32)], axis=0).astype(bf16)
            probs[j, :, g * 256 : (g + 1) * 256] = prob
            out = diagonal(dot(prob, value, TN))
            att_view[j * SLOTS : j * SLOTS + KEYS, g * 128 : (g + 1) * 128] = out[:KEYS]

    @pl.when(step == pl.num_programs(0) - 1)
    def _():
        windows = pl.num_programs(0) * batch
        value = att_s[0:rows, :]
        real = lax.broadcasted_iota(jnp.int32, value.shape, 0) < windows * SLOTS
        att[...] = jnp.where(real, value, 0.0).astype(bf16)


def attention_forward(places, tokens, rows8, small, pos, mask, ws):
    rows, width = tokens.shape
    windows = mask.shape[0]
    pieces = len(ws) if len(ws) > 1 else 0
    heads = pos.shape[0]
    groups = heads // GROUP
    cols = groups * 384
    batch = batch_of(windows)
    steps = windows // batch
    quad_rows = batch * PAD
    out_shape = [
        jax.ShapeDtypeStruct((windows * PAD, cols), bf16),
        jax.ShapeDtypeStruct((windows, PAD, heads * PAD), bf16),
        jax.ShapeDtypeStruct((rows, heads * HEAD_DIM), bf16),
        jax.ShapeDtypeStruct((width, cols), bf16),
        jax.ShapeDtypeStruct((windows * PAD, width), bf16),
    ]
    out_specs = [
        pl.BlockSpec((quad_rows, cols), lambda i, s: (i, 0)),
        pl.BlockSpec((batch, PAD, heads * PAD), lambda i, s: (i, 0, 0)),
        whole((rows, heads * HEAD_DIM)),
        whole((width, cols)),
        pl.BlockSpec((quad_rows, width), lambda i, s: (i, 0)),
    ]
    return pl.pallas_call(
        functools.partial(fwd_kernel, groups, pieces),
        grid_spec=pltpu.PrefetchScalarGridSpec(
            num_scalar_prefetch=1,
            grid=(steps,),
            in_specs=[
                whole((rows, width)),
                whole(rows8.shape),
                whole(small.shape),
                whole(pos.shape),
                pl.BlockSpec((batch, KEYS, 128), lambda i, s: (i, 0, 0)),
            ]
            + [whole(w.shape) for w in ws],
            out_specs=out_specs,
            scratch_shapes=[
                pltpu.VMEM((rows + SPARE, width), f32),
                pltpu.VMEM((rows + SPARE, heads * HEAD_DIM), f32),
                pltpu.VMEM((KEYS, heads * PAD), f32),
            ],
        ),
        out_shape=tuple(out_shape),
        compiler_params=params(),
        cost_estimate=cost(11 * groups / 3),
        name="attention_forward",
    )(places, tokens, rows8, small, pos, mask, *ws)


def proj_kernel(parts, pieces, places, *refs):
    atts, ws = refs[:parts], list(refs[parts : 2 * parts - (1 if pieces else 0)])
    refs = refs[parts + len(ws) :]
    tokens, rows8, middle, low = refs[pieces : pieces + 4]
    if pieces:
        joined = refs[pieces + 4]
        for r, piece in enumerate(refs[:pieces]):
            size = piece.shape[1]
            joined[:, pl.ds(pl.multiple_of(places[r] * size, 128), size)] = piece[...]
        ws.append(joined)
    for start, size in row_blocks(tokens.shape[0]):
        at = slice(start, start + size)
        value = tokens[at, :].astype(f32) + rows8[2:3, :]
        for a, w in zip(atts, ws):
            value = value + dot(a[at, :], w[...])
        middle[at, :] = value
        centred, inverse = norm_parts(value)
        low[at, :] = (centred * inverse * rows8[3:4, :] + rows8[4:5, :]).astype(bf16)


def project(places, atts, ws, pieces, tokens, rows8):
    rows, width = tokens.shape
    ins = [*atts, *ws, *pieces, tokens, rows8]
    out_shape = [jax.ShapeDtypeStruct((rows, width), f32), jax.ShapeDtypeStruct((rows, width), bf16)]
    if pieces:
        out_shape.append(jax.ShapeDtypeStruct((pieces[0].shape[0], width), bf16))
    return pl.pallas_call(
        functools.partial(proj_kernel, len(atts), len(pieces)),
        grid_spec=pltpu.PrefetchScalarGridSpec(
            num_scalar_prefetch=1,
            grid=(1,),
            in_specs=[whole(v.shape) for v in ins],
            out_specs=[whole(o.shape) for o in out_shape],
        ),
        out_shape=tuple(out_shape),
        compiler_params=params(),
        cost_estimate=cost(5),
        name="project",
    )(places, *ins)


def gelu_parts(x):
    z = jnp.abs(x) * 0.7071067811865476
    t = 1.0 / (1.0 + 0.3275911 * z)
    e = jnp.exp(-z * z)
    half = t * (0.127414796 + t * (-0.142248368 + t * (0.7107068705 + t * (-0.7265760135 + t * 0.5307027145)))) * e
    cdf = jnp.where(x >= 0.0, 1.0 - half, half)
    return cdf, e * 0.3989422804014327


def mlp_kernel(first, last, held_pieces, base, order, *refs):
    low, dy, small, rows8 = refs[:4]
    ws, refs = refs[4 : 8 if held_pieces else 6], refs[8 if held_pieces else 6 :]
    if not first:
        out_in, two_in = refs[:2]
        refs = refs[2:]
    if last:
        middle, own, other, gbias, block_out, grad_middle, branch, sums = refs[:8]
        acc_out, acc_two, hid_s, gp_s = refs[8:12]
        refs = refs[12:]
    else:
        own, other, gbias, acc_out, acc_two, hid_s, gp_s = refs[:7]
        refs = refs[7:]
    step = pl.program_id(0)
    rows = low.shape[0]
    copies, carry = [], []
    if not first:
        *refs, carry_sems = refs
        carry = [
            pltpu.make_async_copy(out_in, acc_out, carry_sems.at[0]),
            pltpu.make_async_copy(two_in, acc_two, carry_sems.at[1]),
        ]
    if held_pieces:
        held, sems = refs
        for i, w in enumerate(ws):
            r, k = i // 2, i % 2
            copies.append(pltpu.make_async_copy(w, held.at[k, r * PIECE : (r + 1) * PIECE], sems.at[i]))
        for copy in copies:
            copy.start()
        up, down = held.at[0], held.at[1]
        up_dims, back_dims = NT, ((1,), (0,))
    else:
        up, down = ws
        up_dims, back_dims = ((1,), (0,)), NT

    @pl.when(step == 0)
    def _():
        if first:
            acc_out[...] = jnp.zeros_like(acc_out)
            acc_two[...] = jnp.zeros_like(acc_two)
        for copy in carry:
            copy.start()

    for copy in copies[0::2]:
        copy.wait()
    bias = [small[base + 3 * order[2 * step + t // 3] + t % 3] for t in range(6)]
    bias = jnp.concatenate(bias, axis=1)
    total = jnp.zeros(bias.shape, f32)
    for start, size in row_blocks(rows):
        at = slice(start, start + size)
        pre = dot(low[at, :], up[...], up_dims) + bias
        if start == 0:
            for copy in copies[1::2]:
                copy.wait()
        back = dot(dy[at, :], down[...], NT)
        cdf, pdf = gelu_parts(pre)
        hid = (pre * cdf).astype(bf16)
        gp = (back * (cdf + pre * pdf)).astype(bf16)
        hid_s[at, :] = hid
        gp_s[at, :] = gp
        total = total + col_sum(gp.astype(f32))
        if start == 0:

            @pl.when(step == 0)
            def _():
                for copy in carry:
                    copy.wait()

        acc_out[at, :] += dot(hid, down[...])
        acc_two[at, :] += dot(gp, up[...], back_dims)
    gbias[0] = total

    def weight_rows(out, at, piece):
        cols = slice(piece * PIECE, (piece + 1) * PIECE)
        out[at : at + PIECE, :] = dot(hid_s[:, cols], dy[...], TN).astype(bf16)
        out[at + PIECE : at + 2 * PIECE, :] = dot(gp_s[:, cols], low[...], TN).astype(bf16)

    if held_pieces:
        weight_rows(own, 0, 0)
        weight_rows(other, 0, 1)
    else:
        for out, now in ((own, step < pl.num_programs(0) // 2), (other, step >= pl.num_programs(0) // 2)):

            @pl.when(now)
            def _(out=out):
                for t in range(2):
                    weight_rows(out, 2 * t * PIECE, t)

    if last:

        @pl.when(step == pl.num_programs(0) - 1)
        def _():
            s_gain = s_shift = s_branch = s_down = jnp.zeros((1, low.shape[1]), f32)
            for start, size in row_blocks(rows):
                at = slice(start, start + size)
                mid = middle[at, :]
                block_out[at, :] = (mid + acc_out[at, :] + rows8[5:6, :]).astype(bf16)
                two = acc_two[at, :]
                up_grad = dy[at, :].astype(f32)
                grad, for_gain = norm_back(mid, rows8[3:4, :], two)
                grad = grad + up_grad
                grad_middle[at, :] = grad
                low_grad = grad.astype(bf16)
                branch[at, :] = low_grad
                s_gain += col_sum(for_gain)
                s_shift += col_sum(two)
                s_branch += col_sum(low_grad.astype(f32))
                s_down += col_sum(up_grad)
            sums[...] = jnp.concatenate([s_gain, s_shift, s_branch, s_down], axis=0)


def mlp(order, low, dy, small, base, rows8, ws, carried=None, middle=None):
    rows, width = low.shape
    held = isinstance(ws, list)
    units = 2 * PIECE if held else ws[1].shape[0]
    steps = units // (2 * PIECE)
    first, last = carried is None, middle is not None
    ins = [low, dy, small, rows8, *ws]
    specs = [whole((rows, width)), whole((rows, width)), whole(small.shape), whole(rows8.shape)]
    if held:
        specs += [pl.BlockSpec(memory_space=pl.ANY)] * 4
        grads = [jax.ShapeDtypeStruct((2 * PIECE, width), bf16)] * 2
        grad_specs = [whole((2 * PIECE, width))] * 2
    else:
        specs += [
            pl.BlockSpec((width, 2 * PIECE), lambda i, o: (0, o[2 * i] // 2)),
            pl.BlockSpec((2 * PIECE, width), lambda i, o: (o[2 * i] // 2, 0)),
        ]
        many = steps // 2
        grads = [jax.ShapeDtypeStruct((many * 4 * PIECE, width), bf16)] * 2
        grad_specs = [
            pl.BlockSpec((4 * PIECE, width), lambda i, o: (jnp.minimum(i, many - 1), 0)),
            pl.BlockSpec((4 * PIECE, width), lambda i, o: (jnp.maximum(i - many, 0), 0)),
        ]
    outs = [*grads, jax.ShapeDtypeStruct((steps, 1, 2 * PIECE), f32)]
    out_specs = [*grad_specs, pl.BlockSpec((1, 1, 2 * PIECE), lambda i, o: (i, 0, 0))]
    scratch = []
    if not first:
        ins += list(carried)
        specs += [pl.BlockSpec(memory_space=pl.ANY)] * 2
    if last:
        ins.append(middle)
        specs.append(whole((rows, width)))
        outs += [
            jax.ShapeDtypeStruct((rows, width), bf16),
            jax.ShapeDtypeStruct((rows, width), f32),
            jax.ShapeDtypeStruct((rows, width), bf16),
            jax.ShapeDtypeStruct((4, width), f32),
        ]
        out_specs += [whole((rows, width))] * 3 + [whole((4, width))]
        scratch = [pltpu.VMEM((rows, width), f32)] * 2
    else:
        outs += [jax.ShapeDtypeStruct((rows, width), f32)] * 2
        out_specs += [whole((rows, width))] * 2
    scratch += [pltpu.VMEM((rows, 2 * PIECE), bf16)] * 2
    if held:
        scratch += [pltpu.VMEM((2, 2 * PIECE, width), bf16), pltpu.SemaphoreType.DMA((4,))]
    if not first:
        scratch.append(pltpu.SemaphoreType.DMA((2,)))
    return pl.pallas_call(
        functools.partial(mlp_kernel, first, last, held, base),
        grid_spec=pltpu.PrefetchScalarGridSpec(
            num_scalar_prefetch=1, grid=(steps,), in_specs=specs, out_specs=out_specs, scratch_shapes=scratch
        ),
        out_shape=tuple(outs),
        compiler_params=params(),
        cost_estimate=cost(11 * steps),
        name="mlp",
    )(order, *ins)


def bwd_kernel(parts, each, with_proj, core, branch, normed, *refs):
    units = parts * each
    atts, refs = refs[: parts * with_proj], refs[parts * with_proj :]
    wprojs, qkvs, probs = refs[:units], refs[units : 2 * units], refs[2 * units : 3 * units]
    gqkv, bias_sum, col_sums, theirs = refs[3 * units : 3 * units + 4]
    mine, (wide, padded, wcat, total) = refs[3 * units + 4 : -4], refs[-4:]
    step = pl.program_id(0)
    rows = branch.shape[0]
    half = normed.shape[1] // 2

    @pl.when(step == 0)
    def _():
        wide[0:rows, :] = branch[...].astype(f32)
        wide[rows:, :] = jnp.zeros_like(wide[rows:, :])
        bias_sum[...] = jnp.zeros_like(bias_sum)
        col_sums[...] = jnp.zeros_like(col_sums)
        for u in range(units):
            wcat[u * 128 : (u + 1) * 128, :] = wprojs[u][...]
        if with_proj:
            for out_at, place in ((mine, core[0]), (None, 1 - core[0])):
                right = branch[:, pl.ds(pl.multiple_of(place * half, 128), half)]
                for p in range(parts):
                    value = dot(atts[p][...], right, TN).astype(bf16)
                    if out_at is None:
                        theirs[p, :, each * 384 :] = value
                    else:
                        mine[p][:, each * 384 :] = value

    batch = probs[0].shape[0]
    pad_windows(wide, padded, step, batch)
    block_mask = block_mask_of()
    scale = HEAD_DIM ** (-0.5)
    grads = dot(padded[...], wcat[...], NT)
    grads = jnp.where(window_rows_mask(batch * PAD, grads.shape[1]), grads, 0.0).astype(bf16)
    for u in range(units):
        qkv, at = qkvs[u], u * 384
        bias_total = jnp.zeros((KEYS, 256), f32)
        col_total = [jnp.zeros((1, 128), f32)] * 2
        for j in range(batch):
            rows_at = slice(j * PAD, (j + 1) * PAD)
            query = qkv[rows_at, 0:128]
            key = qkv[rows_at, 128:256]
            value = qkv[rows_at, 256:384]
            prob_low = probs[u][j]
            grad = spread(grads[rows_at, u * 128 : (u + 1) * 128], block_mask)
            prob = prob_low.astype(f32)[:KEYS]
            prob_grad = dot(value, grad, NT)[:KEYS]
            both = prob * prob_grad
            score_grad = both - prob * jnp.sum(both, axis=0, keepdims=True)
            score_grad = jnp.concatenate([score_grad, jnp.zeros((PAD - KEYS, 256), f32)], axis=0).astype(bf16)
            bias_total = bias_total + score_grad.astype(f32)[:KEYS]
            grad_value = dot(prob_low, grad).astype(bf16)
            grad_key = (dot(score_grad, spread(query, block_mask)) * scale).astype(bf16)
            grad_query = (diagonal(dot(score_grad, key, TN)) * scale).astype(bf16)
            gqkv[rows_at, at : at + 128] = grad_query
            gqkv[rows_at, at + 128 : at + 256] = grad_key
            gqkv[rows_at, at + 256 : at + 384] = grad_value
            col_total[0] = col_total[0] + col_sum(grad_query.astype(f32))
            col_total[1] = col_total[1] + col_sum(grad_value.astype(f32))
        bias_sum[:, u * 256 : (u + 1) * 256] += bias_total
        col_sums[0:1, u * 128 : (u + 1) * 128] += col_total[0]
        col_sums[1:2, u * 128 : (u + 1) * 128] += col_total[1]
    grad = dot(normed[...], gqkv[...], TN)

    @pl.when(step == 0)
    def _():
        total[...] = grad

    @pl.when(step > 0)
    def _():
        total[...] += grad

    @pl.when(step == pl.num_programs(0) - 1)
    def _():
        for p in range(parts):
            cols = slice(p * each * 384, (p + 1) * each * 384)
            mine[p][:, 0 : each * 384] = total[pl.ds(pl.multiple_of(core[0] * half, 16), half), cols].astype(bf16)
            other = pl.ds(pl.multiple_of((1 - core[0]) * half, 16), half)
            theirs[p, :, 0 : each * 384] = total[other, cols].astype(bf16)


def attention_backward(core, branch, normed, parts, atts=()):
    rows, width = branch.shape
    units = [u for part in parts for u in part]
    windows = units[0][2].shape[0]
    count, each = len(units), len(parts[0])
    batch = batch_of(windows)
    quad_rows = batch * PAD
    half = (width // 2, each * 384 + (width // 2 if atts else 0))
    in_specs = [whole((rows, width)), pl.BlockSpec((quad_rows, width), lambda i, s: (i, 0))]
    in_specs += [whole(a.shape) for a in atts]
    in_specs += [pl.BlockSpec((128, width), lambda i, s, g=g: (g, 0)) for _, _, _, g in units]
    in_specs += [pl.BlockSpec((quad_rows, 384), lambda i, s, g=g: (i, g)) for _, _, _, g in units]
    in_specs += [pl.BlockSpec((batch, PAD, 256), lambda i, s, g=g: (i, 0, g)) for _, _, _, g in units]
    return pl.pallas_call(
        functools.partial(bwd_kernel, len(parts), each, 1 if atts else 0),
        grid_spec=pltpu.PrefetchScalarGridSpec(
            num_scalar_prefetch=1,
            grid=(windows // batch,),
            in_specs=in_specs,
            out_specs=[
                pl.BlockSpec((quad_rows, count * 384), lambda i, s: (i, 0)),
                whole((KEYS, count * 256)),
                whole((2, count * 128)),
                whole((len(parts), *half)),
            ]
            + [whole(half)] * len(parts),
            scratch_shapes=[
                pltpu.VMEM((rows + SPARE, width), f32),
                pltpu.VMEM((quad_rows, width), bf16),
                pltpu.VMEM((count * 128, width), bf16),
                pltpu.VMEM((width, count * 384), f32),
            ],
        ),
        out_shape=(
            jax.ShapeDtypeStruct((windows * PAD, count * 384), bf16),
            jax.ShapeDtypeStruct((KEYS, count * 256), f32),
            jax.ShapeDtypeStruct((2, count * 128), f32),
            jax.ShapeDtypeStruct((len(parts), *half), bf16),
        )
        + (jax.ShapeDtypeStruct(half, bf16),) * len(parts),
        compiler_params=params(),
        cost_estimate=cost(5 * count),
        name="attention_backward",
    )(core, branch, normed, *atts, *[u[0] for u in units], *[u[1] for u in units], *[u[2] for u in units])


def input_kernel(plan, arrays, *refs):
    gqkvs, refs = refs[:arrays], refs[arrays:]
    ws, refs = refs[: -6], refs[-6:]
    tokens, grad_middle, rows8, grad_tokens, sums, compact = refs
    step = pl.program_id(0)
    total = None
    for a, a_at, w, w_at, size in plan:
        term = dot(gqkvs[a][:, a_at : a_at + size], ws[w][:, w_at : w_at + size], NT)
        total = term if total is None else total + term
    batch = total.shape[0] // PAD
    view = step_rows(compact, step, batch)
    for j in range(batch):
        view[j * SLOTS : j * SLOTS + KEYS, :] = total[j * PAD : j * PAD + KEYS]

    @pl.when(step == pl.num_programs(0) - 1)
    def _():
        rows = tokens.shape[0]
        windows = pl.num_programs(0) * batch
        s_gain = s_shift = jnp.zeros((1, tokens.shape[1]), f32)
        for start, size in row_blocks(rows):
            at = slice(start, start + size)
            one = compact[at, :]
            if start + size == rows:
                real = start + lax.broadcasted_iota(jnp.int32, one.shape, 0) < windows * SLOTS
                one = jnp.where(real, one, 0.0)
            grad, for_gain = norm_back(tokens[at, :].astype(f32), rows8[0:1, :], one)
            grad_tokens[at, :] = (grad_middle[at, :] + grad).astype(bf16)
            s_gain += col_sum(for_gain)
            s_shift += col_sum(one)
        sums[...] = jnp.concatenate([s_gain, s_shift], axis=0)


def input_backward(plan, gqkvs, ws, tokens, grad_middle, rows8):
    rows, width = tokens.shape
    quad_rows = batch_of(gqkvs[0].shape[0] // PAD) * PAD
    steps = gqkvs[0].shape[0] // quad_rows
    return pl.pallas_call(
        functools.partial(input_kernel, plan, len(gqkvs)),
        grid=(steps,),
        in_specs=[pl.BlockSpec((quad_rows, a.shape[1]), lambda i: (i, 0)) for a in gqkvs]
        + [whole(w.shape) for w in ws]
        + [whole((rows, width)), whole((rows, width)), whole(rows8.shape)],
        out_specs=[whole((rows, width)), whole((2, width))],
        out_shape=(jax.ShapeDtypeStruct((rows, width), bf16), jax.ShapeDtypeStruct((2, width), f32)),
        scratch_shapes=[pltpu.VMEM((rows + SPARE, width), f32)],
        compiler_params=params(),
        cost_estimate=cost(11),
        name="input_backward",
    )(*gqkvs, *ws, tokens, grad_middle, rows8)


def stack_kernel(count, *refs):
    rows8, small = refs[-2:]
    rows8[...] = jnp.zeros_like(rows8)
    for i, ref in enumerate(refs[:count]):
        rows8[i : i + 1, :] = ref[...].astype(f32).reshape(1, -1)
    at = 0
    for ref in refs[count:-2]:
        value = ref[...].astype(f32)
        for start in range(0, ref.shape[0], 128):
            small[at] = value[start : start + 128].reshape(1, 128)
            at += 1


def stack_rows(vectors, others):
    count = sum(v.shape[0] for v in others) // 128
    return pl.pallas_call(
        functools.partial(stack_kernel, len(vectors)),
        out_shape=(
            jax.ShapeDtypeStruct((8, vectors[0].shape[0]), f32),
            jax.ShapeDtypeStruct((count, 1, 128), f32),
        ),
        cost_estimate=cost(1),
        name="stack_rows",
    )(*vectors, *others)


def pack_kernel(core, source, out):
    out[...] = source[...]


def pack_half(core, weight, axis):
    out = tuple(n // 2 if i == axis else n for i, n in enumerate(weight.shape))
    return pl.pallas_call(
        pack_kernel,
        grid_spec=pltpu.PrefetchScalarGridSpec(
            num_scalar_prefetch=1,
            grid=(1,),
            in_specs=[pl.BlockSpec(out, lambda i, s: (s[0], 0) if axis == 0 else (0, s[0]))],
            out_specs=whole(out),
        ),
        out_shape=jax.ShapeDtypeStruct(out, weight.dtype),
        compiler_params=params(16),
        cost_estimate=cost(2),
        name="pack_half",
    )(core, weight)


def pack_piece_kernel(place, up, down, up_out, down_out):
    up_out[...] = up[...].astype(f32).T.astype(bf16)
    down_out[...] = down[...]


def pack_piece(place, w_up, w_down):
    width = w_up.shape[0]
    return pl.pallas_call(
        pack_piece_kernel,
        grid_spec=pltpu.PrefetchScalarGridSpec(
            num_scalar_prefetch=1,
            grid=(1,),
            in_specs=[
                pl.BlockSpec((width, PIECE), lambda i, s: (0, s[0])),
                pl.BlockSpec((PIECE, width), lambda i, s: (s[0], 0)),
            ],
            out_specs=[whole((PIECE, width))] * 2,
        ),
        out_shape=(jax.ShapeDtypeStruct((PIECE, width), bf16),) * 2,
        compiler_params=params(32),
        cost_estimate=cost(3),
        name="pack_piece",
    )(place, w_up, w_down)


def group_order():
    at = lax.broadcasted_iota(jnp.int32, (384, 384), 1)
    source = (at % 128) // 32 * 96 + at // 128 * 32 + at % 32
    return (lax.broadcasted_iota(jnp.int32, (384, 384), 0) == source).astype(f32).astype(bf16)


def place_mlp_kernel(places, *refs):
    step = pl.program_id(0)
    grad_down, grad_up = refs[-2:]
    for i in range(4):

        @pl.when(step == i)
        def _(down=refs[2 * i], up=refs[2 * i + 1]):
            grad_down[...] = down[...].astype(f32)
            grad_up[...] = up[...].astype(f32).T


def place_mlp(places, pieces, down_shape, up_shape):
    size = pieces[0].shape[0]
    return pl.pallas_call(
        place_mlp_kernel,
        grid_spec=pltpu.PrefetchScalarGridSpec(
            num_scalar_prefetch=1,
            grid=(4,),
            in_specs=[whole(p.shape) for p in pieces],
            out_specs=[
                pl.BlockSpec((size, down_shape[1]), lambda i, s: (s[i], 0)),
                pl.BlockSpec((up_shape[0], size), lambda i, s: (0, s[i])),
            ],
        ),
        out_shape=(jax.ShapeDtypeStruct(down_shape, f32), jax.ShapeDtypeStruct(up_shape, f32)),
        compiler_params=params(),
        cost_estimate=cost(8),
        name="place_mlp",
    )(places, *pieces)


def place_two_kernel(places, *refs):
    step = pl.program_id(0)
    grad_qkv, grad_proj = refs[-2:]
    for i in range(4):

        @pl.when(step == i)
        def _(first=refs[2 * i], second=refs[2 * i + 1]):
            order = group_order()
            grad_qkv[:, 0:384] = dot(first[:, 0:384], order, NT)
            grad_qkv[:, 384:768] = dot(first[:, 384:768], order, NT)
            grad_qkv[:, 768:1152] = dot(second[...], order, NT)
            grad_proj[...] = first[:, 768:1152].astype(f32)


def place_two(places, firsts, seconds, qkv_shape, proj_shape):
    pieces = [p for pair in zip(firsts, seconds) for p in pair]
    rows = firsts[0].shape[0]
    return pl.pallas_call(
        place_two_kernel,
        grid_spec=pltpu.PrefetchScalarGridSpec(
            num_scalar_prefetch=1,
            grid=(4,),
            in_specs=[whole(p.shape) for p in pieces],
            out_specs=[
                pl.BlockSpec((rows, qkv_shape[1]), lambda i, s: (s[i], 0)),
                pl.BlockSpec((rows, proj_shape[1] // 2), lambda i, s: (s[i] % 2, s[i] // 2)),
            ],
        ),
        out_shape=(jax.ShapeDtypeStruct(qkv_shape, f32), jax.ShapeDtypeStruct(proj_shape, f32)),
        compiler_params=params(),
        cost_estimate=cost(5),
        name="place_two",
    )(places, *pieces)


def pair_onehot(rel_index, table_rows):
    turned_index = jnp.pad(rel_index.T, ((0, KEYS - SLOTS), (0, PAD - SLOTS)), constant_values=-1)
    offsets = jnp.arange(table_rows, dtype=jnp.int32)
    return (turned_index[None] == offsets[:, None, None]).astype(bf16)


def position_rows(onehot, table):
    return dot(table, onehot.reshape(onehot.shape[0], KEYS * PAD), TN).reshape(table.shape[1], KEYS, PAD)


def table_grad(onehot, sums):
    rows = onehot.shape[0]
    heads = sums.shape[1] // PAD
    flat = jnp.transpose(sums.reshape(KEYS, heads, PAD), (0, 2, 1)).reshape(KEYS * PAD, heads)
    high = flat.astype(bf16)
    rest = (flat - high.astype(f32)).astype(bf16)
    low = (flat - high.astype(f32) - rest.astype(f32)).astype(bf16)
    both = dot(onehot.reshape(rows, KEYS * PAD), jnp.concatenate([high, rest, low], axis=1))
    return both[:, :heads] + both[:, heads : 2 * heads] + both[:, 2 * heads :]


def window_mask(labels):
    shaped = labels.reshape(-1, SLOTS)
    keys = jnp.pad(shaped, ((0, 0), (0, KEYS - SLOTS)), constant_values=-2)[:, :, None]
    queries = jnp.pad(shaped, ((0, 0), (0, PAD - SLOTS)), constant_values=-3)
    queries = jnp.concatenate([queries, queries], axis=1)[:, None, :]
    key_at = jnp.arange(KEYS)[None, :, None]
    query_at = (jnp.arange(128) % PAD)[None, None, :]
    allowed = (keys == queries) & ((keys >= 0) | (key_at == query_at))
    outside = (key_at >= SLOTS) | (query_at >= SLOTS)
    return (allowed | outside).astype(f32)


class Links:
    def __init__(self):
        at = lax.axis_index("dp")
        self.core = at % 2
        self.x = at // 2 % 2
        self.z = at // 4
        self.inner = (self.z == 1) | (self.z == 2)

    def y_swap(self, value):
        return lax.ppermute(value, "mp", [(0, 1), (1, 0)])

    def flip(self, value, bit):
        return lax.ppermute(value, "dp", [(i, i ^ bit) for i in range(16)])

    def core_swap(self, value):
        return self.flip(value, 1)

    def x_swap(self, value):
        return self.flip(value, 2)

    def z_pairs(self, value):
        return self.flip(value, 4)

    def z_all(self, value):
        return [self.flip(value, 4), self.flip(value, 8), self.flip(value, 12)]

    def z_total(self, value, others):
        pair, far = value.astype(f32) + others[0].astype(f32), others[1].astype(f32) + others[2].astype(f32)
        return (pair + far).astype(value.dtype)

    def z_move(self, value, pairs):
        return lax.ppermute(value, "dp", [(s * 4 + i, d * 4 + i) for s, d in pairs for i in range(4)])

    def z_sum(self, value):
        value = value + self.z_move(value, [(0, 1), (3, 2)])
        value = value + self.z_move(value, [(1, 2), (2, 1)])
        return jnp.where(self.inner, value, self.z_move(value, [(1, 0), (2, 3)]))

    def order(self):
        places = [2 * (self.core ^ (r >> 1)) + (self.x ^ (r & 1)) for r in range(4)]
        return jnp.stack(places).astype(jnp.int32)


def tie(value, *others):
    return lax.optimization_barrier((value, *others))[0]


class Sequence:
    def __init__(self):
        self.last = None

    def __call__(self, value):
        return value if self.last is None else tie(value, self.last)

    def mark(self, value):
        self.last = value
        return value

    def fence(self, value, *others):
        return self.mark(tie(value, *others))


def cut_sum(place, rows, terms):
    cut = [lax.dynamic_slice(t, (start + place * rows, 0), (rows, t.shape[1])).astype(f32) for t, start in terms]
    return sum(cut[1:], cut[0]).astype(bf16)


class Chain:
    def __init__(self, links, seq, value, came=None):
        self.links, self.seq, self.value, self.came = links, seq, value, came
        self.step = 0
        if came is None:
            self.came = links.z_move(seq.mark(value), [(0, 1), (3, 2)])
            self.step = 1

    def next(self):
        links, seq = self.links, self.seq
        pairs = ([(0, 1), (3, 2)], [(1, 2), (2, 1)], [(1, 0), (2, 3)])
        if self.step < 3:
            self.value = seq.mark(seq(self.value) + self.came)
            self.came = links.z_move(self.value, pairs[self.step])
        elif self.step == 3:
            self.value = seq.mark(jnp.where(links.inner, seq(self.value), self.came))
            self.came = links.x_swap(self.value)
            self.core = links.core_swap(self.value)
        else:
            self.beside = seq.mark(seq(self.came))
            self.pieces = [self.value, self.beside, self.core, links.core_swap(self.beside)]
        self.step += 1


class SmallChain:
    def __init__(self, links, seq, value, shared, mine):
        self.links, self.seq, self.value = links, seq, seq(value)
        self.shared, self.mine = shared, mine
        self.came = links.core_swap(self.value)
        self.step = 0

    def next(self):
        links = self.links
        if self.step == 0:
            self.value = self.seq.mark(self.seq(self.value) + self.came)
            self.came = links.x_swap(self.value)
        elif self.step == 1:
            self.value = self.seq.mark(self.seq(self.value) + self.came)
            self.came = links.z_all(self.value)
        elif self.step == 2:
            self.value = self.seq.mark(links.z_total(self.seq(self.value), self.came))
            n = self.shared + self.mine
            self.came = links.y_swap(jnp.concatenate([self.value[: self.shared], self.value[n:]]))
            self.value = self.value[:n]
        else:
            self.value = self.seq.mark(self.seq(self.value) + self.came)
        self.step += 1


def on_device(
    direct,
    tokens,
    image_ids,
    rel_index,
    gain_one,
    shift_one,
    w_qkv,
    bias_query,
    bias_value,
    bias_table,
    w_proj,
    bias_proj,
    gain_two,
    shift_two,
    w_up,
    bias_up,
    w_down,
    bias_down,
    cotangent,
):
    mp = lax.axis_index("mp")
    real_rows = tokens.shape[0]
    labels = lax.dynamic_slice(image_ids, (mp * real_rows,), (real_rows,))
    spare = -real_rows % 16
    tokens = jnp.pad(tokens, ((0, spare), (0, 0)))
    cotangent = jnp.pad(cotangent, ((0, spare), (0, 0)))
    width = tokens.shape[1]
    small_size = bias_query.shape[0] + bias_value.shape[0] + bias_up.shape[0]
    biases = [bias_query, bias_value, bias_up]
    onehot = pair_onehot(rel_index, bias_table.shape[0])
    mask = window_mask(labels)

    if direct:
        links = Links()
        core, x = links.core, links.x
        half = width // 2
        core_at = core.astype(jnp.int32).reshape(1)
        first_own = pack_half(core_at, w_qkv, 0)
        first = links.y_swap(first_own)
        names = ("loc", "rem")
        inputs = dict(loc=[w_qkv], rem=None)
        small = dict(rem=None)
        tables = dict(loc=bias_table, rem=links.y_swap(bias_table))
        w_projs = dict(loc=w_proj)
        by_core_x = (2 * core + x).astype(jnp.int32).reshape(1)
        by_core = jnp.stack([2 * core, 2 * core + 1, 2 - 2 * core, 3 - 2 * core]).astype(jnp.int32)
        orders = dict(loc=core_at, rem=jnp.stack([core, 1 - core]).astype(jnp.int32))
        halves = [("loc", by_core, (w_up, w_down))] + [
            ("rem", 2 * orders["rem"] + t, None) for t in (x, 1 - x)
        ]
        halves = [halves[1], halves[0], halves[2]]
        tokens_first = tie(tokens, first_own)
    else:
        names = ("all",)

        def whole_of(value, axis):
            return lax.all_gather(value, "mp", axis=axis, tiled=True)

        inputs = dict(all=[whole_of(w_qkv, 1)])
        up_all, down_all = whole_of(w_up, 1), whole_of(w_down, 0)
        biases = [whole_of(b, 0) for b in biases]
        small = {}
        tables = dict(all=whole_of(bias_table, 1))
        w_projs = dict(all=whole_of(w_proj, 0))
        core_at = jnp.zeros((1,), jnp.int32)
        orders = dict(all=core_at)
        halves = [("all", jnp.arange(down_all.shape[0] // PIECE, dtype=jnp.int32), (up_all, down_all))]

    rows8, small[names[0]] = stack_rows([gain_one, shift_one, bias_proj, gain_two, shift_two, bias_down], biases)
    if direct:
        small["rem"] = links.y_swap(small["loc"])
    small_pieces = sum(places.shape[0] for name, places, _ in halves if name == names[0]) * 3
    qkv, probs, att, w_in = {}, {}, {}, {}
    for name in names:
        positions = position_rows(onehot, tables[name])
        if inputs[name] is None:
            first = tie(first, qkv["loc"], positions)
            inputs[name] = [first, links.core_swap(first)]
            proj_own = pack_half(core_at, tie(w_proj, first), 1)
            sent = list(pack_piece(by_core_x, tie(w_up, first), w_down))
            proj_far = links.y_swap(tie(proj_own, first))
            came = [links.y_swap(tie(sent[0], first))]
        got = attention_forward(
            orders[name], tokens_first if name == "loc" else tokens, rows8, small[name], positions, mask, inputs[name]
        )
        qkv[name], probs[name], att[name], w_in[name], normed = got[:5]
    pieces = []
    if direct:
        proj_far, came[0] = tie(proj_far, qkv["rem"], came[0]), tie(came[0], qkv["rem"], proj_far)
        pieces = [proj_far, links.core_swap(proj_far)]
        came.append(links.y_swap(tie(sent[1], came[0])))
    got = project(orders[names[-1]], [att[n] for n in names], [w_projs[n] for n in w_projs], pieces, tokens, rows8)
    middle, low_two = got[:2]
    if direct:
        w_projs["rem"] = got[2]
    own, other, up_bias_grad = [], [], []
    carried = None
    for i, (name, places, ws) in enumerate(halves):
        last = i == len(halves) - 1
        low_now = low_two
        base = small[name].shape[0] - small_pieces
        if direct and i == 0:
            came = [tie(piece, low_two, *came) for piece in came]
            beside = [links.x_swap(came[0])]
            ws = came + [links.core_swap(piece) for piece in came]
        if direct and i == 1:
            fence = (own[0], beside[0])
            theirs_f = links.core_swap(tie(other[0], *fence))
            beside.append(links.x_swap(tie(came[1], *fence)))
            swapped = [links.core_swap(tie(beside[0], *fence))]
            far_f = own[0] + theirs_f
            got_f = links.y_swap(far_f)
            low_now = tie(low_two, far_f)
        if direct and i == 2:
            fence = (own[1], beside[1], got_f, swapped[0])
            beside[1] = tie(beside[1], *fence)
            swapped.append(links.core_swap(beside[1]))
            theirs_hidden = links.core_swap(tie(other[1], swapped[1]))
            ws = beside + swapped
        got = mlp(places, low_now, cotangent, small[name], base, rows8, ws, carried, middle if last else None)
        own.append(got[0])
        other.append(got[1])
        up_bias_grad.append(got[2])
        carried = got[3:5]
    block_out, grad_middle, branch, sums_two = got[3:7]

    def unit(name, group):
        return (w_projs[name], qkv[name], probs[name], group)

    if direct:
        seq = Sequence()
        branch = seq.fence(branch, theirs_hidden)
        rows = 2 * PIECE
        theirs_s = links.core_swap(seq(other[2]))
        send_f = seq.mark(cut_sum(x, rows, [(seq(own[1]), 0), (theirs_hidden, 0), (tie(got_f, branch), -x * rows)]))
        beside_f = links.x_swap(send_f)
        far_s = seq.mark(seq(own[2]) + theirs_s)
        got_s = links.y_swap(far_s)
        got = attention_backward(
            core_at,
            seq(branch),
            normed,
            [[unit(name, g) for g in range(2)] for name in ("rem", "loc")],
            [att["rem"], att["loc"]],
        )
        gqkv_a, bias_a, cols_a, theirs_a, rem_a, loc_a = got
        gqkv_a = seq.fence(gqkv_a, beside_f, got_s)
        theirs_a = links.core_swap(seq(theirs_a))

        def kept(at):
            start = (1 - x) * rows + at
            cut = [lax.dynamic_slice(t, (start, 0), (PIECE, width)) for t in (seq(own[1]), theirs_hidden)]
            cut = [t.astype(f32) for t in (*cut, got_s[at : at + PIECE], beside_f[at : at + PIECE])]
            return sum(cut[1:], cut[0]).astype(bf16)

        chain_0_value = seq.mark(kept(0))
        far_a = seq.mark(seq(rem_a) + theirs_a[0])
        got_a = links.y_swap(far_a)
        chain_0 = Chain(links, seq, seq(chain_0_value))
        chain_1_value = seq.mark(kept(PIECE))
        got = attention_backward(core_at, seq(branch), normed, [[unit(name, 2)] for name in ("rem", "loc")])
        gqkv_b, bias_b, cols_b, theirs_b, rem_b, loc_b = got
        gqkv_b = seq.fence(gqkv_b, chain_0.came, got_a)
        theirs_b = links.core_swap(seq(theirs_b))
        chain_0.next()
        chain_1 = Chain(links, seq, seq(chain_1_value))
        theirs_a = theirs_a.reshape(-1, theirs_a.shape[2])
        def along_x(loc, theirs, got):
            quarter = half // 2
            terms = [(seq(loc), 0), (theirs, half), (got, 0)]
            send = seq.mark(cut_sum(1 - x, quarter, terms))
            return Chain(links, seq, cut_sum(x, quarter, terms), links.x_swap(send))

        chain_a = along_x(loc_a, theirs_a, got_a)
        far_b = seq.mark(seq(rem_b) + theirs_b[0])
        got_b = links.y_swap(far_b)
        theirs_b = theirs_b.reshape(-1, theirs_b.shape[2])
        plan = ((0, 0, 1, 0, 768), (0, 768, 0, 0, 768), (1, 0, 1, 768, 384), (1, 384, 0, 768, 384))
        grad_tokens, sums_one = input_backward(
            plan, [gqkv_a, gqkv_b], [w_in["loc"], w_in["rem"]], tokens, grad_middle, seq(rows8)
        )
        sums_one = seq.fence(sums_one, chain_0.came, chain_1.came, chain_a.came, got_b)
        chain_a.next()
        bias_a, bias_b, cols_a, cols_b = [seq(v) for v in (bias_a, bias_b, cols_a, cols_b)]
        up_bias_grad = [seq(v) for v in up_bias_grad]

        chain_0.next()
        chain_1.next()
        chain_b = along_x(loc_b, theirs_b, got_b)

        def by_place(first, second):
            return jnp.where(core == 0, jnp.concatenate([first, second]), jnp.concatenate([second, first]))

        by_t = [jnp.where(x == t, up_bias_grad[0], up_bias_grad[2]) for t in range(2)]
        rem = [jnp.concatenate([grad[0, 0, at : at + PIECE] for grad in by_t]) for at in (0, PIECE)]
        bias_up_parts = [by_place(*rem), by_place(up_bias_grad[1][0, 0], up_bias_grad[1][1, 0])]

        def of_part(at):
            sums = [bias_a[:, at * 512 : (at + 1) * 512], bias_b[:, at * 256 : (at + 1) * 256]]
            cols = [cols_a[:, at * 256 : (at + 1) * 256], cols_b[:, at * 128 : (at + 1) * 128]]
            table = table_grad(onehot, jnp.concatenate(sums, axis=1))
            return [jnp.concatenate(cols, axis=1).reshape(-1), bias_up_parts[at], table.reshape(-1)]

        values = [sums_two.reshape(-1), sums_one.reshape(-1), *of_part(1), *of_part(0)]
        small_chain = SmallChain(links, seq, jnp.concatenate(values), 6 * width, small_size + bias_table.size)
        waves = (
            (chain_a, chain_b, chain_0, chain_1, small_chain),
            (chain_a, chain_b, chain_1, chain_0, small_chain),
            (chain_a, chain_1, chain_b, small_chain),
        )
        for wave in waves:
            for chain in wave:
                chain.next()
        pairs = [p for pair in zip(chain_0.pieces, chain_1.pieces) for p in pair]
        places = jnp.stack([2 * c + t for c in (core, 1 - core) for t in (1 - x, x)]).astype(jnp.int32)
        grad_down, grad_up = place_mlp(tie(places, seq.last), pairs, w_down.shape, w_up.shape)
        grad_down = seq.mark(grad_down)
        for chain in (chain_b, chain_a, small_chain, chain_b):
            chain.next()
        grad_qkv, grad_proj = place_two(links.order(), chain_a.pieces, chain_b.pieces, w_qkv.shape, w_proj.shape)
        got = small_chain.value
        two = got[: 4 * width].reshape(4, width)
        late = got[4 * width : 6 * width].reshape(2, width)
        got = got[6 * width :]
        cols = bias_query.shape[0]
        grad_query_b, grad_value_b = got[:cols], got[cols : 2 * cols]
        grad_up_bias = got[2 * cols : small_size]
        grad_table = got[small_size:].reshape(bias_table.shape)
    else:
        groups = tables["all"].shape[1] // GROUP
        got = attention_backward(core_at, branch, normed, [[unit("all", g) for g in range(groups)]])
        gqkv, bias_sums, col_sums, second_half, first_half = got
        grad_tokens, sums_one = input_backward(
            ((0, 0, 0, 0, gqkv.shape[1]),), [gqkv], [w_in["all"]], tokens, grad_middle, rows8
        )

        def summed(value, axis):
            value = lax.psum_scatter(value, "mp", scatter_dimension=axis, tiled=True)
            return lax.psum(value, "dp")

        hidden_grads = jnp.concatenate([own[0], other[0]]).reshape(-1, 2, PIECE, width)
        grad_down = summed(hidden_grads[:, 0].reshape(-1, width), 0).astype(f32)
        grad_up = summed(hidden_grads[:, 1].reshape(-1, width).T, 1).astype(f32)
        cols = gqkv.shape[1]
        grad_proj = summed(dot(att["all"], branch, TN).astype(bf16), 0).astype(f32)
        in_order = jnp.concatenate([first_half, second_half[0]], axis=0).reshape(-1, 384)
        natural = dot(in_order, group_order(), NT).reshape(width, cols).astype(bf16)
        grad_qkv = summed(natural, 1).astype(f32)
        grad_query_b = summed(col_sums[0], 0)
        grad_value_b = summed(col_sums[1], 0)
        grad_up_bias = summed(up_bias_grad[0].reshape(-1), 0)
        grad_table = summed(table_grad(onehot, bias_sums), 1)
        two, late = lax.psum((sums_two, sums_one), ("dp", "mp"))
    return (
        block_out[:real_rows],
        grad_tokens[:real_rows],
        late[0],
        late[1],
        grad_qkv,
        grad_query_b,
        grad_value_b,
        grad_table,
        grad_proj,
        two[2],
        two[0],
        two[1],
        grad_up,
        grad_up_bias,
        grad_down,
        two[3],
    )


def solution(mesh):
    direct = mesh.shape["dp"] == 16 and mesh.shape["mp"] == 2
    return jax.shard_map(
        functools.partial(on_device, direct),
        mesh=mesh,
        in_specs=(
            P(("dp", "mp"), None),
            P("dp"),
            P(),
            P(),
            P(),
            P(None, "mp"),
            P("mp"),
            P("mp"),
            P(None, "mp"),
            P("mp", None),
            P(),
            P(),
            P(),
            P(None, "mp"),
            P("mp"),
            P("mp", None),
            P(),
            P(("dp", "mp"), None),
        ),
        out_specs=(
            P(("dp", "mp"), None),
            P(("dp", "mp"), None),
            P(),
            P(),
            P(None, "mp"),
            P("mp"),
            P("mp"),
            P(None, "mp"),
            P("mp", None),
            P(),
            P(),
            P(),
            P(None, "mp"),
            P("mp"),
            P("mp", None),
            P(),
        ),
        check_vma=False,
    )
```

```python
import functools

import jax
import jax.numpy as jnp
from jax import lax
from jax.experimental import pallas as pl
from jax.experimental.pallas import tpu as pltpu
from jax.sharding import PartitionSpec as P

HEAD_DIM = 32
SLOTS = 49
PAD = 64
KEYS = 56
PIECE = 384
GROUP = 4
SPARE = 16
norm_eps = 1e-05
mask_fill = -1000000000.0
f32 = jnp.float32
bf16 = jnp.bfloat16
MIB = 1024 * 1024


def cost(micros):
    return pl.CostEstimate(flops=int(micros * 1.0e9), bytes_accessed=int(micros * 1.0e5), transcendentals=0)


def params(limit=56):
    return pltpu.CompilerParams(vmem_limit_bytes=limit * MIB)


def whole(shape):
    return pl.BlockSpec(shape, lambda *_: (0,) * len(shape))


def dot(left, right, dims=((1,), (0,))):
    return lax.dot_general(left, right, (dims, ((), ())), preferred_element_type=f32)


NT = ((1,), (1,))
TN = ((0,), (0,))


def norm_parts(values):
    mean = jnp.mean(values, axis=-1, keepdims=True)
    centred = values - mean
    spread = jnp.mean(centred * centred, axis=-1, keepdims=True)
    return centred, lax.rsqrt(spread + norm_eps)


def norm_back(values, gain, grad):
    centred, inverse = norm_parts(values)
    unit = centred * inverse
    scaled = grad * gain
    first = jnp.mean(scaled, axis=-1, keepdims=True)
    second = jnp.mean(scaled * unit, axis=-1, keepdims=True)
    return inverse * (scaled - first - unit * second), grad * unit


def col_sum(values):
    return jnp.sum(values, axis=0, keepdims=True)


def row_blocks(rows):
    size = 256 if rows % 16 == 0 else rows
    starts = list(range(0, rows, size))
    if len(starts) > 1 and rows - starts[-1] < 128:
        starts.pop()
    return [(s, (starts[i + 1] if i + 1 < len(starts) else rows) - s) for i, s in enumerate(starts)]


def diagonal(rows_of_heads):
    lane = lax.broadcasted_iota(jnp.int32, (PAD, 128), 1)
    out = rows_of_heads[3 * PAD :]
    for head in (2, 1, 0):
        out = jnp.where(lane < (head + 1) * HEAD_DIM, rows_of_heads[head * PAD : (head + 1) * PAD], out)
    return out


def spread(rows, block_mask):
    return jnp.concatenate([rows] * GROUP, axis=0) * block_mask


def block_mask_of():
    row = lax.broadcasted_iota(jnp.int32, (GROUP * PAD, 128), 0) // PAD
    lane = lax.broadcasted_iota(jnp.int32, (GROUP * PAD, 128), 1) // HEAD_DIM
    return (row == lane).astype(f32).astype(bf16)


def window_rows_mask(rows, cols):
    return lax.rem(lax.broadcasted_iota(jnp.int32, (rows, cols), 0), PAD) < SLOTS


def batch_of(windows):
    return 8 if windows % 8 == 0 else windows


def step_rows(ref, step, batch):
    if batch % 8:
        return ref
    return ref.at[pl.ds(pl.multiple_of(step * batch * SLOTS, 8), batch * SLOTS + SPARE)]


def pad_windows(src, dst, step, batch):
    view = step_rows(src, step, batch)
    for j in range(batch):
        dst[j * PAD : (j + 1) * PAD, :] = view[j * SLOTS : j * SLOTS + PAD, :].astype(bf16)


def fwd_kernel(groups, pieces, places, tokens, rows8, small, pos, mask, *refs):
    ws, refs = refs[: max(pieces, 1)], refs[max(pieces, 1) :]
    qkv, probs, att, wp, padded = refs[:5]
    normed, att_s, pos_s = refs[-3:]
    step = pl.program_id(0)
    rows = tokens.shape[0]

    @pl.when(step == 0)
    def _():
        centred, inverse = norm_parts(tokens[...].astype(f32))
        value = (centred * inverse * rows8[0:1, :] + rows8[1:2, :]).astype(bf16)
        normed[0:rows, :] = value.astype(f32)
        normed[rows:, :] = jnp.zeros_like(normed[rows:, :])
        order = group_order()
        for r, w in enumerate(ws):
            if pieces:
                size = w.shape[0]
                at = pl.ds(pl.multiple_of(places[r] * size, 16), size)
            else:
                at = slice(0, w.shape[0])
            for g in range(groups):
                cols = slice(g * 384, (g + 1) * 384)
                wp[at, cols] = dot(w[:, cols], order).astype(bf16)
        slot = lax.broadcasted_iota(jnp.int32, (KEYS, 128), 0) < SLOTS
        for h in range(0, groups * GROUP, 2):
            both = jnp.concatenate([pos[h], pos[h + 1]], axis=1)
            pos_s[:, h * PAD : (h + 2) * PAD] = jnp.where(slot, both, 2 * mask_fill)

    batch = mask.shape[0]
    pad_windows(normed, padded, step, batch)
    att_view = step_rows(att_s, step, batch)
    block_mask = block_mask_of()
    keep = window_rows_mask(batch * PAD, 128)
    left = padded[...]
    for g in range(groups):
        value = dot(left, wp[:, g * 384 : (g + 1) * 384])
        for part, bias in enumerate((small[g], None, small[groups + g])):
            piece = value[:, part * 128 : (part + 1) * 128]
            if bias is not None:
                piece = piece + bias
            qkv[:, g * 384 + part * 128 : g * 384 + (part + 1) * 128] = jnp.where(keep, piece, 0.0).astype(bf16)
    for j in range(batch):
        rows_at = slice(j * PAD, (j + 1) * PAD)
        allowed = mask[j] > 0.0
        allowed = jnp.concatenate([allowed, allowed], axis=1)
        for g in range(groups):
            at = g * 384
            query = qkv[rows_at, at : at + 128]
            key = qkv[rows_at, at + 128 : at + 256]
            value = qkv[rows_at, at + 256 : at + 384]
            raw = dot(key, spread(query, block_mask), NT)[:KEYS]
            scores = raw * HEAD_DIM ** (-0.5) + pos_s[:, g * 256 : (g + 1) * 256]
            scores = jnp.where(allowed, scores, mask_fill)
            top = jnp.max(scores, axis=0, keepdims=True)
            power = jnp.exp(scores - top)
            total = jnp.sum(power, axis=0, keepdims=True)
            prob = power * (1.0 / total)
            prob = jnp.concatenate([prob, jnp.zeros((PAD - KEYS, 256), f32)], axis=0).astype(bf16)
            probs[j, :, g * 256 : (g + 1) * 256] = prob
            out = diagonal(dot(prob, value, TN))
            att_view[j * SLOTS : j * SLOTS + KEYS, g * 128 : (g + 1) * 128] = out[:KEYS]

    @pl.when(step == pl.num_programs(0) - 1)
    def _():
        windows = pl.num_programs(0) * batch
        value = att_s[0:rows, :]
        real = lax.broadcasted_iota(jnp.int32, value.shape, 0) < windows * SLOTS
        att[...] = jnp.where(real, value, 0.0).astype(bf16)


def attention_forward(places, tokens, rows8, small, pos, mask, ws):
    rows, width = tokens.shape
    windows = mask.shape[0]
    pieces = len(ws) if len(ws) > 1 else 0
    heads = pos.shape[0]
    groups = heads // GROUP
    cols = groups * 384
    batch = batch_of(windows)
    steps = windows // batch
    quad_rows = batch * PAD
    out_shape = [
        jax.ShapeDtypeStruct((windows * PAD, cols), bf16),
        jax.ShapeDtypeStruct((windows, PAD, heads * PAD), bf16),
        jax.ShapeDtypeStruct((rows, heads * HEAD_DIM), bf16),
        jax.ShapeDtypeStruct((width, cols), bf16),
        jax.ShapeDtypeStruct((windows * PAD, width), bf16),
    ]
    out_specs = [
        pl.BlockSpec((quad_rows, cols), lambda i, s: (i, 0)),
        pl.BlockSpec((batch, PAD, heads * PAD), lambda i, s: (i, 0, 0)),
        whole((rows, heads * HEAD_DIM)),
        whole((width, cols)),
        pl.BlockSpec((quad_rows, width), lambda i, s: (i, 0)),
    ]
    return pl.pallas_call(
        functools.partial(fwd_kernel, groups, pieces),
        grid_spec=pltpu.PrefetchScalarGridSpec(
            num_scalar_prefetch=1,
            grid=(steps,),
            in_specs=[
                whole((rows, width)),
                whole(rows8.shape),
                whole(small.shape),
                whole(pos.shape),
                pl.BlockSpec((batch, KEYS, 128), lambda i, s: (i, 0, 0)),
            ]
            + [whole(w.shape) for w in ws],
            out_specs=out_specs,
            scratch_shapes=[
                pltpu.VMEM((rows + SPARE, width), f32),
                pltpu.VMEM((rows + SPARE, heads * HEAD_DIM), f32),
                pltpu.VMEM((KEYS, heads * PAD), f32),
            ],
        ),
        out_shape=tuple(out_shape),
        compiler_params=params(),
        cost_estimate=cost(11 * groups / 3),
        name="attention_forward",
    )(places, tokens, rows8, small, pos, mask, *ws)


def proj_kernel(parts, pieces, places, *refs):
    atts, ws = refs[:parts], list(refs[parts : 2 * parts - (1 if pieces else 0)])
    refs = refs[parts + len(ws) :]
    tokens, rows8, middle, low = refs[pieces : pieces + 4]
    if pieces:
        joined = refs[pieces + 4]
        for r, piece in enumerate(refs[:pieces]):
            size = piece.shape[1]
            joined[:, pl.ds(pl.multiple_of(places[r] * size, 128), size)] = piece[...]
        ws.append(joined)
    for start, size in row_blocks(tokens.shape[0]):
        at = slice(start, start + size)
        value = tokens[at, :].astype(f32) + rows8[2:3, :]
        for a, w in zip(atts, ws):
            value = value + dot(a[at, :], w[...])
        middle[at, :] = value
        centred, inverse = norm_parts(value)
        low[at, :] = (centred * inverse * rows8[3:4, :] + rows8[4:5, :]).astype(bf16)


def project(places, atts, ws, pieces, tokens, rows8):
    rows, width = tokens.shape
    ins = [*atts, *ws, *pieces, tokens, rows8]
    out_shape = [jax.ShapeDtypeStruct((rows, width), f32), jax.ShapeDtypeStruct((rows, width), bf16)]
    if pieces:
        out_shape.append(jax.ShapeDtypeStruct((pieces[0].shape[0], width), bf16))
    return pl.pallas_call(
        functools.partial(proj_kernel, len(atts), len(pieces)),
        grid_spec=pltpu.PrefetchScalarGridSpec(
            num_scalar_prefetch=1,
            grid=(1,),
            in_specs=[whole(v.shape) for v in ins],
            out_specs=[whole(o.shape) for o in out_shape],
        ),
        out_shape=tuple(out_shape),
        compiler_params=params(),
        cost_estimate=cost(5),
        name="project",
    )(places, *ins)


def gelu_parts(x):
    z = jnp.abs(x) * 0.7071067811865476
    t = 1.0 / (1.0 + 0.3275911 * z)
    e = jnp.exp(-z * z)
    half = t * (0.127414796 + t * (-0.142248368 + t * (0.7107068705 + t * (-0.7265760135 + t * 0.5307027145)))) * e
    cdf = jnp.where(x >= 0.0, 1.0 - half, half)
    return cdf, e * 0.3989422804014327


def mlp_kernel(first, last, held_pieces, base, order, *refs):
    low, dy, small, rows8 = refs[:4]
    ws, refs = refs[4 : 8 if held_pieces else 6], refs[8 if held_pieces else 6 :]
    if not first:
        out_in, two_in = refs[:2]
        refs = refs[2:]
    if last:
        middle, own, other, gbias, block_out, grad_middle, branch, sums = refs[:8]
        acc_out, acc_two, hid_s, gp_s = refs[8:12]
        refs = refs[12:]
    else:
        own, other, gbias, acc_out, acc_two, hid_s, gp_s = refs[:7]
        refs = refs[7:]
    step = pl.program_id(0)
    rows = low.shape[0]
    copies, carry = [], []
    if not first:
        *refs, carry_sems = refs
        carry = [
            pltpu.make_async_copy(out_in, acc_out, carry_sems.at[0]),
            pltpu.make_async_copy(two_in, acc_two, carry_sems.at[1]),
        ]
    if held_pieces:
        held, sems = refs
        for i, w in enumerate(ws):
            r, k = i // 2, i % 2
            copies.append(pltpu.make_async_copy(w, held.at[k, r * PIECE : (r + 1) * PIECE], sems.at[i]))
        for copy in copies:
            copy.start()
        up, down = held.at[0], held.at[1]
        up_dims, back_dims = NT, ((1,), (0,))
    else:
        up, down = ws
        up_dims, back_dims = ((1,), (0,)), NT

    @pl.when(step == 0)
    def _():
        if first:
            acc_out[...] = jnp.zeros_like(acc_out)
            acc_two[...] = jnp.zeros_like(acc_two)
        for copy in carry:
            copy.start()

    for copy in copies[0::2]:
        copy.wait()
    bias = [small[base + 3 * order[2 * step + t // 3] + t % 3] for t in range(6)]
    bias = jnp.concatenate(bias, axis=1)
    total = jnp.zeros(bias.shape, f32)
    for start, size in row_blocks(rows):
        at = slice(start, start + size)
        pre = dot(low[at, :], up[...], up_dims) + bias
        if start == 0:
            for copy in copies[1::2]:
                copy.wait()
        back = dot(dy[at, :], down[...], NT)
        cdf, pdf = gelu_parts(pre)
        hid = (pre * cdf).astype(bf16)
        gp = (back * (cdf + pre * pdf)).astype(bf16)
        hid_s[at, :] = hid
        gp_s[at, :] = gp
        total = total + col_sum(gp.astype(f32))
        if start == 0:

            @pl.when(step == 0)
            def _():
                for copy in carry:
                    copy.wait()

        acc_out[at, :] += dot(hid, down[...])
        acc_two[at, :] += dot(gp, up[...], back_dims)
    gbias[0] = total

    def weight_rows(out, at, piece):
        cols = slice(piece * PIECE, (piece + 1) * PIECE)
        out[at : at + PIECE, :] = dot(hid_s[:, cols], dy[...], TN).astype(bf16)
        out[at + PIECE : at + 2 * PIECE, :] = dot(gp_s[:, cols], low[...], TN).astype(bf16)

    if held_pieces:
        weight_rows(own, 0, 0)
        weight_rows(other, 0, 1)
    else:
        for out, now in ((own, step < pl.num_programs(0) // 2), (other, step >= pl.num_programs(0) // 2)):

            @pl.when(now)
            def _(out=out):
                for t in range(2):
                    weight_rows(out, 2 * t * PIECE, t)

    if last:

        @pl.when(step == pl.num_programs(0) - 1)
        def _():
            s_gain = s_shift = s_branch = s_down = jnp.zeros((1, low.shape[1]), f32)
            for start, size in row_blocks(rows):
                at = slice(start, start + size)
                mid = middle[at, :]
                block_out[at, :] = (mid + acc_out[at, :] + rows8[5:6, :]).astype(bf16)
                two = acc_two[at, :]
                up_grad = dy[at, :].astype(f32)
                grad, for_gain = norm_back(mid, rows8[3:4, :], two)
                grad = grad + up_grad
                grad_middle[at, :] = grad
                low_grad = grad.astype(bf16)
                branch[at, :] = low_grad
                s_gain += col_sum(for_gain)
                s_shift += col_sum(two)
                s_branch += col_sum(low_grad.astype(f32))
                s_down += col_sum(up_grad)
            sums[...] = jnp.concatenate([s_gain, s_shift, s_branch, s_down], axis=0)


def mlp(order, low, dy, small, base, rows8, ws, carried=None, middle=None):
    rows, width = low.shape
    held = isinstance(ws, list)
    units = 2 * PIECE if held else ws[1].shape[0]
    steps = units // (2 * PIECE)
    first, last = carried is None, middle is not None
    ins = [low, dy, small, rows8, *ws]
    specs = [whole((rows, width)), whole((rows, width)), whole(small.shape), whole(rows8.shape)]
    if held:
        specs += [pl.BlockSpec(memory_space=pl.ANY)] * 4
        grads = [jax.ShapeDtypeStruct((2 * PIECE, width), bf16)] * 2
        grad_specs = [whole((2 * PIECE, width))] * 2
    else:
        specs += [
            pl.BlockSpec((width, 2 * PIECE), lambda i, o: (0, o[2 * i] // 2)),
            pl.BlockSpec((2 * PIECE, width), lambda i, o: (o[2 * i] // 2, 0)),
        ]
        many = steps // 2
        grads = [jax.ShapeDtypeStruct((many * 4 * PIECE, width), bf16)] * 2
        grad_specs = [
            pl.BlockSpec((4 * PIECE, width), lambda i, o: (jnp.minimum(i, many - 1), 0)),
            pl.BlockSpec((4 * PIECE, width), lambda i, o: (jnp.maximum(i - many, 0), 0)),
        ]
    outs = [*grads, jax.ShapeDtypeStruct((steps, 1, 2 * PIECE), f32)]
    out_specs = [*grad_specs, pl.BlockSpec((1, 1, 2 * PIECE), lambda i, o: (i, 0, 0))]
    scratch = []
    if not first:
        ins += list(carried)
        specs += [pl.BlockSpec(memory_space=pl.ANY)] * 2
    if last:
        ins.append(middle)
        specs.append(whole((rows, width)))
        outs += [
            jax.ShapeDtypeStruct((rows, width), bf16),
            jax.ShapeDtypeStruct((rows, width), f32),
            jax.ShapeDtypeStruct((rows, width), bf16),
            jax.ShapeDtypeStruct((4, width), f32),
        ]
        out_specs += [whole((rows, width))] * 3 + [whole((4, width))]
        scratch = [pltpu.VMEM((rows, width), f32)] * 2
    else:
        outs += [jax.ShapeDtypeStruct((rows, width), f32)] * 2
        out_specs += [whole((rows, width))] * 2
    scratch += [pltpu.VMEM((rows, 2 * PIECE), bf16)] * 2
    if held:
        scratch += [pltpu.VMEM((2, 2 * PIECE, width), bf16), pltpu.SemaphoreType.DMA((4,))]
    if not first:
        scratch.append(pltpu.SemaphoreType.DMA((2,)))
    return pl.pallas_call(
        functools.partial(mlp_kernel, first, last, held, base),
        grid_spec=pltpu.PrefetchScalarGridSpec(
            num_scalar_prefetch=1, grid=(steps,), in_specs=specs, out_specs=out_specs, scratch_shapes=scratch
        ),
        out_shape=tuple(outs),
        compiler_params=params(),
        cost_estimate=cost(11 * steps),
        name="mlp",
    )(order, *ins)


def bwd_kernel(parts, each, with_proj, core, branch, normed, *refs):
    units = parts * each
    atts, refs = refs[: parts * with_proj], refs[parts * with_proj :]
    wprojs, qkvs, probs = refs[:units], refs[units : 2 * units], refs[2 * units : 3 * units]
    gqkv, bias_sum, col_sums, theirs = refs[3 * units : 3 * units + 4]
    mine, (wide, padded, wcat, total) = refs[3 * units + 4 : -4], refs[-4:]
    step = pl.program_id(0)
    rows = branch.shape[0]
    half = normed.shape[1] // 2

    @pl.when(step == 0)
    def _():
        wide[0:rows, :] = branch[...].astype(f32)
        wide[rows:, :] = jnp.zeros_like(wide[rows:, :])
        bias_sum[...] = jnp.zeros_like(bias_sum)
        col_sums[...] = jnp.zeros_like(col_sums)
        for u in range(units):
            wcat[u * 128 : (u + 1) * 128, :] = wprojs[u][...]
        if with_proj:
            for out_at, place in ((mine, core[0]), (None, 1 - core[0])):
                right = branch[:, pl.ds(pl.multiple_of(place * half, 128), half)]
                for p in range(parts):
                    value = dot(atts[p][...], right, TN).astype(bf16)
                    if out_at is None:
                        theirs[p, :, each * 384 :] = value
                    else:
                        mine[p][:, each * 384 :] = value

    batch = probs[0].shape[0]
    pad_windows(wide, padded, step, batch)
    block_mask = block_mask_of()
    scale = HEAD_DIM ** (-0.5)
    grads = dot(padded[...], wcat[...], NT)
    grads = jnp.where(window_rows_mask(batch * PAD, grads.shape[1]), grads, 0.0).astype(bf16)
    for u in range(units):
        qkv, at = qkvs[u], u * 384
        bias_total = jnp.zeros((KEYS, 256), f32)
        col_total = [jnp.zeros((1, 128), f32)] * 2
        for j in range(batch):
            rows_at = slice(j * PAD, (j + 1) * PAD)
            query = qkv[rows_at, 0:128]
            key = qkv[rows_at, 128:256]
            value = qkv[rows_at, 256:384]
            prob_low = probs[u][j]
            grad = spread(grads[rows_at, u * 128 : (u + 1) * 128], block_mask)
            prob = prob_low.astype(f32)[:KEYS]
            prob_grad = dot(value, grad, NT)[:KEYS]
            both = prob * prob_grad
            score_grad = both - prob * jnp.sum(both, axis=0, keepdims=True)
            score_grad = jnp.concatenate([score_grad, jnp.zeros((PAD - KEYS, 256), f32)], axis=0).astype(bf16)
            bias_total = bias_total + score_grad.astype(f32)[:KEYS]
            grad_value = dot(prob_low, grad).astype(bf16)
            grad_key = (dot(score_grad, spread(query, block_mask)) * scale).astype(bf16)
            grad_query = (diagonal(dot(score_grad, key, TN)) * scale).astype(bf16)
            gqkv[rows_at, at : at + 128] = grad_query
            gqkv[rows_at, at + 128 : at + 256] = grad_key
            gqkv[rows_at, at + 256 : at + 384] = grad_value
            col_total[0] = col_total[0] + col_sum(grad_query.astype(f32))
            col_total[1] = col_total[1] + col_sum(grad_value.astype(f32))
        bias_sum[:, u * 256 : (u + 1) * 256] += bias_total
        col_sums[0:1, u * 128 : (u + 1) * 128] += col_total[0]
        col_sums[1:2, u * 128 : (u + 1) * 128] += col_total[1]
    grad = dot(normed[...], gqkv[...], TN)

    @pl.when(step == 0)
    def _():
        total[...] = grad

    @pl.when(step > 0)
    def _():
        total[...] += grad

    @pl.when(step == pl.num_programs(0) - 1)
    def _():
        for p in range(parts):
            cols = slice(p * each * 384, (p + 1) * each * 384)
            mine[p][:, 0 : each * 384] = total[pl.ds(pl.multiple_of(core[0] * half, 16), half), cols].astype(bf16)
            other = pl.ds(pl.multiple_of((1 - core[0]) * half, 16), half)
            theirs[p, :, 0 : each * 384] = total[other, cols].astype(bf16)


def attention_backward(core, branch, normed, parts, atts=()):
    rows, width = branch.shape
    units = [u for part in parts for u in part]
    windows = units[0][2].shape[0]
    count, each = len(units), len(parts[0])
    batch = batch_of(windows)
    quad_rows = batch * PAD
    half = (width // 2, each * 384 + (width // 2 if atts else 0))
    in_specs = [whole((rows, width)), pl.BlockSpec((quad_rows, width), lambda i, s: (i, 0))]
    in_specs += [whole(a.shape) for a in atts]
    in_specs += [pl.BlockSpec((128, width), lambda i, s, g=g: (g, 0)) for _, _, _, g in units]
    in_specs += [pl.BlockSpec((quad_rows, 384), lambda i, s, g=g: (i, g)) for _, _, _, g in units]
    in_specs += [pl.BlockSpec((batch, PAD, 256), lambda i, s, g=g: (i, 0, g)) for _, _, _, g in units]
    return pl.pallas_call(
        functools.partial(bwd_kernel, len(parts), each, 1 if atts else 0),
        grid_spec=pltpu.PrefetchScalarGridSpec(
            num_scalar_prefetch=1,
            grid=(windows // batch,),
            in_specs=in_specs,
            out_specs=[
                pl.BlockSpec((quad_rows, count * 384), lambda i, s: (i, 0)),
                whole((KEYS, count * 256)),
                whole((2, count * 128)),
                whole((len(parts), *half)),
            ]
            + [whole(half)] * len(parts),
            scratch_shapes=[
                pltpu.VMEM((rows + SPARE, width), f32),
                pltpu.VMEM((quad_rows, width), bf16),
                pltpu.VMEM((count * 128, width), bf16),
                pltpu.VMEM((width, count * 384), f32),
            ],
        ),
        out_shape=(
            jax.ShapeDtypeStruct((windows * PAD, count * 384), bf16),
            jax.ShapeDtypeStruct((KEYS, count * 256), f32),
            jax.ShapeDtypeStruct((2, count * 128), f32),
            jax.ShapeDtypeStruct((len(parts), *half), bf16),
        )
        + (jax.ShapeDtypeStruct(half, bf16),) * len(parts),
        compiler_params=params(),
        cost_estimate=cost(5 * count),
        name="attention_backward",
    )(core, branch, normed, *atts, *[u[0] for u in units], *[u[1] for u in units], *[u[2] for u in units])


def input_kernel(plan, arrays, *refs):
    gqkvs, refs = refs[:arrays], refs[arrays:]
    ws, refs = refs[: -6], refs[-6:]
    tokens, grad_middle, rows8, grad_tokens, sums, compact = refs
    step = pl.program_id(0)
    total = None
    for a, a_at, w, w_at, size in plan:
        term = dot(gqkvs[a][:, a_at : a_at + size], ws[w][:, w_at : w_at + size], NT)
        total = term if total is None else total + term
    batch = total.shape[0] // PAD
    view = step_rows(compact, step, batch)
    for j in range(batch):
        view[j * SLOTS : j * SLOTS + KEYS, :] = total[j * PAD : j * PAD + KEYS]

    @pl.when(step == pl.num_programs(0) - 1)
    def _():
        rows = tokens.shape[0]
        windows = pl.num_programs(0) * batch
        s_gain = s_shift = jnp.zeros((1, tokens.shape[1]), f32)
        for start, size in row_blocks(rows):
            at = slice(start, start + size)
            one = compact[at, :]
            if start + size == rows:
                real = start + lax.broadcasted_iota(jnp.int32, one.shape, 0) < windows * SLOTS
                one = jnp.where(real, one, 0.0)
            grad, for_gain = norm_back(tokens[at, :].astype(f32), rows8[0:1, :], one)
            grad_tokens[at, :] = (grad_middle[at, :] + grad).astype(bf16)
            s_gain += col_sum(for_gain)
            s_shift += col_sum(one)
        sums[...] = jnp.concatenate([s_gain, s_shift], axis=0)


def input_backward(plan, gqkvs, ws, tokens, grad_middle, rows8):
    rows, width = tokens.shape
    quad_rows = batch_of(gqkvs[0].shape[0] // PAD) * PAD
    steps = gqkvs[0].shape[0] // quad_rows
    return pl.pallas_call(
        functools.partial(input_kernel, plan, len(gqkvs)),
        grid=(steps,),
        in_specs=[pl.BlockSpec((quad_rows, a.shape[1]), lambda i: (i, 0)) for a in gqkvs]
        + [whole(w.shape) for w in ws]
        + [whole((rows, width)), whole((rows, width)), whole(rows8.shape)],
        out_specs=[whole((rows, width)), whole((2, width))],
        out_shape=(jax.ShapeDtypeStruct((rows, width), bf16), jax.ShapeDtypeStruct((2, width), f32)),
        scratch_shapes=[pltpu.VMEM((rows + SPARE, width), f32)],
        compiler_params=params(),
        cost_estimate=cost(11),
        name="input_backward",
    )(*gqkvs, *ws, tokens, grad_middle, rows8)


def stack_kernel(count, *refs):
    rows8, small = refs[-2:]
    rows8[...] = jnp.zeros_like(rows8)
    for i, ref in enumerate(refs[:count]):
        rows8[i : i + 1, :] = ref[...].astype(f32).reshape(1, -1)
    at = 0
    for ref in refs[count:-2]:
        value = ref[...].astype(f32)
        for start in range(0, ref.shape[0], 128):
            small[at] = value[start : start + 128].reshape(1, 128)
            at += 1


def stack_rows(vectors, others):
    count = sum(v.shape[0] for v in others) // 128
    return pl.pallas_call(
        functools.partial(stack_kernel, len(vectors)),
        out_shape=(
            jax.ShapeDtypeStruct((8, vectors[0].shape[0]), f32),
            jax.ShapeDtypeStruct((count, 1, 128), f32),
        ),
        cost_estimate=cost(1),
        name="stack_rows",
    )(*vectors, *others)


def pack_kernel(core, source, out):
    out[...] = source[...]


def pack_half(core, weight, axis):
    out = tuple(n // 2 if i == axis else n for i, n in enumerate(weight.shape))
    return pl.pallas_call(
        pack_kernel,
        grid_spec=pltpu.PrefetchScalarGridSpec(
            num_scalar_prefetch=1,
            grid=(1,),
            in_specs=[pl.BlockSpec(out, lambda i, s: (s[0], 0) if axis == 0 else (0, s[0]))],
            out_specs=whole(out),
        ),
        out_shape=jax.ShapeDtypeStruct(out, weight.dtype),
        compiler_params=params(16),
        cost_estimate=cost(2),
        name="pack_half",
    )(core, weight)


def pack_piece_kernel(place, up, down, up_out, down_out):
    up_out[...] = up[...].astype(f32).T.astype(bf16)
    down_out[...] = down[...]


def pack_piece(place, w_up, w_down):
    width = w_up.shape[0]
    return pl.pallas_call(
        pack_piece_kernel,
        grid_spec=pltpu.PrefetchScalarGridSpec(
            num_scalar_prefetch=1,
            grid=(1,),
            in_specs=[
                pl.BlockSpec((width, PIECE), lambda i, s: (0, s[0])),
                pl.BlockSpec((PIECE, width), lambda i, s: (s[0], 0)),
            ],
            out_specs=[whole((PIECE, width))] * 2,
        ),
        out_shape=(jax.ShapeDtypeStruct((PIECE, width), bf16),) * 2,
        compiler_params=params(32),
        cost_estimate=cost(3),
        name="pack_piece",
    )(place, w_up, w_down)


def group_order():
    at = lax.broadcasted_iota(jnp.int32, (384, 384), 1)
    source = (at % 128) // 32 * 96 + at // 128 * 32 + at % 32
    return (lax.broadcasted_iota(jnp.int32, (384, 384), 0) == source).astype(f32).astype(bf16)


def place_mlp_kernel(places, *refs):
    step = pl.program_id(0)
    grad_down, grad_up = refs[-2:]
    for i in range(4):

        @pl.when(step == i)
        def _(down=refs[2 * i], up=refs[2 * i + 1]):
            grad_down[...] = down[...].astype(f32)
            grad_up[...] = up[...].astype(f32).T


def place_mlp(places, pieces, down_shape, up_shape):
    size = pieces[0].shape[0]
    return pl.pallas_call(
        place_mlp_kernel,
        grid_spec=pltpu.PrefetchScalarGridSpec(
            num_scalar_prefetch=1,
            grid=(4,),
            in_specs=[whole(p.shape) for p in pieces],
            out_specs=[
                pl.BlockSpec((size, down_shape[1]), lambda i, s: (s[i], 0)),
                pl.BlockSpec((up_shape[0], size), lambda i, s: (0, s[i])),
            ],
        ),
        out_shape=(jax.ShapeDtypeStruct(down_shape, f32), jax.ShapeDtypeStruct(up_shape, f32)),
        compiler_params=params(),
        cost_estimate=cost(8),
        name="place_mlp",
    )(places, *pieces)


def place_two_kernel(places, *refs):
    step = pl.program_id(0)
    grad_qkv, grad_proj = refs[-2:]
    for i in range(4):

        @pl.when(step == i)
        def _(first=refs[2 * i], second=refs[2 * i + 1]):
            order = group_order()
            grad_qkv[:, 0:384] = dot(first[:, 0:384], order, NT)
            grad_qkv[:, 384:768] = dot(first[:, 384:768], order, NT)
            grad_qkv[:, 768:1152] = dot(second[...], order, NT)
            grad_proj[...] = first[:, 768:1152].astype(f32)


def place_two(places, firsts, seconds, qkv_shape, proj_shape):
    pieces = [p for pair in zip(firsts, seconds) for p in pair]
    rows = firsts[0].shape[0]
    return pl.pallas_call(
        place_two_kernel,
        grid_spec=pltpu.PrefetchScalarGridSpec(
            num_scalar_prefetch=1,
            grid=(4,),
            in_specs=[whole(p.shape) for p in pieces],
            out_specs=[
                pl.BlockSpec((rows, qkv_shape[1]), lambda i, s: (s[i], 0)),
                pl.BlockSpec((rows, proj_shape[1] // 2), lambda i, s: (s[i] % 2, s[i] // 2)),
            ],
        ),
        out_shape=(jax.ShapeDtypeStruct(qkv_shape, f32), jax.ShapeDtypeStruct(proj_shape, f32)),
        compiler_params=params(),
        cost_estimate=cost(5),
        name="place_two",
    )(places, *pieces)


def pair_onehot(rel_index, table_rows):
    turned_index = jnp.pad(rel_index.T, ((0, KEYS - SLOTS), (0, PAD - SLOTS)), constant_values=-1)
    offsets = jnp.arange(table_rows, dtype=jnp.int32)
    return (turned_index[None] == offsets[:, None, None]).astype(bf16)


def position_rows(onehot, table):
    return dot(table, onehot.reshape(onehot.shape[0], KEYS * PAD), TN).reshape(table.shape[1], KEYS, PAD)


def table_grad(onehot, sums):
    rows = onehot.shape[0]
    heads = sums.shape[1] // PAD
    flat = jnp.transpose(sums.reshape(KEYS, heads, PAD), (0, 2, 1)).reshape(KEYS * PAD, heads)
    high = flat.astype(bf16)
    rest = (flat - high.astype(f32)).astype(bf16)
    low = (flat - high.astype(f32) - rest.astype(f32)).astype(bf16)
    both = dot(onehot.reshape(rows, KEYS * PAD), jnp.concatenate([high, rest, low], axis=1))
    return both[:, :heads] + both[:, heads : 2 * heads] + both[:, 2 * heads :]


def window_mask(labels):
    shaped = labels.reshape(-1, SLOTS)
    keys = jnp.pad(shaped, ((0, 0), (0, KEYS - SLOTS)), constant_values=-2)[:, :, None]
    queries = jnp.pad(shaped, ((0, 0), (0, PAD - SLOTS)), constant_values=-3)
    queries = jnp.concatenate([queries, queries], axis=1)[:, None, :]
    key_at = jnp.arange(KEYS)[None, :, None]
    query_at = (jnp.arange(128) % PAD)[None, None, :]
    allowed = (keys == queries) & ((keys >= 0) | (key_at == query_at))
    outside = (key_at >= SLOTS) | (query_at >= SLOTS)
    return (allowed | outside).astype(f32)


class Links:
    def __init__(self):
        at = lax.axis_index("dp")
        self.core = at % 2
        self.x = at // 2 % 2
        self.z = at // 4
        self.inner = (self.z == 1) | (self.z == 2)

    def y_swap(self, value):
        return lax.ppermute(value, "mp", [(0, 1), (1, 0)])

    def flip(self, value, bit):
        return lax.ppermute(value, "dp", [(i, i ^ bit) for i in range(16)])

    def core_swap(self, value):
        return self.flip(value, 1)

    def x_swap(self, value):
        return self.flip(value, 2)

    def z_pairs(self, value):
        return self.flip(value, 4)

    def z_all(self, value):
        return [self.flip(value, 4), self.flip(value, 8), self.flip(value, 12)]

    def z_total(self, value, others):
        pair, far = value.astype(f32) + others[0].astype(f32), others[1].astype(f32) + others[2].astype(f32)
        return (pair + far).astype(value.dtype)

    def z_move(self, value, pairs):
        return lax.ppermute(value, "dp", [(s * 4 + i, d * 4 + i) for s, d in pairs for i in range(4)])

    def z_sum(self, value):
        value = value + self.z_move(value, [(0, 1), (3, 2)])
        value = value + self.z_move(value, [(1, 2), (2, 1)])
        return jnp.where(self.inner, value, self.z_move(value, [(1, 0), (2, 3)]))

    def order(self):
        places = [2 * (self.core ^ (r >> 1)) + (self.x ^ (r & 1)) for r in range(4)]
        return jnp.stack(places).astype(jnp.int32)


def tie(value, *others):
    return lax.optimization_barrier((value, *others))[0]


class Sequence:
    def __init__(self):
        self.last = None

    def __call__(self, value):
        return value if self.last is None else tie(value, self.last)

    def mark(self, value):
        self.last = value
        return value

    def fence(self, value, *others):
        return self.mark(tie(value, *others))


def cut_sum(place, rows, terms):
    cut = [lax.dynamic_slice(t, (start + place * rows, 0), (rows, t.shape[1])).astype(f32) for t, start in terms]
    return sum(cut[1:], cut[0]).astype(bf16)


class Chain:
    def __init__(self, links, seq, value, came=None):
        self.links, self.seq, self.value, self.came = links, seq, value, came
        self.step = 0
        if came is None:
            self.came = links.z_move(seq.mark(value), [(0, 1), (3, 2)])
            self.step = 1

    def next(self):
        links, seq = self.links, self.seq
        pairs = ([(0, 1), (3, 2)], [(1, 2), (2, 1)], [(1, 0), (2, 3)])
        if self.step < 3:
            self.value = seq.mark(seq(self.value) + self.came)
            self.came = links.z_move(self.value, pairs[self.step])
        elif self.step == 3:
            self.value = seq.mark(jnp.where(links.inner, seq(self.value), self.came))
            self.came = links.x_swap(self.value)
            self.core = links.core_swap(self.value)
        else:
            self.beside = seq.mark(seq(self.came))
            self.pieces = [self.value, self.beside, self.core, links.core_swap(self.beside)]
        self.step += 1


class SmallChain:
    def __init__(self, links, seq, value, shared, mine):
        self.links, self.seq, self.value = links, seq, seq(value)
        self.shared, self.mine = shared, mine
        self.came = links.core_swap(self.value)
        self.step = 0

    def next(self):
        links = self.links
        if self.step == 0:
            self.value = self.seq.mark(self.seq(self.value) + self.came)
            self.came = links.x_swap(self.value)
        elif self.step == 1:
            self.value = self.seq.mark(self.seq(self.value) + self.came)
            self.came = links.z_all(self.value)
        elif self.step == 2:
            self.value = self.seq.mark(links.z_total(self.seq(self.value), self.came))
            n = self.shared + self.mine
            self.came = links.y_swap(jnp.concatenate([self.value[: self.shared], self.value[n:]]))
            self.value = self.value[:n]
        else:
            self.value = self.seq.mark(self.seq(self.value) + self.came)
        self.step += 1


def on_device(
    direct,
    tokens,
    image_ids,
    rel_index,
    gain_one,
    shift_one,
    w_qkv,
    bias_query,
    bias_value,
    bias_table,
    w_proj,
    bias_proj,
    gain_two,
    shift_two,
    w_up,
    bias_up,
    w_down,
    bias_down,
    cotangent,
):
    mp = lax.axis_index("mp")
    real_rows = tokens.shape[0]
    labels = lax.dynamic_slice(image_ids, (mp * real_rows,), (real_rows,))
    spare = -real_rows % 16
    tokens = jnp.pad(tokens, ((0, spare), (0, 0)))
    cotangent = jnp.pad(cotangent, ((0, spare), (0, 0)))
    width = tokens.shape[1]
    small_size = bias_query.shape[0] + bias_value.shape[0] + bias_up.shape[0]
    biases = [bias_query, bias_value, bias_up]
    onehot = pair_onehot(rel_index, bias_table.shape[0])
    mask = window_mask(labels)

    if direct:
        links = Links()
        core, x = links.core, links.x
        half = width // 2
        core_at = core.astype(jnp.int32).reshape(1)
        first_own = pack_half(core_at, w_qkv, 0)
        first = links.y_swap(first_own)
        names = ("loc", "rem")
        inputs = dict(loc=[w_qkv], rem=None)
        small = dict(rem=None)
        tables = dict(loc=bias_table, rem=links.y_swap(bias_table))
        w_projs = dict(loc=w_proj)
        by_core_x = (2 * core + x).astype(jnp.int32).reshape(1)
        by_core = jnp.stack([2 * core, 2 * core + 1, 2 - 2 * core, 3 - 2 * core]).astype(jnp.int32)
        orders = dict(loc=core_at, rem=jnp.stack([core, 1 - core]).astype(jnp.int32))
        halves = [("loc", by_core, (w_up, w_down))] + [
            ("rem", 2 * orders["rem"] + t, None) for t in (x, 1 - x)
        ]
        halves = [halves[1], halves[0], halves[2]]
        tokens_first = tie(tokens, first_own)
    else:
        names = ("all",)

        def whole_of(value, axis):
            return lax.all_gather(value, "mp", axis=axis, tiled=True)

        inputs = dict(all=[whole_of(w_qkv, 1)])
        up_all, down_all = whole_of(w_up, 1), whole_of(w_down, 0)
        biases = [whole_of(b, 0) for b in biases]
        small = {}
        tables = dict(all=whole_of(bias_table, 1))
        w_projs = dict(all=whole_of(w_proj, 0))
        core_at = jnp.zeros((1,), jnp.int32)
        orders = dict(all=core_at)
        halves = [("all", jnp.arange(down_all.shape[0] // PIECE, dtype=jnp.int32), (up_all, down_all))]

    rows8, small[names[0]] = stack_rows([gain_one, shift_one, bias_proj, gain_two, shift_two, bias_down], biases)
    if direct:
        small["rem"] = links.y_swap(small["loc"])
    small_pieces = sum(places.shape[0] for name, places, _ in halves if name == names[0]) * 3
    qkv, probs, att, w_in = {}, {}, {}, {}
    for name in names:
        positions = position_rows(onehot, tables[name])
        if inputs[name] is None:
            first = tie(first, qkv["loc"], positions)
            inputs[name] = [first, links.core_swap(first)]
            proj_own = pack_half(core_at, tie(w_proj, first), 1)
            sent = list(pack_piece(by_core_x, tie(w_up, first), w_down))
            proj_far = links.y_swap(tie(proj_own, first))
            came = [links.y_swap(tie(sent[0], first))]
        got = attention_forward(
            orders[name], tokens_first if name == "loc" else tokens, rows8, small[name], positions, mask, inputs[name]
        )
        qkv[name], probs[name], att[name], w_in[name], normed = got[:5]
    pieces = []
    if direct:
        proj_far, came[0] = tie(proj_far, qkv["rem"], came[0]), tie(came[0], qkv["rem"], proj_far)
        pieces = [proj_far, links.core_swap(proj_far)]
        came.append(links.y_swap(tie(sent[1], came[0])))
    got = project(orders[names[-1]], [att[n] for n in names], [w_projs[n] for n in w_projs], pieces, tokens, rows8)
    middle, low_two = got[:2]
    if direct:
        w_projs["rem"] = got[2]
    own, other, up_bias_grad = [], [], []
    carried = None
    for i, (name, places, ws) in enumerate(halves):
        last = i == len(halves) - 1
        low_now = low_two
        base = small[name].shape[0] - small_pieces
        if direct and i == 0:
            came = [tie(piece, low_two, *came) for piece in came]
            beside = [links.x_swap(came[0])]
            ws = came + [links.core_swap(piece) for piece in came]
        if direct and i == 1:
            fence = (own[0], beside[0])
            theirs_f = links.core_swap(tie(other[0], *fence))
            beside.append(links.x_swap(tie(came[1], *fence)))
            swapped = [links.core_swap(tie(beside[0], *fence))]
            far_f = own[0] + theirs_f
            got_f = links.y_swap(far_f)
            low_now = tie(low_two, far_f)
        if direct and i == 2:
            fence = (own[1], beside[1], got_f, swapped[0])
            beside[1] = tie(beside[1], *fence)
            swapped.append(links.core_swap(beside[1]))
            theirs_hidden = links.core_swap(tie(other[1], swapped[1]))
            ws = beside + swapped
        got = mlp(places, low_now, cotangent, small[name], base, rows8, ws, carried, middle if last else None)
        own.append(got[0])
        other.append(got[1])
        up_bias_grad.append(got[2])
        carried = got[3:5]
    block_out, grad_middle, branch, sums_two = got[3:7]

    def unit(name, group):
        return (w_projs[name], qkv[name], probs[name], group)

    if direct:
        seq = Sequence()
        branch = seq.fence(branch, theirs_hidden)
        rows = 2 * PIECE
        theirs_s = links.core_swap(seq(other[2]))
        send_f = seq.mark(cut_sum(x, rows, [(seq(own[1]), 0), (theirs_hidden, 0), (tie(got_f, branch), -x * rows)]))
        beside_f = links.x_swap(send_f)
        far_s = seq.mark(seq(own[2]) + theirs_s)
        got_s = links.y_swap(far_s)
        got = attention_backward(
            core_at,
            seq(branch),
            normed,
            [[unit(name, g) for g in range(2)] for name in ("rem", "loc")],
            [att["rem"], att["loc"]],
        )
        gqkv_a, bias_a, cols_a, theirs_a, rem_a, loc_a = got
        gqkv_a = seq.fence(gqkv_a, beside_f, got_s)
        theirs_a = links.core_swap(seq(theirs_a))

        def kept(at):
            start = (1 - x) * rows + at
            cut = [lax.dynamic_slice(t, (start, 0), (PIECE, width)) for t in (seq(own[1]), theirs_hidden)]
            cut = [t.astype(f32) for t in (*cut, got_s[at : at + PIECE], beside_f[at : at + PIECE])]
            return sum(cut[1:], cut[0]).astype(bf16)

        chain_0_value = seq.mark(kept(0))
        far_a = seq.mark(seq(rem_a) + theirs_a[0])
        got_a = links.y_swap(far_a)
        chain_0 = Chain(links, seq, seq(chain_0_value))
        chain_1_value = seq.mark(kept(PIECE))
        got = attention_backward(core_at, seq(branch), normed, [[unit(name, 2)] for name in ("rem", "loc")])
        gqkv_b, bias_b, cols_b, theirs_b, rem_b, loc_b = got
        gqkv_b = seq.fence(gqkv_b, chain_0.came, got_a)
        theirs_b = links.core_swap(seq(theirs_b))
        chain_0.next()
        chain_1 = Chain(links, seq, seq(chain_1_value))
        theirs_a = theirs_a.reshape(-1, theirs_a.shape[2])
        def along_x(loc, theirs, got):
            quarter = half // 2
            terms = [(seq(loc), 0), (theirs, half), (got, 0)]
            send = seq.mark(cut_sum(1 - x, quarter, terms))
            return Chain(links, seq, cut_sum(x, quarter, terms), links.x_swap(send))

        chain_a = along_x(loc_a, theirs_a, got_a)
        far_b = seq.mark(seq(rem_b) + theirs_b[0])
        got_b = links.y_swap(far_b)
        theirs_b = theirs_b.reshape(-1, theirs_b.shape[2])
        plan = ((0, 0, 1, 0, 768), (0, 768, 0, 0, 768), (1, 0, 1, 768, 384), (1, 384, 0, 768, 384))
        grad_tokens, sums_one = input_backward(
            plan, [gqkv_a, gqkv_b], [w_in["loc"], w_in["rem"]], tokens, grad_middle, seq(rows8)
        )
        sums_one = seq.fence(sums_one, chain_0.came, chain_1.came, chain_a.came, got_b)
        chain_a.next()
        bias_a, bias_b, cols_a, cols_b = [seq(v) for v in (bias_a, bias_b, cols_a, cols_b)]
        up_bias_grad = [seq(v) for v in up_bias_grad]

        chain_0.next()
        chain_1.next()
        chain_b = along_x(loc_b, theirs_b, got_b)

        def by_place(first, second):
            return jnp.where(core == 0, jnp.concatenate([first, second]), jnp.concatenate([second, first]))

        by_t = [jnp.where(x == t, up_bias_grad[0], up_bias_grad[2]) for t in range(2)]
        rem = [jnp.concatenate([grad[0, 0, at : at + PIECE] for grad in by_t]) for at in (0, PIECE)]
        bias_up_parts = [by_place(*rem), by_place(up_bias_grad[1][0, 0], up_bias_grad[1][1, 0])]

        def of_part(at):
            sums = [bias_a[:, at * 512 : (at + 1) * 512], bias_b[:, at * 256 : (at + 1) * 256]]
            cols = [cols_a[:, at * 256 : (at + 1) * 256], cols_b[:, at * 128 : (at + 1) * 128]]
            table = table_grad(onehot, jnp.concatenate(sums, axis=1))
            return [jnp.concatenate(cols, axis=1).reshape(-1), bias_up_parts[at], table.reshape(-1)]

        values = [sums_two.reshape(-1), sums_one.reshape(-1), *of_part(1), *of_part(0)]
        small_chain = SmallChain(links, seq, jnp.concatenate(values), 6 * width, small_size + bias_table.size)
        waves = (
            (chain_b, chain_a, chain_0, chain_1, small_chain),
            (chain_a, chain_b, chain_1, chain_0, small_chain),
            (chain_a, chain_1, chain_b, small_chain),
        )
        for wave in waves:
            for chain in wave:
                chain.next()
        pairs = [p for pair in zip(chain_0.pieces, chain_1.pieces) for p in pair]
        places = jnp.stack([2 * c + t for c in (core, 1 - core) for t in (1 - x, x)]).astype(jnp.int32)
        grad_down, grad_up = place_mlp(tie(places, seq.last), pairs, w_down.shape, w_up.shape)
        grad_down = seq.mark(grad_down)
        for chain in (chain_b, chain_a, small_chain, chain_b):
            chain.next()
        grad_qkv, grad_proj = place_two(links.order(), chain_a.pieces, chain_b.pieces, w_qkv.shape, w_proj.shape)
        got = small_chain.value
        two = got[: 4 * width].reshape(4, width)
        late = got[4 * width : 6 * width].reshape(2, width)
        got = got[6 * width :]
        cols = bias_query.shape[0]
        grad_query_b, grad_value_b = got[:cols], got[cols : 2 * cols]
        grad_up_bias = got[2 * cols : small_size]
        grad_table = got[small_size:].reshape(bias_table.shape)
    else:
        groups = tables["all"].shape[1] // GROUP
        got = attention_backward(core_at, branch, normed, [[unit("all", g) for g in range(groups)]])
        gqkv, bias_sums, col_sums, second_half, first_half = got
        grad_tokens, sums_one = input_backward(
            ((0, 0, 0, 0, gqkv.shape[1]),), [gqkv], [w_in["all"]], tokens, grad_middle, rows8
        )

        def summed(value, axis):
            value = lax.psum_scatter(value, "mp", scatter_dimension=axis, tiled=True)
            return lax.psum(value, "dp")

        hidden_grads = jnp.concatenate([own[0], other[0]]).reshape(-1, 2, PIECE, width)
        grad_down = summed(hidden_grads[:, 0].reshape(-1, width), 0).astype(f32)
        grad_up = summed(hidden_grads[:, 1].reshape(-1, width).T, 1).astype(f32)
        cols = gqkv.shape[1]
        grad_proj = summed(dot(att["all"], branch, TN).astype(bf16), 0).astype(f32)
        in_order = jnp.concatenate([first_half, second_half[0]], axis=0).reshape(-1, 384)
        natural = dot(in_order, group_order(), NT).reshape(width, cols).astype(bf16)
        grad_qkv = summed(natural, 1).astype(f32)
        grad_query_b = summed(col_sums[0], 0)
        grad_value_b = summed(col_sums[1], 0)
        grad_up_bias = summed(up_bias_grad[0].reshape(-1), 0)
        grad_table = summed(table_grad(onehot, bias_sums), 1)
        two, late = lax.psum((sums_two, sums_one), ("dp", "mp"))
    return (
        block_out[:real_rows],
        grad_tokens[:real_rows],
        late[0],
        late[1],
        grad_qkv,
        grad_query_b,
        grad_value_b,
        grad_table,
        grad_proj,
        two[2],
        two[0],
        two[1],
        grad_up,
        grad_up_bias,
        grad_down,
        two[3],
    )


def solution(mesh):
    direct = mesh.shape["dp"] == 16 and mesh.shape["mp"] == 2
    return jax.shard_map(
        functools.partial(on_device, direct),
        mesh=mesh,
        in_specs=(
            P(("dp", "mp"), None),
            P("dp"),
            P(),
            P(),
            P(),
            P(None, "mp"),
            P("mp"),
            P("mp"),
            P(None, "mp"),
            P("mp", None),
            P(),
            P(),
            P(),
            P(None, "mp"),
            P("mp"),
            P("mp", None),
            P(),
            P(("dp", "mp"), None),
        ),
        out_specs=(
            P(("dp", "mp"), None),
            P(("dp", "mp"), None),
            P(),
            P(),
            P(None, "mp"),
            P("mp"),
            P("mp"),
            P(None, "mp"),
            P("mp", None),
            P(),
            P(),
            P(),
            P(None, "mp"),
            P("mp"),
            P("mp", None),
            P(),
        ),
        check_vma=False,
    )
```

```python
import functools

import jax
import jax.numpy as jnp
from jax import lax
from jax.experimental import pallas as pl
from jax.experimental.pallas import tpu as pltpu
from jax.sharding import PartitionSpec as P

HEAD_DIM = 32
SLOTS = 49
PAD = 64
KEYS = 56
PIECE = 384
GROUP = 4
SPARE = 16
norm_eps = 1e-05
mask_fill = -1000000000.0
f32 = jnp.float32
bf16 = jnp.bfloat16
MIB = 1024 * 1024


def cost(micros):
    return pl.CostEstimate(flops=int(micros * 1.0e9), bytes_accessed=int(micros * 1.0e5), transcendentals=0)


def params(limit=56):
    return pltpu.CompilerParams(vmem_limit_bytes=limit * MIB)


def whole(shape):
    return pl.BlockSpec(shape, lambda *_: (0,) * len(shape))


def dot(left, right, dims=((1,), (0,))):
    return lax.dot_general(left, right, (dims, ((), ())), preferred_element_type=f32)


NT = ((1,), (1,))
TN = ((0,), (0,))


def norm_parts(values):
    mean = jnp.mean(values, axis=-1, keepdims=True)
    centred = values - mean
    spread = jnp.mean(centred * centred, axis=-1, keepdims=True)
    return centred, lax.rsqrt(spread + norm_eps)


def norm_back(values, gain, grad):
    centred, inverse = norm_parts(values)
    unit = centred * inverse
    scaled = grad * gain
    first = jnp.mean(scaled, axis=-1, keepdims=True)
    second = jnp.mean(scaled * unit, axis=-1, keepdims=True)
    return inverse * (scaled - first - unit * second), grad * unit


def col_sum(values):
    return jnp.sum(values, axis=0, keepdims=True)


def row_blocks(rows):
    size = 256 if rows % 16 == 0 else rows
    starts = list(range(0, rows, size))
    if len(starts) > 1 and rows - starts[-1] < 128:
        starts.pop()
    return [(s, (starts[i + 1] if i + 1 < len(starts) else rows) - s) for i, s in enumerate(starts)]


def diagonal(rows_of_heads):
    lane = lax.broadcasted_iota(jnp.int32, (PAD, 128), 1)
    out = rows_of_heads[3 * PAD :]
    for head in (2, 1, 0):
        out = jnp.where(lane < (head + 1) * HEAD_DIM, rows_of_heads[head * PAD : (head + 1) * PAD], out)
    return out


def spread(rows, block_mask):
    return jnp.concatenate([rows] * GROUP, axis=0) * block_mask


def block_mask_of():
    row = lax.broadcasted_iota(jnp.int32, (GROUP * PAD, 128), 0) // PAD
    lane = lax.broadcasted_iota(jnp.int32, (GROUP * PAD, 128), 1) // HEAD_DIM
    return (row == lane).astype(f32).astype(bf16)


def window_rows_mask(rows, cols):
    return lax.rem(lax.broadcasted_iota(jnp.int32, (rows, cols), 0), PAD) < SLOTS


def batch_of(windows):
    return 8 if windows % 8 == 0 else windows


def step_rows(ref, step, batch):
    if batch % 8:
        return ref
    return ref.at[pl.ds(pl.multiple_of(step * batch * SLOTS, 8), batch * SLOTS + SPARE)]


def pad_windows(src, dst, step, batch):
    view = step_rows(src, step, batch)
    for j in range(batch):
        dst[j * PAD : (j + 1) * PAD, :] = view[j * SLOTS : j * SLOTS + PAD, :].astype(bf16)


def fwd_kernel(groups, pieces, places, tokens, rows8, small, pos, mask, *refs):
    ws, refs = refs[: max(pieces, 1)], refs[max(pieces, 1) :]
    qkv, probs, att, wp, padded = refs[:5]
    normed, att_s, pos_s = refs[-3:]
    step = pl.program_id(0)
    rows = tokens.shape[0]

    @pl.when(step == 0)
    def _():
        centred, inverse = norm_parts(tokens[...].astype(f32))
        value = (centred * inverse * rows8[0:1, :] + rows8[1:2, :]).astype(bf16)
        normed[0:rows, :] = value.astype(f32)
        normed[rows:, :] = jnp.zeros_like(normed[rows:, :])
        order = group_order()
        for r, w in enumerate(ws):
            if pieces:
                size = w.shape[0]
                at = pl.ds(pl.multiple_of(places[r] * size, 16), size)
            else:
                at = slice(0, w.shape[0])
            for g in range(groups):
                cols = slice(g * 384, (g + 1) * 384)
                wp[at, cols] = dot(w[:, cols], order).astype(bf16)
        slot = lax.broadcasted_iota(jnp.int32, (KEYS, 128), 0) < SLOTS
        for h in range(0, groups * GROUP, 2):
            both = jnp.concatenate([pos[h], pos[h + 1]], axis=1)
            pos_s[:, h * PAD : (h + 2) * PAD] = jnp.where(slot, both, 2 * mask_fill)

    batch = mask.shape[0]
    pad_windows(normed, padded, step, batch)
    att_view = step_rows(att_s, step, batch)
    block_mask = block_mask_of()
    keep = window_rows_mask(batch * PAD, 128)
    left = padded[...]
    for g in range(groups):
        value = dot(left, wp[:, g * 384 : (g + 1) * 384])
        for part, bias in enumerate((small[g], None, small[groups + g])):
            piece = value[:, part * 128 : (part + 1) * 128]
            if bias is not None:
                piece = piece + bias
            qkv[:, g * 384 + part * 128 : g * 384 + (part + 1) * 128] = jnp.where(keep, piece, 0.0).astype(bf16)
    for j in range(batch):
        rows_at = slice(j * PAD, (j + 1) * PAD)
        allowed = mask[j] > 0.0
        allowed = jnp.concatenate([allowed, allowed], axis=1)
        for g in range(groups):
            at = g * 384
            query = qkv[rows_at, at : at + 128]
            key = qkv[rows_at, at + 128 : at + 256]
            value = qkv[rows_at, at + 256 : at + 384]
            raw = dot(key, spread(query, block_mask), NT)[:KEYS]
            scores = raw * HEAD_DIM ** (-0.5) + pos_s[:, g * 256 : (g + 1) * 256]
            scores = jnp.where(allowed, scores, mask_fill)
            top = jnp.max(scores, axis=0, keepdims=True)
            power = jnp.exp(scores - top)
            total = jnp.sum(power, axis=0, keepdims=True)
            prob = power * (1.0 / total)
            prob = jnp.concatenate([prob, jnp.zeros((PAD - KEYS, 256), f32)], axis=0).astype(bf16)
            probs[j, :, g * 256 : (g + 1) * 256] = prob
            out = diagonal(dot(prob, value, TN))
            att_view[j * SLOTS : j * SLOTS + KEYS, g * 128 : (g + 1) * 128] = out[:KEYS]

    @pl.when(step == pl.num_programs(0) - 1)
    def _():
        windows = pl.num_programs(0) * batch
        value = att_s[0:rows, :]
        real = lax.broadcasted_iota(jnp.int32, value.shape, 0) < windows * SLOTS
        att[...] = jnp.where(real, value, 0.0).astype(bf16)


def attention_forward(places, tokens, rows8, small, pos, mask, ws):
    rows, width = tokens.shape
    windows = mask.shape[0]
    pieces = len(ws) if len(ws) > 1 else 0
    heads = pos.shape[0]
    groups = heads // GROUP
    cols = groups * 384
    batch = batch_of(windows)
    steps = windows // batch
    quad_rows = batch * PAD
    out_shape = [
        jax.ShapeDtypeStruct((windows * PAD, cols), bf16),
        jax.ShapeDtypeStruct((windows, PAD, heads * PAD), bf16),
        jax.ShapeDtypeStruct((rows, heads * HEAD_DIM), bf16),
        jax.ShapeDtypeStruct((width, cols), bf16),
        jax.ShapeDtypeStruct((windows * PAD, width), bf16),
    ]
    out_specs = [
        pl.BlockSpec((quad_rows, cols), lambda i, s: (i, 0)),
        pl.BlockSpec((batch, PAD, heads * PAD), lambda i, s: (i, 0, 0)),
        whole((rows, heads * HEAD_DIM)),
        whole((width, cols)),
        pl.BlockSpec((quad_rows, width), lambda i, s: (i, 0)),
    ]
    return pl.pallas_call(
        functools.partial(fwd_kernel, groups, pieces),
        grid_spec=pltpu.PrefetchScalarGridSpec(
            num_scalar_prefetch=1,
            grid=(steps,),
            in_specs=[
                whole((rows, width)),
                whole(rows8.shape),
                whole(small.shape),
                whole(pos.shape),
                pl.BlockSpec((batch, KEYS, 128), lambda i, s: (i, 0, 0)),
            ]
            + [whole(w.shape) for w in ws],
            out_specs=out_specs,
            scratch_shapes=[
                pltpu.VMEM((rows + SPARE, width), f32),
                pltpu.VMEM((rows + SPARE, heads * HEAD_DIM), f32),
                pltpu.VMEM((KEYS, heads * PAD), f32),
            ],
        ),
        out_shape=tuple(out_shape),
        compiler_params=params(),
        cost_estimate=cost(11 * groups / 3),
        name="attention_forward",
    )(places, tokens, rows8, small, pos, mask, *ws)


def proj_kernel(parts, pieces, places, *refs):
    atts, ws = refs[:parts], list(refs[parts : 2 * parts - (1 if pieces else 0)])
    refs = refs[parts + len(ws) :]
    tokens, rows8, middle, low = refs[pieces : pieces + 4]
    if pieces:
        joined = refs[pieces + 4]
        for r, piece in enumerate(refs[:pieces]):
            size = piece.shape[1]
            joined[:, pl.ds(pl.multiple_of(places[r] * size, 128), size)] = piece[...]
        ws.append(joined)
    for start, size in row_blocks(tokens.shape[0]):
        at = slice(start, start + size)
        value = tokens[at, :].astype(f32) + rows8[2:3, :]
        for a, w in zip(atts, ws):
            value = value + dot(a[at, :], w[...])
        middle[at, :] = value
        centred, inverse = norm_parts(value)
        low[at, :] = (centred * inverse * rows8[3:4, :] + rows8[4:5, :]).astype(bf16)


def project(places, atts, ws, pieces, tokens, rows8):
    rows, width = tokens.shape
    ins = [*atts, *ws, *pieces, tokens, rows8]
    out_shape = [jax.ShapeDtypeStruct((rows, width), f32), jax.ShapeDtypeStruct((rows, width), bf16)]
    if pieces:
        out_shape.append(jax.ShapeDtypeStruct((pieces[0].shape[0], width), bf16))
    return pl.pallas_call(
        functools.partial(proj_kernel, len(atts), len(pieces)),
        grid_spec=pltpu.PrefetchScalarGridSpec(
            num_scalar_prefetch=1,
            grid=(1,),
            in_specs=[whole(v.shape) for v in ins],
            out_specs=[whole(o.shape) for o in out_shape],
        ),
        out_shape=tuple(out_shape),
        compiler_params=params(),
        cost_estimate=cost(5),
        name="project",
    )(places, *ins)


def gelu_parts(x):
    z = jnp.abs(x) * 0.7071067811865476
    t = 1.0 / (1.0 + 0.3275911 * z)
    e = jnp.exp(-z * z)
    half = t * (0.127414796 + t * (-0.142248368 + t * (0.7107068705 + t * (-0.7265760135 + t * 0.5307027145)))) * e
    cdf = jnp.where(x >= 0.0, 1.0 - half, half)
    return cdf, e * 0.3989422804014327


def mlp_kernel(first, last, held_pieces, base, order, *refs):
    low, dy, small, rows8 = refs[:4]
    ws, refs = refs[4 : 8 if held_pieces else 6], refs[8 if held_pieces else 6 :]
    if not first:
        out_in, two_in = refs[:2]
        refs = refs[2:]
    if last:
        middle, own, other, gbias, block_out, grad_middle, branch, sums = refs[:8]
        acc_out, acc_two, hid_s, gp_s = refs[8:12]
        refs = refs[12:]
    else:
        own, other, gbias, acc_out, acc_two, hid_s, gp_s = refs[:7]
        refs = refs[7:]
    step = pl.program_id(0)
    rows = low.shape[0]
    copies, carry = [], []
    if not first:
        *refs, carry_sems = refs
        carry = [
            pltpu.make_async_copy(out_in, acc_out, carry_sems.at[0]),
            pltpu.make_async_copy(two_in, acc_two, carry_sems.at[1]),
        ]
    if held_pieces:
        held, sems = refs
        for i, w in enumerate(ws):
            r, k = i // 2, i % 2
            copies.append(pltpu.make_async_copy(w, held.at[k, r * PIECE : (r + 1) * PIECE], sems.at[i]))
        for copy in copies:
            copy.start()
        up, down = held.at[0], held.at[1]
        up_dims, back_dims = NT, ((1,), (0,))
    else:
        up, down = ws
        up_dims, back_dims = ((1,), (0,)), NT

    @pl.when(step == 0)
    def _():
        if first:
            acc_out[...] = jnp.zeros_like(acc_out)
            acc_two[...] = jnp.zeros_like(acc_two)
        for copy in carry:
            copy.start()

    for copy in copies[0::2]:
        copy.wait()
    bias = [small[base + 3 * order[2 * step + t // 3] + t % 3] for t in range(6)]
    bias = jnp.concatenate(bias, axis=1)
    total = jnp.zeros(bias.shape, f32)
    for start, size in row_blocks(rows):
        at = slice(start, start + size)
        pre = dot(low[at, :], up[...], up_dims) + bias
        if start == 0:
            for copy in copies[1::2]:
                copy.wait()
        back = dot(dy[at, :], down[...], NT)
        cdf, pdf = gelu_parts(pre)
        hid = (pre * cdf).astype(bf16)
        gp = (back * (cdf + pre * pdf)).astype(bf16)
        hid_s[at, :] = hid
        gp_s[at, :] = gp
        total = total + col_sum(gp.astype(f32))
        if start == 0:

            @pl.when(step == 0)
            def _():
                for copy in carry:
                    copy.wait()

        acc_out[at, :] += dot(hid, down[...])
        acc_two[at, :] += dot(gp, up[...], back_dims)
    gbias[0] = total

    def weight_rows(out, at, piece):
        cols = slice(piece * PIECE, (piece + 1) * PIECE)
        out[at : at + PIECE, :] = dot(hid_s[:, cols], dy[...], TN).astype(bf16)
        out[at + PIECE : at + 2 * PIECE, :] = dot(gp_s[:, cols], low[...], TN).astype(bf16)

    if held_pieces:
        weight_rows(own, 0, 0)
        weight_rows(other, 0, 1)
    else:
        for out, now in ((own, step < pl.num_programs(0) // 2), (other, step >= pl.num_programs(0) // 2)):

            @pl.when(now)
            def _(out=out):
                for t in range(2):
                    weight_rows(out, 2 * t * PIECE, t)

    if last:

        @pl.when(step == pl.num_programs(0) - 1)
        def _():
            s_gain = s_shift = s_branch = s_down = jnp.zeros((1, low.shape[1]), f32)
            for start, size in row_blocks(rows):
                at = slice(start, start + size)
                mid = middle[at, :]
                block_out[at, :] = (mid + acc_out[at, :] + rows8[5:6, :]).astype(bf16)
                two = acc_two[at, :]
                up_grad = dy[at, :].astype(f32)
                grad, for_gain = norm_back(mid, rows8[3:4, :], two)
                grad = grad + up_grad
                grad_middle[at, :] = grad
                low_grad = grad.astype(bf16)
                branch[at, :] = low_grad
                s_gain += col_sum(for_gain)
                s_shift += col_sum(two)
                s_branch += col_sum(low_grad.astype(f32))
                s_down += col_sum(up_grad)
            sums[...] = jnp.concatenate([s_gain, s_shift, s_branch, s_down], axis=0)


def mlp(order, low, dy, small, base, rows8, ws, carried=None, middle=None):
    rows, width = low.shape
    held = isinstance(ws, list)
    units = 2 * PIECE if held else ws[1].shape[0]
    steps = units // (2 * PIECE)
    first, last = carried is None, middle is not None
    ins = [low, dy, small, rows8, *ws]
    specs = [whole((rows, width)), whole((rows, width)), whole(small.shape), whole(rows8.shape)]
    if held:
        specs += [pl.BlockSpec(memory_space=pl.ANY)] * 4
        grads = [jax.ShapeDtypeStruct((2 * PIECE, width), bf16)] * 2
        grad_specs = [whole((2 * PIECE, width))] * 2
    else:
        specs += [
            pl.BlockSpec((width, 2 * PIECE), lambda i, o: (0, o[2 * i] // 2)),
            pl.BlockSpec((2 * PIECE, width), lambda i, o: (o[2 * i] // 2, 0)),
        ]
        many = steps // 2
        grads = [jax.ShapeDtypeStruct((many * 4 * PIECE, width), bf16)] * 2
        grad_specs = [
            pl.BlockSpec((4 * PIECE, width), lambda i, o: (jnp.minimum(i, many - 1), 0)),
            pl.BlockSpec((4 * PIECE, width), lambda i, o: (jnp.maximum(i - many, 0), 0)),
        ]
    outs = [*grads, jax.ShapeDtypeStruct((steps, 1, 2 * PIECE), f32)]
    out_specs = [*grad_specs, pl.BlockSpec((1, 1, 2 * PIECE), lambda i, o: (i, 0, 0))]
    scratch = []
    if not first:
        ins += list(carried)
        specs += [pl.BlockSpec(memory_space=pl.ANY)] * 2
    if last:
        ins.append(middle)
        specs.append(whole((rows, width)))
        outs += [
            jax.ShapeDtypeStruct((rows, width), bf16),
            jax.ShapeDtypeStruct((rows, width), f32),
            jax.ShapeDtypeStruct((rows, width), bf16),
            jax.ShapeDtypeStruct((4, width), f32),
        ]
        out_specs += [whole((rows, width))] * 3 + [whole((4, width))]
        scratch = [pltpu.VMEM((rows, width), f32)] * 2
    else:
        outs += [jax.ShapeDtypeStruct((rows, width), f32)] * 2
        out_specs += [whole((rows, width))] * 2
    scratch += [pltpu.VMEM((rows, 2 * PIECE), bf16)] * 2
    if held:
        scratch += [pltpu.VMEM((2, 2 * PIECE, width), bf16), pltpu.SemaphoreType.DMA((4,))]
    if not first:
        scratch.append(pltpu.SemaphoreType.DMA((2,)))
    return pl.pallas_call(
        functools.partial(mlp_kernel, first, last, held, base),
        grid_spec=pltpu.PrefetchScalarGridSpec(
            num_scalar_prefetch=1, grid=(steps,), in_specs=specs, out_specs=out_specs, scratch_shapes=scratch
        ),
        out_shape=tuple(outs),
        compiler_params=params(),
        cost_estimate=cost(11 * steps),
        name="mlp",
    )(order, *ins)


def bwd_kernel(parts, each, with_proj, core, branch, normed, *refs):
    units = parts * each
    atts, refs = refs[: parts * with_proj], refs[parts * with_proj :]
    wprojs, qkvs, probs = refs[:units], refs[units : 2 * units], refs[2 * units : 3 * units]
    gqkv, bias_sum, col_sums, theirs = refs[3 * units : 3 * units + 4]
    mine, (wide, padded, wcat, total) = refs[3 * units + 4 : -4], refs[-4:]
    step = pl.program_id(0)
    rows = branch.shape[0]
    half = normed.shape[1] // 2

    @pl.when(step == 0)
    def _():
        wide[0:rows, :] = branch[...].astype(f32)
        wide[rows:, :] = jnp.zeros_like(wide[rows:, :])
        bias_sum[...] = jnp.zeros_like(bias_sum)
        col_sums[...] = jnp.zeros_like(col_sums)
        for u in range(units):
            wcat[u * 128 : (u + 1) * 128, :] = wprojs[u][...]
        if with_proj:
            for out_at, place in ((mine, core[0]), (None, 1 - core[0])):
                right = branch[:, pl.ds(pl.multiple_of(place * half, 128), half)]
                for p in range(parts):
                    value = dot(atts[p][...], right, TN).astype(bf16)
                    if out_at is None:
                        theirs[p, :, each * 384 :] = value
                    else:
                        mine[p][:, each * 384 :] = value

    batch = probs[0].shape[0]
    pad_windows(wide, padded, step, batch)
    block_mask = block_mask_of()
    scale = HEAD_DIM ** (-0.5)
    grads = dot(padded[...], wcat[...], NT)
    grads = jnp.where(window_rows_mask(batch * PAD, grads.shape[1]), grads, 0.0).astype(bf16)
    for u in range(units):
        qkv, at = qkvs[u], u * 384
        bias_total = jnp.zeros((KEYS, 256), f32)
        col_total = [jnp.zeros((1, 128), f32)] * 2
        for j in range(batch):
            rows_at = slice(j * PAD, (j + 1) * PAD)
            query = qkv[rows_at, 0:128]
            key = qkv[rows_at, 128:256]
            value = qkv[rows_at, 256:384]
            prob_low = probs[u][j]
            grad = spread(grads[rows_at, u * 128 : (u + 1) * 128], block_mask)
            prob = prob_low.astype(f32)[:KEYS]
            prob_grad = dot(value, grad, NT)[:KEYS]
            both = prob * prob_grad
            score_grad = both - prob * jnp.sum(both, axis=0, keepdims=True)
            score_grad = jnp.concatenate([score_grad, jnp.zeros((PAD - KEYS, 256), f32)], axis=0).astype(bf16)
            bias_total = bias_total + score_grad.astype(f32)[:KEYS]
            grad_value = dot(prob_low, grad).astype(bf16)
            grad_key = (dot(score_grad, spread(query, block_mask)) * scale).astype(bf16)
            grad_query = (diagonal(dot(score_grad, key, TN)) * scale).astype(bf16)
            gqkv[rows_at, at : at + 128] = grad_query
            gqkv[rows_at, at + 128 : at + 256] = grad_key
            gqkv[rows_at, at + 256 : at + 384] = grad_value
            col_total[0] = col_total[0] + col_sum(grad_query.astype(f32))
            col_total[1] = col_total[1] + col_sum(grad_value.astype(f32))
        bias_sum[:, u * 256 : (u + 1) * 256] += bias_total
        col_sums[0:1, u * 128 : (u + 1) * 128] += col_total[0]
        col_sums[1:2, u * 128 : (u + 1) * 128] += col_total[1]
    grad = dot(normed[...], gqkv[...], TN)

    @pl.when(step == 0)
    def _():
        total[...] = grad

    @pl.when(step > 0)
    def _():
        total[...] += grad

    @pl.when(step == pl.num_programs(0) - 1)
    def _():
        for p in range(parts):
            cols = slice(p * each * 384, (p + 1) * each * 384)
            mine[p][:, 0 : each * 384] = total[pl.ds(pl.multiple_of(core[0] * half, 16), half), cols].astype(bf16)
            other = pl.ds(pl.multiple_of((1 - core[0]) * half, 16), half)
            theirs[p, :, 0 : each * 384] = total[other, cols].astype(bf16)


def attention_backward(core, branch, normed, parts, atts=()):
    rows, width = branch.shape
    units = [u for part in parts for u in part]
    windows = units[0][2].shape[0]
    count, each = len(units), len(parts[0])
    batch = batch_of(windows)
    quad_rows = batch * PAD
    half = (width // 2, each * 384 + (width // 2 if atts else 0))
    in_specs = [whole((rows, width)), pl.BlockSpec((quad_rows, width), lambda i, s: (i, 0))]
    in_specs += [whole(a.shape) for a in atts]
    in_specs += [pl.BlockSpec((128, width), lambda i, s, g=g: (g, 0)) for _, _, _, g in units]
    in_specs += [pl.BlockSpec((quad_rows, 384), lambda i, s, g=g: (i, g)) for _, _, _, g in units]
    in_specs += [pl.BlockSpec((batch, PAD, 256), lambda i, s, g=g: (i, 0, g)) for _, _, _, g in units]
    return pl.pallas_call(
        functools.partial(bwd_kernel, len(parts), each, 1 if atts else 0),
        grid_spec=pltpu.PrefetchScalarGridSpec(
            num_scalar_prefetch=1,
            grid=(windows // batch,),
            in_specs=in_specs,
            out_specs=[
                pl.BlockSpec((quad_rows, count * 384), lambda i, s: (i, 0)),
                whole((KEYS, count * 256)),
                whole((2, count * 128)),
                whole((len(parts), *half)),
            ]
            + [whole(half)] * len(parts),
            scratch_shapes=[
                pltpu.VMEM((rows + SPARE, width), f32),
                pltpu.VMEM((quad_rows, width), bf16),
                pltpu.VMEM((count * 128, width), bf16),
                pltpu.VMEM((width, count * 384), f32),
            ],
        ),
        out_shape=(
            jax.ShapeDtypeStruct((windows * PAD, count * 384), bf16),
            jax.ShapeDtypeStruct((KEYS, count * 256), f32),
            jax.ShapeDtypeStruct((2, count * 128), f32),
            jax.ShapeDtypeStruct((len(parts), *half), bf16),
        )
        + (jax.ShapeDtypeStruct(half, bf16),) * len(parts),
        compiler_params=params(),
        cost_estimate=cost(5 * count),
        name="attention_backward",
    )(core, branch, normed, *atts, *[u[0] for u in units], *[u[1] for u in units], *[u[2] for u in units])


def input_kernel(plan, arrays, *refs):
    gqkvs, refs = refs[:arrays], refs[arrays:]
    ws, refs = refs[: -6], refs[-6:]
    tokens, grad_middle, rows8, grad_tokens, sums, compact = refs
    step = pl.program_id(0)
    total = None
    for a, a_at, w, w_at, size in plan:
        term = dot(gqkvs[a][:, a_at : a_at + size], ws[w][:, w_at : w_at + size], NT)
        total = term if total is None else total + term
    batch = total.shape[0] // PAD
    view = step_rows(compact, step, batch)
    for j in range(batch):
        view[j * SLOTS : j * SLOTS + KEYS, :] = total[j * PAD : j * PAD + KEYS]

    @pl.when(step == pl.num_programs(0) - 1)
    def _():
        rows = tokens.shape[0]
        windows = pl.num_programs(0) * batch
        s_gain = s_shift = jnp.zeros((1, tokens.shape[1]), f32)
        for start, size in row_blocks(rows):
            at = slice(start, start + size)
            one = compact[at, :]
            if start + size == rows:
                real = start + lax.broadcasted_iota(jnp.int32, one.shape, 0) < windows * SLOTS
                one = jnp.where(real, one, 0.0)
            grad, for_gain = norm_back(tokens[at, :].astype(f32), rows8[0:1, :], one)
            grad_tokens[at, :] = (grad_middle[at, :] + grad).astype(bf16)
            s_gain += col_sum(for_gain)
            s_shift += col_sum(one)
        sums[...] = jnp.concatenate([s_gain, s_shift], axis=0)


def input_backward(plan, gqkvs, ws, tokens, grad_middle, rows8):
    rows, width = tokens.shape
    quad_rows = batch_of(gqkvs[0].shape[0] // PAD) * PAD
    steps = gqkvs[0].shape[0] // quad_rows
    return pl.pallas_call(
        functools.partial(input_kernel, plan, len(gqkvs)),
        grid=(steps,),
        in_specs=[pl.BlockSpec((quad_rows, a.shape[1]), lambda i: (i, 0)) for a in gqkvs]
        + [whole(w.shape) for w in ws]
        + [whole((rows, width)), whole((rows, width)), whole(rows8.shape)],
        out_specs=[whole((rows, width)), whole((2, width))],
        out_shape=(jax.ShapeDtypeStruct((rows, width), bf16), jax.ShapeDtypeStruct((2, width), f32)),
        scratch_shapes=[pltpu.VMEM((rows + SPARE, width), f32)],
        compiler_params=params(),
        cost_estimate=cost(11),
        name="input_backward",
    )(*gqkvs, *ws, tokens, grad_middle, rows8)


def stack_kernel(count, *refs):
    rows8, small = refs[-2:]
    rows8[...] = jnp.zeros_like(rows8)
    for i, ref in enumerate(refs[:count]):
        rows8[i : i + 1, :] = ref[...].astype(f32).reshape(1, -1)
    at = 0
    for ref in refs[count:-2]:
        value = ref[...].astype(f32)
        for start in range(0, ref.shape[0], 128):
            small[at] = value[start : start + 128].reshape(1, 128)
            at += 1


def stack_rows(vectors, others):
    count = sum(v.shape[0] for v in others) // 128
    return pl.pallas_call(
        functools.partial(stack_kernel, len(vectors)),
        out_shape=(
            jax.ShapeDtypeStruct((8, vectors[0].shape[0]), f32),
            jax.ShapeDtypeStruct((count, 1, 128), f32),
        ),
        cost_estimate=cost(1),
        name="stack_rows",
    )(*vectors, *others)


def pack_kernel(core, source, out):
    out[...] = source[...]


def pack_half(core, weight, axis):
    out = tuple(n // 2 if i == axis else n for i, n in enumerate(weight.shape))
    return pl.pallas_call(
        pack_kernel,
        grid_spec=pltpu.PrefetchScalarGridSpec(
            num_scalar_prefetch=1,
            grid=(1,),
            in_specs=[pl.BlockSpec(out, lambda i, s: (s[0], 0) if axis == 0 else (0, s[0]))],
            out_specs=whole(out),
        ),
        out_shape=jax.ShapeDtypeStruct(out, weight.dtype),
        compiler_params=params(16),
        cost_estimate=cost(2),
        name="pack_half",
    )(core, weight)


def pack_piece_kernel(place, up, down, up_out, down_out):
    up_out[...] = up[...].astype(f32).T.astype(bf16)
    down_out[...] = down[...]


def pack_piece(place, w_up, w_down):
    width = w_up.shape[0]
    return pl.pallas_call(
        pack_piece_kernel,
        grid_spec=pltpu.PrefetchScalarGridSpec(
            num_scalar_prefetch=1,
            grid=(1,),
            in_specs=[
                pl.BlockSpec((width, PIECE), lambda i, s: (0, s[0])),
                pl.BlockSpec((PIECE, width), lambda i, s: (s[0], 0)),
            ],
            out_specs=[whole((PIECE, width))] * 2,
        ),
        out_shape=(jax.ShapeDtypeStruct((PIECE, width), bf16),) * 2,
        compiler_params=params(32),
        cost_estimate=cost(3),
        name="pack_piece",
    )(place, w_up, w_down)


def group_order():
    at = lax.broadcasted_iota(jnp.int32, (384, 384), 1)
    source = (at % 128) // 32 * 96 + at // 128 * 32 + at % 32
    return (lax.broadcasted_iota(jnp.int32, (384, 384), 0) == source).astype(f32).astype(bf16)


def place_mlp_kernel(places, *refs):
    step = pl.program_id(0)
    grad_down, grad_up = refs[-2:]
    for i in range(4):

        @pl.when(step == i)
        def _(down=refs[2 * i], up=refs[2 * i + 1]):
            grad_down[...] = down[...].astype(f32)
            grad_up[...] = up[...].astype(f32).T


def place_mlp(places, pieces, down_shape, up_shape):
    size = pieces[0].shape[0]
    return pl.pallas_call(
        place_mlp_kernel,
        grid_spec=pltpu.PrefetchScalarGridSpec(
            num_scalar_prefetch=1,
            grid=(4,),
            in_specs=[whole(p.shape) for p in pieces],
            out_specs=[
                pl.BlockSpec((size, down_shape[1]), lambda i, s: (s[i], 0)),
                pl.BlockSpec((up_shape[0], size), lambda i, s: (0, s[i])),
            ],
        ),
        out_shape=(jax.ShapeDtypeStruct(down_shape, f32), jax.ShapeDtypeStruct(up_shape, f32)),
        compiler_params=params(),
        cost_estimate=cost(8),
        name="place_mlp",
    )(places, *pieces)


def place_two_kernel(places, *refs):
    step = pl.program_id(0)
    grad_qkv, grad_proj = refs[-2:]
    for i in range(4):

        @pl.when(step == i)
        def _(first=refs[2 * i], second=refs[2 * i + 1]):
            order = group_order()
            grad_qkv[:, 0:384] = dot(first[:, 0:384], order, NT)
            grad_qkv[:, 384:768] = dot(first[:, 384:768], order, NT)
            grad_qkv[:, 768:1152] = dot(second[...], order, NT)
            grad_proj[...] = first[:, 768:1152].astype(f32)


def place_two(places, firsts, seconds, qkv_shape, proj_shape):
    pieces = [p for pair in zip(firsts, seconds) for p in pair]
    rows = firsts[0].shape[0]
    return pl.pallas_call(
        place_two_kernel,
        grid_spec=pltpu.PrefetchScalarGridSpec(
            num_scalar_prefetch=1,
            grid=(4,),
            in_specs=[whole(p.shape) for p in pieces],
            out_specs=[
                pl.BlockSpec((rows, qkv_shape[1]), lambda i, s: (s[i], 0)),
                pl.BlockSpec((rows, proj_shape[1] // 2), lambda i, s: (s[i] % 2, s[i] // 2)),
            ],
        ),
        out_shape=(jax.ShapeDtypeStruct(qkv_shape, f32), jax.ShapeDtypeStruct(proj_shape, f32)),
        compiler_params=params(),
        cost_estimate=cost(5),
        name="place_two",
    )(places, *pieces)


def pair_onehot(rel_index, table_rows):
    turned_index = jnp.pad(rel_index.T, ((0, KEYS - SLOTS), (0, PAD - SLOTS)), constant_values=-1)
    offsets = jnp.arange(table_rows, dtype=jnp.int32)
    return (turned_index[None] == offsets[:, None, None]).astype(bf16)


def position_rows(onehot, table):
    return dot(table, onehot.reshape(onehot.shape[0], KEYS * PAD), TN).reshape(table.shape[1], KEYS, PAD)


def table_grad(onehot, sums):
    rows = onehot.shape[0]
    heads = sums.shape[1] // PAD
    flat = jnp.transpose(sums.reshape(KEYS, heads, PAD), (0, 2, 1)).reshape(KEYS * PAD, heads)
    high = flat.astype(bf16)
    rest = (flat - high.astype(f32)).astype(bf16)
    low = (flat - high.astype(f32) - rest.astype(f32)).astype(bf16)
    both = dot(onehot.reshape(rows, KEYS * PAD), jnp.concatenate([high, rest, low], axis=1))
    return both[:, :heads] + both[:, heads : 2 * heads] + both[:, 2 * heads :]


def window_mask(labels):
    shaped = labels.reshape(-1, SLOTS)
    keys = jnp.pad(shaped, ((0, 0), (0, KEYS - SLOTS)), constant_values=-2)[:, :, None]
    queries = jnp.pad(shaped, ((0, 0), (0, PAD - SLOTS)), constant_values=-3)
    queries = jnp.concatenate([queries, queries], axis=1)[:, None, :]
    key_at = jnp.arange(KEYS)[None, :, None]
    query_at = (jnp.arange(128) % PAD)[None, None, :]
    allowed = (keys == queries) & ((keys >= 0) | (key_at == query_at))
    outside = (key_at >= SLOTS) | (query_at >= SLOTS)
    return (allowed | outside).astype(f32)


class Links:
    def __init__(self):
        at = lax.axis_index("dp")
        self.core = at % 2
        self.x = at // 2 % 2
        self.z = at // 4
        self.inner = (self.z == 1) | (self.z == 2)

    def y_swap(self, value):
        return lax.ppermute(value, "mp", [(0, 1), (1, 0)])

    def flip(self, value, bit):
        return lax.ppermute(value, "dp", [(i, i ^ bit) for i in range(16)])

    def core_swap(self, value):
        return self.flip(value, 1)

    def x_swap(self, value):
        return self.flip(value, 2)

    def z_pairs(self, value):
        return self.flip(value, 4)

    def z_all(self, value):
        return [self.flip(value, 4), self.flip(value, 8), self.flip(value, 12)]

    def z_total(self, value, others):
        pair, far = value.astype(f32) + others[0].astype(f32), others[1].astype(f32) + others[2].astype(f32)
        return (pair + far).astype(value.dtype)

    def z_move(self, value, pairs):
        return lax.ppermute(value, "dp", [(s * 4 + i, d * 4 + i) for s, d in pairs for i in range(4)])

    def z_sum(self, value):
        value = value + self.z_move(value, [(0, 1), (3, 2)])
        value = value + self.z_move(value, [(1, 2), (2, 1)])
        return jnp.where(self.inner, value, self.z_move(value, [(1, 0), (2, 3)]))

    def order(self):
        places = [2 * (self.core ^ (r >> 1)) + (self.x ^ (r & 1)) for r in range(4)]
        return jnp.stack(places).astype(jnp.int32)


def tie(value, *others):
    return lax.optimization_barrier((value, *others))[0]


class Sequence:
    def __init__(self):
        self.last = None

    def __call__(self, value):
        return value if self.last is None else tie(value, self.last)

    def mark(self, value):
        self.last = value
        return value

    def fence(self, value, *others):
        return self.mark(tie(value, *others))


def cut_sum(place, rows, terms):
    cut = [lax.dynamic_slice(t, (start + place * rows, 0), (rows, t.shape[1])).astype(f32) for t, start in terms]
    return sum(cut[1:], cut[0]).astype(bf16)


class Chain:
    def __init__(self, links, seq, value, came=None):
        self.links, self.seq, self.value, self.came = links, seq, value, came
        self.step = 0
        if came is None:
            self.came = links.z_move(seq.mark(value), [(0, 1), (3, 2)])
            self.step = 1

    def next(self):
        links, seq = self.links, self.seq
        pairs = ([(0, 1), (3, 2)], [(1, 2), (2, 1)], [(1, 0), (2, 3)])
        if self.step < 3:
            self.value = seq.mark(seq(self.value) + self.came)
            self.came = links.z_move(self.value, pairs[self.step])
        elif self.step == 3:
            self.value = seq.mark(jnp.where(links.inner, seq(self.value), self.came))
            self.came = links.x_swap(self.value)
            self.core = links.core_swap(self.value)
        else:
            self.beside = seq.mark(seq(self.came))
            self.pieces = [self.value, self.beside, self.core, links.core_swap(self.beside)]
        self.step += 1


class SmallChain:
    def __init__(self, links, seq, value, shared, mine):
        self.links, self.seq, self.value = links, seq, seq(value)
        self.shared, self.mine = shared, mine
        self.came = links.core_swap(self.value)
        self.step = 0

    def next(self):
        links = self.links
        if self.step == 0:
            self.value = self.seq.mark(self.seq(self.value) + self.came)
            self.came = links.x_swap(self.value)
        elif self.step == 1:
            self.value = self.seq.mark(self.seq(self.value) + self.came)
            self.came = links.z_all(self.value)
        elif self.step == 2:
            self.value = self.seq.mark(links.z_total(self.seq(self.value), self.came))
            n = self.shared + self.mine
            self.came = links.y_swap(jnp.concatenate([self.value[: self.shared], self.value[n:]]))
            self.value = self.value[:n]
        else:
            self.value = self.seq.mark(self.seq(self.value) + self.came)
        self.step += 1


def on_device(
    direct,
    tokens,
    image_ids,
    rel_index,
    gain_one,
    shift_one,
    w_qkv,
    bias_query,
    bias_value,
    bias_table,
    w_proj,
    bias_proj,
    gain_two,
    shift_two,
    w_up,
    bias_up,
    w_down,
    bias_down,
    cotangent,
):
    mp = lax.axis_index("mp")
    real_rows = tokens.shape[0]
    labels = lax.dynamic_slice(image_ids, (mp * real_rows,), (real_rows,))
    spare = -real_rows % 16
    tokens = jnp.pad(tokens, ((0, spare), (0, 0)))
    cotangent = jnp.pad(cotangent, ((0, spare), (0, 0)))
    width = tokens.shape[1]
    small_size = bias_query.shape[0] + bias_value.shape[0] + bias_up.shape[0]
    biases = [bias_query, bias_value, bias_up]
    onehot = pair_onehot(rel_index, bias_table.shape[0])
    mask = window_mask(labels)

    if direct:
        links = Links()
        core, x = links.core, links.x
        half = width // 2
        core_at = core.astype(jnp.int32).reshape(1)
        first_own = pack_half(core_at, w_qkv, 0)
        first = links.y_swap(first_own)
        names = ("loc", "rem")
        inputs = dict(loc=[w_qkv], rem=None)
        small = dict(rem=None)
        tables = dict(loc=bias_table, rem=links.y_swap(bias_table))
        w_projs = dict(loc=w_proj)
        by_core_x = (2 * core + x).astype(jnp.int32).reshape(1)
        by_core = jnp.stack([2 * core, 2 * core + 1, 2 - 2 * core, 3 - 2 * core]).astype(jnp.int32)
        orders = dict(loc=core_at, rem=jnp.stack([core, 1 - core]).astype(jnp.int32))
        halves = [("loc", by_core, (w_up, w_down))] + [
            ("rem", 2 * orders["rem"] + t, None) for t in (x, 1 - x)
        ]
        halves = [halves[1], halves[0], halves[2]]
        tokens_first = tie(tokens, first_own)
    else:
        names = ("all",)

        def whole_of(value, axis):
            return lax.all_gather(value, "mp", axis=axis, tiled=True)

        inputs = dict(all=[whole_of(w_qkv, 1)])
        up_all, down_all = whole_of(w_up, 1), whole_of(w_down, 0)
        biases = [whole_of(b, 0) for b in biases]
        small = {}
        tables = dict(all=whole_of(bias_table, 1))
        w_projs = dict(all=whole_of(w_proj, 0))
        core_at = jnp.zeros((1,), jnp.int32)
        orders = dict(all=core_at)
        halves = [("all", jnp.arange(down_all.shape[0] // PIECE, dtype=jnp.int32), (up_all, down_all))]

    rows8, small[names[0]] = stack_rows([gain_one, shift_one, bias_proj, gain_two, shift_two, bias_down], biases)
    if direct:
        small["rem"] = links.y_swap(small["loc"])
    small_pieces = sum(places.shape[0] for name, places, _ in halves if name == names[0]) * 3
    qkv, probs, att, w_in = {}, {}, {}, {}
    for name in names:
        positions = position_rows(onehot, tables[name])
        if inputs[name] is None:
            first = tie(first, qkv["loc"], positions)
            inputs[name] = [first, links.core_swap(first)]
            proj_own = pack_half(core_at, tie(w_proj, first), 1)
            sent = list(pack_piece(by_core_x, tie(w_up, first), w_down))
            proj_far = links.y_swap(tie(proj_own, first))
            came = [links.y_swap(tie(sent[0], first))]
        got = attention_forward(
            orders[name], tokens_first if name == "loc" else tokens, rows8, small[name], positions, mask, inputs[name]
        )
        qkv[name], probs[name], att[name], w_in[name], normed = got[:5]
    pieces = []
    if direct:
        proj_far, came[0] = tie(proj_far, qkv["rem"], came[0]), tie(came[0], qkv["rem"], proj_far)
        pieces = [proj_far, links.core_swap(proj_far)]
        came.append(links.y_swap(tie(sent[1], came[0])))
    got = project(orders[names[-1]], [att[n] for n in names], [w_projs[n] for n in w_projs], pieces, tokens, rows8)
    middle, low_two = got[:2]
    if direct:
        w_projs["rem"] = got[2]
    own, other, up_bias_grad = [], [], []
    carried = None
    for i, (name, places, ws) in enumerate(halves):
        last = i == len(halves) - 1
        low_now = low_two
        base = small[name].shape[0] - small_pieces
        if direct and i == 0:
            came = [tie(piece, low_two, *came) for piece in came]
            beside = [links.x_swap(came[0])]
            ws = came + [links.core_swap(piece) for piece in came]
        if direct and i == 1:
            fence = (own[0], beside[0])
            theirs_f = links.core_swap(tie(other[0], *fence))
            beside.append(links.x_swap(tie(came[1], *fence)))
            swapped = [links.core_swap(tie(beside[0], *fence))]
            far_f = own[0] + theirs_f
            got_f = links.y_swap(far_f)
            low_now = tie(low_two, far_f)
        if direct and i == 2:
            fence = (own[1], beside[1], got_f, swapped[0])
            beside[1] = tie(beside[1], *fence)
            swapped.append(links.core_swap(beside[1]))
            theirs_hidden = links.core_swap(tie(other[1], swapped[1]))
            ws = beside + swapped
        got = mlp(places, low_now, cotangent, small[name], base, rows8, ws, carried, middle if last else None)
        own.append(got[0])
        other.append(got[1])
        up_bias_grad.append(got[2])
        carried = got[3:5]
    block_out, grad_middle, branch, sums_two = got[3:7]

    def unit(name, group):
        return (w_projs[name], qkv[name], probs[name], group)

    if direct:
        seq = Sequence()
        branch = seq.fence(branch, theirs_hidden)
        rows = 2 * PIECE
        theirs_s = links.core_swap(seq(other[2]))
        send_f = seq.mark(cut_sum(x, rows, [(seq(own[1]), 0), (theirs_hidden, 0), (tie(got_f, branch), -x * rows)]))
        beside_f = links.x_swap(send_f)
        far_s = seq.mark(seq(own[2]) + theirs_s)
        got_s = links.y_swap(far_s)
        got = attention_backward(
            core_at,
            seq(branch),
            normed,
            [[unit(name, g) for g in range(2)] for name in ("rem", "loc")],
            [att["rem"], att["loc"]],
        )
        gqkv_a, bias_a, cols_a, theirs_a, rem_a, loc_a = got
        gqkv_a = seq.fence(gqkv_a, beside_f, got_s)
        theirs_a = links.core_swap(seq(theirs_a))

        def kept(at):
            start = (1 - x) * rows + at
            cut = [lax.dynamic_slice(t, (start, 0), (PIECE, width)) for t in (seq(own[1]), theirs_hidden)]
            cut = [t.astype(f32) for t in (*cut, got_s[at : at + PIECE], beside_f[at : at + PIECE])]
            return sum(cut[1:], cut[0]).astype(bf16)

        chain_0_value = seq.mark(kept(0))
        far_a = seq.mark(seq(rem_a) + theirs_a[0])
        got_a = links.y_swap(far_a)
        chain_0 = Chain(links, seq, seq(chain_0_value))
        chain_1_value = seq.mark(kept(PIECE))
        got = attention_backward(core_at, seq(branch), normed, [[unit(name, 2)] for name in ("rem", "loc")])
        gqkv_b, bias_b, cols_b, theirs_b, rem_b, loc_b = got
        gqkv_b = seq.fence(gqkv_b, chain_0.came, got_a)
        theirs_b = links.core_swap(seq(theirs_b))
        chain_0.next()
        chain_1 = Chain(links, seq, seq(chain_1_value))
        theirs_a = theirs_a.reshape(-1, theirs_a.shape[2])
        def along_x(loc, theirs, got):
            quarter = half // 2
            terms = [(seq(loc), 0), (theirs, half), (got, 0)]
            send = seq.mark(cut_sum(1 - x, quarter, terms))
            return Chain(links, seq, cut_sum(x, quarter, terms), links.x_swap(send))

        chain_a = along_x(loc_a, theirs_a, got_a)
        far_b = seq.mark(seq(rem_b) + theirs_b[0])
        got_b = links.y_swap(far_b)
        theirs_b = theirs_b.reshape(-1, theirs_b.shape[2])
        plan = ((0, 0, 1, 0, 768), (0, 768, 0, 0, 768), (1, 0, 1, 768, 384), (1, 384, 0, 768, 384))
        grad_tokens, sums_one = input_backward(
            plan, [gqkv_a, gqkv_b], [w_in["loc"], w_in["rem"]], tokens, grad_middle, seq(rows8)
        )
        sums_one = seq.fence(sums_one, chain_0.came, chain_1.came, chain_a.came, got_b)
        chain_a.next()
        bias_a, bias_b, cols_a, cols_b = [seq(v) for v in (bias_a, bias_b, cols_a, cols_b)]
        up_bias_grad = [seq(v) for v in up_bias_grad]

        chain_0.next()
        chain_1.next()
        chain_b = along_x(loc_b, theirs_b, got_b)

        def by_place(first, second):
            return jnp.where(core == 0, jnp.concatenate([first, second]), jnp.concatenate([second, first]))

        by_t = [jnp.where(x == t, up_bias_grad[0], up_bias_grad[2]) for t in range(2)]
        rem = [jnp.concatenate([grad[0, 0, at : at + PIECE] for grad in by_t]) for at in (0, PIECE)]
        bias_up_parts = [by_place(*rem), by_place(up_bias_grad[1][0, 0], up_bias_grad[1][1, 0])]

        def of_part(at):
            sums = [bias_a[:, at * 512 : (at + 1) * 512], bias_b[:, at * 256 : (at + 1) * 256]]
            cols = [cols_a[:, at * 256 : (at + 1) * 256], cols_b[:, at * 128 : (at + 1) * 128]]
            table = table_grad(onehot, jnp.concatenate(sums, axis=1))
            return [jnp.concatenate(cols, axis=1).reshape(-1), bias_up_parts[at], table.reshape(-1)]

        values = [sums_two.reshape(-1), sums_one.reshape(-1), *of_part(1), *of_part(0)]
        small_chain = SmallChain(links, seq, jnp.concatenate(values), 6 * width, small_size + bias_table.size)
        waves = (
            (chain_b, chain_a, chain_0, chain_1, small_chain),
            (chain_b, chain_a, chain_1, chain_0, small_chain),
            (chain_a, chain_1, chain_b, small_chain),
        )
        for wave in waves:
            for chain in wave:
                chain.next()
        pairs = [p for pair in zip(chain_0.pieces, chain_1.pieces) for p in pair]
        places = jnp.stack([2 * c + t for c in (core, 1 - core) for t in (1 - x, x)]).astype(jnp.int32)
        grad_down, grad_up = place_mlp(tie(places, seq.last), pairs, w_down.shape, w_up.shape)
        grad_down = seq.mark(grad_down)
        for chain in (chain_b, chain_a, small_chain, chain_b):
            chain.next()
        grad_qkv, grad_proj = place_two(links.order(), chain_a.pieces, chain_b.pieces, w_qkv.shape, w_proj.shape)
        got = small_chain.value
        two = got[: 4 * width].reshape(4, width)
        late = got[4 * width : 6 * width].reshape(2, width)
        got = got[6 * width :]
        cols = bias_query.shape[0]
        grad_query_b, grad_value_b = got[:cols], got[cols : 2 * cols]
        grad_up_bias = got[2 * cols : small_size]
        grad_table = got[small_size:].reshape(bias_table.shape)
    else:
        groups = tables["all"].shape[1] // GROUP
        got = attention_backward(core_at, branch, normed, [[unit("all", g) for g in range(groups)]])
        gqkv, bias_sums, col_sums, second_half, first_half = got
        grad_tokens, sums_one = input_backward(
            ((0, 0, 0, 0, gqkv.shape[1]),), [gqkv], [w_in["all"]], tokens, grad_middle, rows8
        )

        def summed(value, axis):
            value = lax.psum_scatter(value, "mp", scatter_dimension=axis, tiled=True)
            return lax.psum(value, "dp")

        hidden_grads = jnp.concatenate([own[0], other[0]]).reshape(-1, 2, PIECE, width)
        grad_down = summed(hidden_grads[:, 0].reshape(-1, width), 0).astype(f32)
        grad_up = summed(hidden_grads[:, 1].reshape(-1, width).T, 1).astype(f32)
        cols = gqkv.shape[1]
        grad_proj = summed(dot(att["all"], branch, TN).astype(bf16), 0).astype(f32)
        in_order = jnp.concatenate([first_half, second_half[0]], axis=0).reshape(-1, 384)
        natural = dot(in_order, group_order(), NT).reshape(width, cols).astype(bf16)
        grad_qkv = summed(natural, 1).astype(f32)
        grad_query_b = summed(col_sums[0], 0)
        grad_value_b = summed(col_sums[1], 0)
        grad_up_bias = summed(up_bias_grad[0].reshape(-1), 0)
        grad_table = summed(table_grad(onehot, bias_sums), 1)
        two, late = lax.psum((sums_two, sums_one), ("dp", "mp"))
    return (
        block_out[:real_rows],
        grad_tokens[:real_rows],
        late[0],
        late[1],
        grad_qkv,
        grad_query_b,
        grad_value_b,
        grad_table,
        grad_proj,
        two[2],
        two[0],
        two[1],
        grad_up,
        grad_up_bias,
        grad_down,
        two[3],
    )


def solution(mesh):
    direct = mesh.shape["dp"] == 16 and mesh.shape["mp"] == 2
    return jax.shard_map(
        functools.partial(on_device, direct),
        mesh=mesh,
        in_specs=(
            P(("dp", "mp"), None),
            P("dp"),
            P(),
            P(),
            P(),
            P(None, "mp"),
            P("mp"),
            P("mp"),
            P(None, "mp"),
            P("mp", None),
            P(),
            P(),
            P(),
            P(None, "mp"),
            P("mp"),
            P("mp", None),
            P(),
            P(("dp", "mp"), None),
        ),
        out_specs=(
            P(("dp", "mp"), None),
            P(("dp", "mp"), None),
            P(),
            P(),
            P(None, "mp"),
            P("mp"),
            P("mp"),
            P(None, "mp"),
            P("mp", None),
            P(),
            P(),
            P(),
            P(None, "mp"),
            P("mp"),
            P("mp", None),
            P(),
        ),
        check_vma=False,
    )
```
